256 devices in a mesh: section: 2 (over core), ctx: 16 (over z, y_lo), tp: 8 (over y_hi, x).
Axes of the slice: x: 4, y: 4 (y_hi: 2, y_lo: 2; y = y_hi * 2 + y_lo), z: 8, core: 2. Of those that a mesh axis runs over, the one named last changes fastest.
Arguments:
- layer_input: bfloat16 [2, 1, 2048, 4096], P('section', None, 'ctx', 'tp'), may hold values from -6 to 6
- loss_cot: bfloat16 [1, 2048, 4096], P(None, 'ctx', 'tp'), may hold values from -6 to 6
- token_weights: int32 [1, 2048], P(None, 'ctx'), may hold values from 0 to 3
- doc_blocks: int32 [1, 3], replicated, may hold values from 1 to 10, 16 in all within a row
- norm_gain: float32 [2, 4096], P('section'), may hold values from 0.5 to 1.5
- qkv_weight: bfloat16 [2, 4096, 6144], P('section', None, 'tp'), may hold values from -12 to 12, as said below
- out_weight: bfloat16 [2, 4096, 4096], P('section', None, 'tp'), may hold values from -0.09375 to 0.09375
Outputs:
- grad_inputs: bfloat16 [2, 1, 2048, 4096], P('section', None, 'ctx', 'tp')
- grad_qkv: float32 [2, 4096, 6144], P('section', 'ctx', 'tp')
- grad_out: float32 [2, 4096, 4096], P('section', 'ctx', 'tp')
The draws below stay inside these ranges and needn't reach their ends.
Inputs may be any that keep to these rules, and one draw needn't show every extreme that they name: `doc_blocks`: each row sums to 16, and its longest document has the max. `qkv_weight`: entries of order 4096 ** -0.5 in the query and value columns.
All inputs are finite; a program needn't handle non-finite values.
Results may differ from the reference program's by a relative error of at most 0.04.
The reference program's roundings to bfloat16 on the way count: a program that leaves them out, or rounds other values in their place, can miss the bound.
Values may be sent and summed in bfloat16 or wider, within the bound.
A program may use at most 128 MiB of HBM per device.

```python
import math
import jax
import jax.numpy as jnp
import numpy as np
from jax import lax

MODEL_WIDTH = 4096
QUERY_HEADS = 32
KEY_VALUE_HEADS = 8
HEAD_SIZE = 128
TOK_DEV = 128
MICRO = 1
DOCS = 3
BLOCK = 128
TOKENS = 2048
N_SECTION = 2
N_CTX = 16
N_TP = 8


def draw_qkv_weight(key, part):
    key = jax.random.fold_in(key, 11)
    primary_keys = jax.random.fold_in(key, 0)
    heads_per_group = QUERY_HEADS // KEY_VALUE_HEADS
    weight_matrices = jax.random.truncated_normal(primary_keys, -4.0, 4.0, (N_SECTION, MODEL_WIDTH, KEY_VALUE_HEADS, heads_per_group + 2, HEAD_SIZE), jnp.float32) * MODEL_WIDTH ** (-0.5)
    return weight_matrices.reshape(N_SECTION, MODEL_WIDTH, (QUERY_HEADS + 2 * KEY_VALUE_HEADS) * HEAD_SIZE).astype(jnp.bfloat16)


def place_ends(values, own_key, smallest, largest):
    longest = values.shape.index(max(values.shape))
    spots = []
    for shift in (0, 1):
        where = [jax.random.randint(jax.random.fold_in(own_key, axis), (), 0, length) for axis, length in enumerate(values.shape)]
        where[longest] = (where[longest] + shift) % values.shape[longest]
        spots.append(tuple(where))
    return values.at[spots[0]].set(smallest).at[spots[1]].set(largest)


def block_levels(key, shape, pieces, least, largest):
    level, own = 1.0, jax.random.fold_in(key, 6)
    for dim, parts in pieces:
        heights = jnp.exp(jax.random.uniform(jax.random.fold_in(own, dim), (parts,), jnp.float32, least / len(pieces), largest / len(pieces)))
        level = level * jnp.repeat(heights, shape[dim] // parts).reshape([-1 if axis == dim else 1 for axis in range(len(shape))])
    return level


def length_profile(amount, total, most, lean):
    weights = [(1 << 20) // math.isqrt(standing ** lean) + 1 for standing in range(2, amount + 1)]
    rest, holding = total - most - (amount - 1), [1] * (amount - 1)
    while rest > 0:
        movable = [i for i in range(amount - 1) if holding[i] < most]
        pool, budget = sum([weights[i] for i in movable]), rest
        for i in movable:
            addition = min(most - holding[i], max(1, budget * weights[i] // pool), rest)
            holding[i] = holding[i] + addition
            rest = rest - addition
    return np.array([most] + holding)


def ragged(key, amount, total, most, slope):
    if amount == 2:
        one = jax.random.randint(key, (), max(1, total - most), min(most, total - 1) + 1)
        return jnp.stack([one, total - one])
    tallies = jnp.asarray(length_profile(amount, total, most, slope), jnp.int32)
    couples = (amount - 1) // 2
    donor, sink = tallies[1:1 + 2 * couples:2], tallies[2:2 + 2 * couples:2]
    room = jnp.minimum(donor - 1, most - sink)
    passed = jax.random.randint(jax.random.fold_in(key, 1), (couples,), 0, 1 << 20) % (room + 1)
    tallies = tallies.at[1:1 + 2 * couples:2].set(donor - passed).at[2:2 + 2 * couples:2].set(sink + passed)
    return tallies[jax.random.permutation(jax.random.fold_in(key, 2), amount)]


def noise(own_key, extent, width, most, cuts=(), kind=jnp.bfloat16):
    values = width * jax.random.normal(own_key, extent, jnp.float32)
    if cuts:
        values = values * block_levels(own_key, extent, cuts, -0.22, 0.18)
    return jnp.clip(values, -most, most).astype(kind)


def setup_inputs(seed: int = 0) -> dict:
    key_of = jax.random.split(jax.random.key(seed), 8)
    return {
        "layer_input": noise(key_of[0], (N_SECTION, MICRO, TOKENS, MODEL_WIDTH), 1.0, 6.0, ((0, 2), (2, 16), (3, 8))),
        "loss_cot": noise(key_of[1], (MICRO, TOKENS, MODEL_WIDTH), 1.0, 6.0, ((1, 16), (2, 8))),
        "token_weights": place_ends(jax.random.randint(key_of[2], (MICRO, TOKENS), 0, 4), jax.random.fold_in(key_of[2], 1), 0, 3).astype(jnp.int32),
        "doc_blocks": jax.vmap(lambda own: ragged(own, DOCS, TOKENS // BLOCK, TOKENS // BLOCK // 2 + TOKENS // BLOCK // 8, 2))(jax.random.split(key_of[3], MICRO)).reshape((MICRO, DOCS)).astype(jnp.int32),
        "norm_gain": jnp.clip(1.0 + 0.1 * jax.random.normal(key_of[4], (N_SECTION, MODEL_WIDTH), jnp.float32), 0.5, 1.5),
        "qkv_weight": draw_qkv_weight(jax.random.fold_in(key_of[7], 71), 0),
        "out_weight": noise(key_of[6], (N_SECTION, MODEL_WIDTH, QUERY_HEADS * HEAD_SIZE), (QUERY_HEADS * HEAD_SIZE) ** -0.5, 0.09375, ((0, 2), (2, 8))),
    }


EPSILON = 1e-05
NEG_FILL = -1e+30

def segment_of(blocks, positions):
    doc_ends = jnp.cumsum(blocks.astype(jnp.int32)) * BLOCK
    return lax.optimization_barrier(jnp.sum((positions[:, None] >= doc_ends[None, :]).astype(jnp.int32), axis=1))

def shard_attention(query_rows, cot_rows, keys_all, values_all, allowed):
    score_scale = HEAD_SIZE ** (-0.5)
    scores = jnp.einsum('rgjd,sgd->gjrs', query_rows.astype(jnp.float32), keys_all.astype(jnp.float32)) * score_scale
    scores = jnp.where(allowed[None, None], scores, NEG_FILL)
    row_peak = lax.optimization_barrier(jnp.max(scores, axis=-1, keepdims=True))
    shifted_exp = jnp.exp(scores - row_peak)
    soft_weights = shifted_exp / lax.optimization_barrier(jnp.sum(shifted_exp, axis=-1, keepdims=True))
    soft_low = soft_weights.astype(jnp.bfloat16)
    attended = jnp.einsum('gjrs,sgd->rgjd', soft_low.astype(jnp.float32), values_all.astype(jnp.float32)).astype(jnp.bfloat16)
    delta_rows = jnp.einsum('rgjd,rgjd->gjr', cot_rows.astype(jnp.float32), attended.astype(jnp.float32))
    dprobs = jnp.einsum('rgjd,sgd->gjrs', cot_rows.astype(jnp.float32), values_all.astype(jnp.float32))
    dscores = (soft_weights * (dprobs - delta_rows[..., None])).astype(jnp.bfloat16)
    query_gradient = (jnp.einsum('gjrs,sgd->rgjd', dscores.astype(jnp.float32), keys_all.astype(jnp.float32)) * score_scale).astype(jnp.bfloat16)
    grad_keys = jnp.einsum('gjrs,rgjd->sgd', dscores.astype(jnp.float32), query_rows.astype(jnp.float32)) * score_scale
    grad_values = jnp.einsum('gjrs,rgjd->sgd', soft_low.astype(jnp.float32), cot_rows.astype(jnp.float32))
    return (attended, query_gradient, grad_keys.astype(jnp.bfloat16), grad_values.astype(jnp.bfloat16))

def layer_backward(rows_in, cotangent, gain_full, joined_weight, output_weight, blocks):
    number_rows = rows_in.shape[0]
    heads_per_group = QUERY_HEADS // KEY_VALUE_HEADS
    widened = rows_in.astype(jnp.float32)
    inv_rms = lax.rsqrt(lax.optimization_barrier(jnp.mean(widened * widened, axis=-1, keepdims=True)) + EPSILON)
    normed = widened * inv_rms
    hidden = (normed * gain_full).astype(jnp.bfloat16)
    combined_rows = jnp.dot(hidden, joined_weight, preferred_element_type=jnp.float32).astype(jnp.bfloat16)
    combined_rows = combined_rows.reshape(number_rows, KEY_VALUE_HEADS, heads_per_group + 2, HEAD_SIZE)
    queries = combined_rows[:, :, :heads_per_group]
    keys_all = combined_rows[:, :, heads_per_group]
    values_all = combined_rows[:, :, heads_per_group + 1]
    head_cotangent = jnp.dot(cotangent, output_weight, preferred_element_type=jnp.float32).astype(jnp.bfloat16)
    head_cotangent = head_cotangent.reshape(number_rows, KEY_VALUE_HEADS, heads_per_group, HEAD_SIZE)
    positions = jnp.arange(number_rows, dtype=jnp.int32)
    segments = segment_of(blocks, positions)

    def per_shard(shard_index):
        row_start = shard_index * TOK_DEV
        query_rows = lax.dynamic_slice_in_dim(queries, row_start, TOK_DEV, 0)
        cot_rows = lax.dynamic_slice_in_dim(head_cotangent, row_start, TOK_DEV, 0)
        query_pos = row_start + jnp.arange(TOK_DEV, dtype=jnp.int32)
        query_seg = lax.dynamic_slice_in_dim(segments, row_start, TOK_DEV, 0)
        allowed = (positions[None, :] <= query_pos[:, None]) & (segments[None, :] == query_seg[:, None])
        return shard_attention(query_rows, cot_rows, keys_all, values_all, allowed)
    attended, query_gradient, key_parts, value_parts = lax.map(per_shard, jnp.arange(N_CTX, dtype=jnp.int32))
    attended = attended.reshape(number_rows, QUERY_HEADS * HEAD_SIZE)
    query_gradient = query_gradient.reshape(number_rows, KEY_VALUE_HEADS, heads_per_group, HEAD_SIZE)
    grad_keys = lax.optimization_barrier(jnp.sum(key_parts.astype(jnp.float32), axis=0)).astype(jnp.bfloat16)
    grad_values = lax.optimization_barrier(jnp.sum(value_parts.astype(jnp.float32), axis=0)).astype(jnp.bfloat16)
    combined_gradient = jnp.concatenate([query_gradient, grad_keys[:, :, None], grad_values[:, :, None]], axis=2)
    combined_gradient = combined_gradient.reshape(number_rows, (QUERY_HEADS + 2 * KEY_VALUE_HEADS) * HEAD_SIZE)
    slice_cols = combined_gradient.shape[1] // N_TP
    grad_slices = combined_gradient.reshape(number_rows, N_TP, slice_cols).transpose(1, 0, 2)
    weight_slices = joined_weight.reshape(MODEL_WIDTH, N_TP, slice_cols).transpose(1, 0, 2)

    def add_slice(running, operands):
        partial_sum = lax.dot_general(operands[0], operands[1], (((1,), (1,)), ((), ())), preferred_element_type=jnp.float32)
        partial_sum = lax.optimization_barrier(partial_sum.astype(jnp.bfloat16))
        return (running + partial_sum.astype(jnp.float32), None)
    feature_grad, _ = lax.scan(add_slice, jnp.zeros((number_rows, MODEL_WIDTH), jnp.float32), (grad_slices, weight_slices))
    scaled = feature_grad * gain_full
    mean_term = lax.optimization_barrier(jnp.mean(scaled * normed, axis=-1, keepdims=True))
    input_grad = (cotangent.astype(jnp.float32) + inv_rms * (scaled - normed * mean_term)).astype(jnp.bfloat16)
    return (hidden, combined_gradient, attended, input_grad)

def regroup(array_in):
    return array_in.reshape(MICRO, N_CTX, TOK_DEV, -1).transpose(1, 0, 2, 3).reshape(N_CTX, MICRO * TOK_DEV, -1)

def weight_grads(hidden_all, joined_all, cot_all, attended_all):

    def add_shard(running, operands):
        first_part = lax.dot_general(operands[0], operands[1], (((0,), (0,)), ((), ())), preferred_element_type=jnp.float32)
        second_part = lax.dot_general(operands[2], operands[3], (((0,), (0,)), ((), ())), preferred_element_type=jnp.float32)
        first_part = lax.optimization_barrier(first_part.astype(jnp.bfloat16))
        second_part = lax.optimization_barrier(second_part.astype(jnp.bfloat16))
        return ((running[0] + first_part.astype(jnp.float32), running[1] + second_part.astype(jnp.float32)), None)
    start_value = (jnp.zeros((MODEL_WIDTH, joined_all.shape[-1]), jnp.float32), jnp.zeros((MODEL_WIDTH, attended_all.shape[-1]), jnp.float32))
    totals, _ = lax.scan(add_shard, start_value, (regroup(hidden_all), regroup(joined_all), regroup(cot_all), regroup(attended_all)))
    return totals

def reference(layer_input, loss_cot, token_weights, doc_blocks, norm_gain, qkv_weight, out_weight):
    cotangents = [(loss_cot[micro_index].astype(jnp.float32) * token_weights[micro_index].astype(jnp.float32)[:, None]).astype(jnp.bfloat16) for micro_index in range(MICRO)]
    grads_in = [None] * N_SECTION
    grads_joined = [None] * N_SECTION
    grads_output = [None] * N_SECTION
    for section_index in range(N_SECTION - 1, -1, -1):
        outcomes = [layer_backward(layer_input[section_index, micro_index], cotangents[micro_index], norm_gain[section_index], qkv_weight[section_index], out_weight[section_index], doc_blocks[micro_index]) for micro_index in range(MICRO)]
        hidden_all = jnp.stack([outcome[0] for outcome in outcomes])
        joined_all = jnp.stack([outcome[1] for outcome in outcomes])
        attended_all = jnp.stack([outcome[2] for outcome in outcomes])
        cot_all = jnp.stack(cotangents)
        first_total, second_total = weight_grads(hidden_all, joined_all, cot_all, attended_all)
        grads_joined[section_index] = first_total
        grads_output[section_index] = second_total
        cotangents = [outcome[3] for outcome in outcomes]
        grads_in[section_index] = jnp.stack(cotangents)
    return (jnp.stack(grads_in), jnp.stack(grads_joined), jnp.stack(grads_output))
```

```python
import functools

import jax
import jax.numpy as jnp
from jax import lax
from jax.experimental import pallas as pl
from jax.experimental.pallas import tpu as pltpu
from jax.sharding import PartitionSpec as P

MESH = pl.DeviceIdType.MESH
GROUP_HEADS = 4
HEAD_SIZE = 128
BLOCK = 128
MAX_DOC = 10
EPSILON = 1e-05
NEG_FILL = -1e30
F32 = jnp.float32
BF16 = jnp.bfloat16

NN = (((1,), (0,)), ((), ()))
NT = (((1,), (1,)), ((), ()))
TN = (((0,), (0,)), ((), ()))


def mm(a, b, dims=NN):
    return lax.dot_general(a, b, dims, preferred_element_type=F32)


def kernel(
    n_ctx, n_tp, window,
    x_ref, loss_ref, tw_ref, docs_ref, gain_ref, wq_hbm, wo_hbm,
    gin_ref, gqkv_ref, gout_ref,
    wq, wo, xfull, cotfull, cot_loc, inv_b,
    kv, q_s, hc_s, att_s, att_n, gq_n, gkv_n, scores, probs, peak, denom, acc,
    dkv_part, dkv_in, feat_f, feat_out, feat_in, rs_out, rs_in,
    hid_z, cot_z, att_z, gq_z, gkv_z, y_out_o, y_out_q, y_out_k, y_in_o, y_in_q, y_in_k,
    w_sem, x_s, x_r, c_s, c_r, kv_s, kv_r, d_s, d_r, f_s, f_r, r_s, r_r,
    hz_s, hz_r, cz_s, cz_r, az_s, az_r, qz_s, qz_r, kz_s, kz_r, y_s, y_r, sec_s, sec_r,
):
    s = lax.axis_index("section")
    c = lax.axis_index("ctx")
    t = lax.axis_index("tp")
    n_z = n_ctx // 2
    z, lo = c // 2, lax.rem(c, 2)
    part = x_ref.shape[1]
    width = part * n_tp
    half = part // 2
    heads = GROUP_HEADS * HEAD_SIZE
    cols = heads + 2 * HEAD_SIZE
    scale = HEAD_SIZE ** (-0.5)
    last = window - 1

    def remote(src, dst, ss, rs, dev):
        return pltpu.make_async_remote_copy(
            src_ref=src, dst_ref=dst, send_sem=ss, recv_sem=rs, device_id=dev, device_id_type=MESH
        )

    def tp_dev(p):
        return {"tp": p}

    def z_dev(p):
        return {"ctx": p * 2 + lo}

    def exchange(n, me, dev, src_of, slot, ss, rs):
        def copy_to(p):
            return remote(src_of(p), slot(me), ss.at[p], rs.at[me], dev(p))

        def copy_from(p):
            return remote(slot(p), slot(p), ss.at[p], rs.at[p], dev(p))

        def start():
            @pl.loop(1, n)
            def _(i):
                copy_to(lax.rem(me + i, n)).start()

        def wait_recv():
            @pl.loop(1, n)
            def _(i):
                copy_from(lax.rem(me + i, n)).wait_recv()

        def wait_send():
            @pl.loop(1, n)
            def _(i):
                copy_to(lax.rem(me + i, n)).wait_send()

        return start, wait_recv, wait_send, copy_to

    rows = lambda ref: lambda p: ref.at[pl.ds(p * BLOCK, BLOCK)]
    whole = lambda ref: lambda p: ref

    x_ex = exchange(n_tp, t, tp_dev, whole(x_ref), lambda p: xfull.at[p], x_s, x_r)
    c_ex = exchange(n_tp, t, tp_dev, whole(cot_loc), lambda p: cotfull.at[p], c_s, c_r)
    f_ex = exchange(n_tp, t, tp_dev, lambda p: feat_out.at[p], lambda p: feat_in.at[p], f_s, f_r)
    r_ex = exchange(n_tp, t, tp_dev, whole(rs_out), lambda p: rs_in.at[p], r_s, r_r)
    hz_ex = exchange(n_z, z, z_dev, lambda p: xfull.at[p], rows(hid_z), hz_s, hz_r)
    cz_ex = exchange(n_z, z, z_dev, lambda p: cotfull.at[p], rows(cot_z), cz_s, cz_r)
    az_ex = exchange(n_z, z, z_dev, whole(att_n), rows(att_z), az_s, az_r)
    qz_ex = exchange(n_z, z, z_dev, whole(gq_n), rows(gq_z), qz_s, qz_r)
    kz_ex = exchange(n_z, z, z_dev, whole(gkv_n), rows(gkv_z), kz_s, kz_r)
    wq_copy = pltpu.make_async_copy(wq_hbm, wq, w_sem.at[0])
    wo_copy = pltpu.make_async_copy(wo_hbm, wo, w_sem.at[1])

    wq_copy.start()
    wo_copy.start()
    kv[...] = jnp.zeros_like(kv)

    barrier = pltpu.get_barrier_semaphore()

    @pl.loop(1, n_tp)
    def _(i):
        pl.semaphore_signal(barrier, inc=1, device_id={"tp": lax.rem(t + i, n_tp)}, device_id_type=MESH)

    @pl.loop(1, n_ctx)
    def _(i):
        pl.semaphore_signal(barrier, inc=1, device_id={"ctx": lax.rem(c + i, n_ctx)}, device_id_type=MESH)

    pl.semaphore_signal(barrier, inc=1, device_id={"section": 1 - s}, device_id_type=MESH)
    pl.semaphore_wait(barrier, n_tp + n_ctx - 1)

    x_ex[0]()
    xfull[t] = x_ref[...]

    @pl.when(s == 1)
    def _():
        weights = jnp.broadcast_to(tw_ref[...].astype(F32), (BLOCK, BLOCK)).T[:, :1]
        cot_loc[...] = (loss_ref[...].astype(F32) * weights).astype(BF16)
        c_ex[0]()

    x_ex[1]()
    square = jnp.zeros((BLOCK, part), F32)
    for p in range(n_tp):
        wide = xfull[p].astype(F32)
        square = square + wide * wide
    inv = lax.rsqrt(jnp.sum(square, axis=1, keepdims=True) / width + EPSILON)
    inv_b[...] = jnp.broadcast_to(inv, inv_b.shape)
    for p in range(n_tp):
        gain = gain_ref[:, p * part : (p + 1) * part]
        xfull[p] = ((xfull[p].astype(F32) * inv) * gain).astype(BF16)

    def project(full, weight, lo_col, n_col):
        total = jnp.zeros((BLOCK, n_col), F32)
        for p in range(n_tp):
            total = total + mm(full[p], weight[p * part : (p + 1) * part, lo_col : lo_col + n_col])
        return total.astype(BF16)

    wq_copy.wait()
    kv[last] = project(xfull, wq, heads, 2 * HEAD_SIZE)

    def kv_copy(d):
        return remote(
            kv.at[last], kv.at[last - d], kv_s.at[d], kv_r.at[d], {"ctx": lax.rem(c + d, n_ctx)}
        )

    @pl.loop(1, window)
    def _(d):
        @pl.when(c + d < n_ctx)
        def _():
            kv_copy(d).start()

    for j in range(0, GROUP_HEADS, 2):
        pair = project(xfull, wq, j * HEAD_SIZE, 2 * HEAD_SIZE)
        q_s[j * BLOCK : (j + 1) * BLOCK] = pair[:, :HEAD_SIZE]
        q_s[(j + 1) * BLOCK : (j + 2) * BLOCK] = pair[:, HEAD_SIZE:]
    hz_ex[0]()
    hid_z[pl.ds(z * BLOCK, BLOCK)] = xfull[z]

    doc_start = jnp.int32(0)
    doc_end = jnp.int32(0)
    for i in range(docs_ref.shape[1]):
        doc_end = doc_end + docs_ref[0, i]
        doc_start = jnp.where(doc_end <= c, doc_end, doc_start)
    own = mm(q_s[...], kv[last, :, :HEAD_SIZE], NT) * scale
    row = lax.broadcasted_iota(jnp.int32, own.shape, 0) % BLOCK
    col = lax.broadcasted_iota(jnp.int32, own.shape, 1)
    own = jnp.where(col <= row, own, NEG_FILL)
    scores[last] = own
    peak[...] = own

    @pl.loop(0, last)
    def _(i):
        j = last - 1 - i

        @pl.when(c - last + j >= 0)
        def _():
            kv_copy(last - j).wait_recv()

        block = mm(q_s[...], kv[j, :, :HEAD_SIZE], NT) * scale
        block = jnp.where(c - last + j >= doc_start, block, NEG_FILL)
        scores[j] = block
        peak[...] = jnp.maximum(peak[...], block)

    peak[...] = jnp.broadcast_to(jnp.max(peak[...], axis=1, keepdims=True), peak.shape)
    denom[...] = jnp.zeros_like(denom)

    @pl.loop(0, window)
    def _(j):
        e = jnp.exp(scores[j] - peak[...])
        scores[j] = e
        denom[...] += e

    denom[...] = jnp.broadcast_to(1.0 / jnp.sum(denom[...], axis=1, keepdims=True), denom.shape)
    acc[...] = jnp.zeros_like(acc)

    @pl.loop(0, window)
    def _(j):
        soft = scores[j] * denom[...]
        low = soft.astype(BF16)
        scores[j] = soft
        probs[j] = low
        acc[...] += mm(low, kv[j, :, HEAD_SIZE:])

    att_s[...] = acc[...].astype(BF16)
    for j in range(GROUP_HEADS):
        att_n[:, j * HEAD_SIZE : (j + 1) * HEAD_SIZE] = att_s[j * BLOCK : (j + 1) * BLOCK]
    az_ex[0]()
    att_z[pl.ds(z * BLOCK, BLOCK)] = att_n[...]

    sec_copy = remote(gin_ref, cot_loc, sec_s, sec_r, {"section": 1 - s})

    @pl.when(s == 0)
    def _():
        sec_copy.wait_recv()
        c_ex[0]()

    cotfull[t] = cot_loc[...]
    wo_copy.wait()
    c_ex[1]()
    for j in range(0, GROUP_HEADS, 2):
        pair = project(cotfull, wo, j * HEAD_SIZE, 2 * HEAD_SIZE)
        hc_s[j * BLOCK : (j + 1) * BLOCK] = pair[:, :HEAD_SIZE]
        hc_s[(j + 1) * BLOCK : (j + 2) * BLOCK] = pair[:, HEAD_SIZE:]

    delta = jnp.sum(hc_s[...].astype(F32) * att_s[...].astype(F32), axis=1, keepdims=True)
    peak[...] = jnp.broadcast_to(delta, peak.shape)
    acc[...] = jnp.zeros_like(acc)

    def dkv_copy(d):
        return remote(
            dkv_part.at[last - d], dkv_in.at[d], d_s.at[d], d_r.at[d],
            {"ctx": lax.rem(c - d + n_ctx, n_ctx)},
        )

    @pl.loop(0, window)
    def _(j):
        dprobs = mm(hc_s[...], kv[j, :, HEAD_SIZE:], NT)
        ds = (scores[j] * (dprobs - peak[...])).astype(BF16)
        acc[...] += mm(ds, kv[j, :, :HEAD_SIZE])
        dkv_part[j, :, :HEAD_SIZE] = (mm(ds, q_s[...], TN) * scale).astype(BF16)
        dkv_part[j, :, HEAD_SIZE:] = mm(probs[j], hc_s[...], TN).astype(BF16)

        @pl.when((j < last) & (c - last + j >= 0))
        def _():
            dkv_copy(last - j).start()

    for j in range(GROUP_HEADS):
        gq_n[:, j * HEAD_SIZE : (j + 1) * HEAD_SIZE] = (
            acc[j * BLOCK : (j + 1) * BLOCK] * scale
        ).astype(BF16)
    qz_ex[0]()
    cz_ex[0]()
    gq_z[pl.ds(z * BLOCK, BLOCK)] = gq_n[...]
    cot_z[pl.ds(z * BLOCK, BLOCK)] = cotfull[z]

    @pl.loop(0, n_tp)
    def _(p):
        feat_f[p] = mm(gq_n[...], wq[pl.ds(p * part, part), :heads], NT)

    acc[:BLOCK] = dkv_part[last, :, :HEAD_SIZE].astype(F32)
    acc[BLOCK : 2 * BLOCK] = dkv_part[last, :, HEAD_SIZE:].astype(F32)

    @pl.loop(1, window)
    def _(d):
        @pl.when(c + d < n_ctx)
        def _():
            dkv_copy(d).wait_recv()
            acc[:BLOCK] += dkv_in[d, :, :HEAD_SIZE].astype(F32)
            acc[BLOCK : 2 * BLOCK] += dkv_in[d, :, HEAD_SIZE:].astype(F32)

    gkv_n[:, :HEAD_SIZE] = acc[:BLOCK].astype(BF16)
    gkv_n[:, HEAD_SIZE:] = acc[BLOCK : 2 * BLOCK].astype(BF16)

    @pl.loop(1, n_tp + 1)
    def _(i):
        p = lax.rem(t + i, n_tp)
        share = feat_f[p] + mm(gkv_n[...], wq[pl.ds(p * part, part), heads:], NT)
        feat_out[p] = share.astype(BF16)

        @pl.when(i < n_tp)
        def _():
            f_ex[3](p).start()

    kz_ex[0]()
    gkv_z[pl.ds(z * BLOCK, BLOCK)] = gkv_n[...]
    feat_in[t] = feat_out[t]
    f_ex[1]()
    feature = jnp.zeros((BLOCK, part), F32)
    for p in range(n_tp):
        feature = feature + feat_in[p].astype(F32)
    inv = inv_b[:, :1]
    gain = gain_ref[:, pl.ds(pl.multiple_of(t * part, part), part)]
    scaled = feature * gain
    normed = x_ref[...].astype(F32) * inv
    row_sum = jnp.sum(scaled * normed, axis=1, keepdims=True)
    rs_out[...] = jnp.broadcast_to(row_sum, (BLOCK, BLOCK)).T[:8]
    r_ex[0]()
    rs_in[t] = rs_out[...]
    r_ex[1]()
    total = rs_in[0]
    for p in range(1, n_tp):
        total = total + rs_in[p]
    mean = jnp.broadcast_to(total[:1] / width, (BLOCK, BLOCK)).T[:, :1]
    gin_ref[...] = (cot_loc[...].astype(F32) + inv * (scaled - normed * mean)).astype(BF16)

    @pl.when(s == 1)
    def _():
        sec_copy.start()

    hz_ex[1]()
    az_ex[1]()
    cz_ex[1]()
    qz_ex[1]()
    kz_ex[1]()
    mate = {"ctx": z * 2 + 1 - lo}
    y_copies = [
        remote(y_out_o, y_in_o, y_s.at[0], y_r.at[0], mate),
        remote(y_out_q, y_in_q, y_s.at[1], y_r.at[1], mate),
        remote(y_out_k, y_in_k, y_s.at[2], y_r.at[2], mate),
    ]
    theirs = pl.ds(pl.multiple_of((1 - lo) * half, half), half)
    mine = pl.ds(pl.multiple_of(lo * half, half), half)
    step = min(256, heads)
    plan = [
        (cot_z, att_z, y_out_o, y_in_o, gout_ref, 0, y_copies[0]),
        (hid_z, gq_z, y_out_q, y_in_q, gqkv_ref, 0, y_copies[1]),
        (hid_z, gkv_z, y_out_k, y_in_k, gqkv_ref, heads, y_copies[2]),
    ]
    for left, right, y_out, _, _, _, copy in plan:
        for k in range(0, right.shape[1], step):
            y_out[:, k : k + step] = mm(left[:, theirs], right[:, k : k + step], TN).astype(BF16)
        copy.start()
    for left, right, _, y_in, out, base, copy in plan:
        for k in range(0, right.shape[1], step):
            out[:, base + k : base + k + step] = mm(left[:, mine], right[:, k : k + step], TN)
        copy.wait_recv()
        for k in range(0, right.shape[1], step):
            out[:, base + k : base + k + step] += y_in[:, k : k + step].astype(F32)

    for ex in (x_ex, c_ex, f_ex, r_ex, hz_ex, cz_ex, az_ex, qz_ex, kz_ex):
        ex[2]()
    for copy in y_copies:
        copy.wait_send()

    @pl.loop(1, window)
    def _(d):
        @pl.when(c + d < n_ctx)
        def _():
            kv_copy(d).wait_send()

        @pl.when(c - d >= 0)
        def _():
            dkv_copy(d).wait_send()

    @pl.when(s == 1)
    def _():
        sec_copy.wait_send()


def body(layer_input, loss_cot, token_weights, doc_blocks, norm_gain, qkv_weight, out_weight):
    n_ctx, n_tp = lax.axis_size("ctx"), lax.axis_size("tp")
    n_z = n_ctx // 2
    part = layer_input.shape[3]
    width = part * n_tp
    cols, heads = qkv_weight.shape[2], out_weight.shape[2]
    window = min(MAX_DOC, n_ctx)
    q_rows = GROUP_HEADS * BLOCK
    kv_cols = 2 * HEAD_SIZE
    half = part // 2
    vmem = lambda shape, dtype=BF16: pltpu.VMEM(shape, dtype)
    dma = lambda *n: pltpu.SemaphoreType.DMA(n)
    scratch = [
        vmem((width, cols)), vmem((width, heads)),
        vmem((n_tp, BLOCK, part)), vmem((n_tp, BLOCK, part)), vmem((BLOCK, part)), vmem((BLOCK, BLOCK), F32),
        vmem((window, BLOCK, kv_cols)),
        vmem((q_rows, HEAD_SIZE)), vmem((q_rows, HEAD_SIZE)), vmem((q_rows, HEAD_SIZE)),
        vmem((BLOCK, heads)), vmem((BLOCK, heads)), vmem((BLOCK, kv_cols)),
        vmem((window, q_rows, BLOCK), F32), vmem((window, q_rows, BLOCK)),
        vmem((q_rows, BLOCK), F32), vmem((q_rows, BLOCK), F32), vmem((q_rows, HEAD_SIZE), F32),
        vmem((window, BLOCK, kv_cols)), vmem((window, BLOCK, kv_cols)),
        vmem((n_tp, BLOCK, part), F32), vmem((n_tp, BLOCK, part)), vmem((n_tp, BLOCK, part)),
        vmem((8, BLOCK), F32), vmem((n_tp, 8, BLOCK), F32),
        vmem((n_z * BLOCK, part)), vmem((n_z * BLOCK, part)), vmem((n_z * BLOCK, heads)),
        vmem((n_z * BLOCK, heads)), vmem((n_z * BLOCK, kv_cols)),
        vmem((half, heads)), vmem((half, heads)), vmem((half, kv_cols)),
        vmem((half, heads)), vmem((half, heads)), vmem((half, kv_cols)),
        dma(2), dma(n_tp), dma(n_tp), dma(n_tp), dma(n_tp), dma(window), dma(window), dma(window), dma(window),
        dma(n_tp), dma(n_tp), dma(n_tp), dma(n_tp),
        dma(n_z), dma(n_z), dma(n_z), dma(n_z), dma(n_z), dma(n_z), dma(n_z), dma(n_z), dma(n_z), dma(n_z),
        dma(3), dma(3), pltpu.SemaphoreType.DMA, pltpu.SemaphoreType.DMA,
    ]
    in_vmem = pl.BlockSpec(memory_space=pltpu.VMEM)
    anywhere = pl.BlockSpec(memory_space=pl.ANY)
    grad_in, grad_qkv, grad_out = pl.pallas_call(
        functools.partial(kernel, n_ctx, n_tp, window),
        out_shape=(
            jax.ShapeDtypeStruct((BLOCK, part), BF16),
            jax.ShapeDtypeStruct((half, cols), F32),
            jax.ShapeDtypeStruct((half, heads), F32),
        ),
        in_specs=[
            in_vmem, in_vmem, in_vmem, pl.BlockSpec(memory_space=pltpu.SMEM), in_vmem, anywhere, anywhere,
        ],
        out_specs=(in_vmem, in_vmem, in_vmem),
        scratch_shapes=scratch,
        compiler_params=pltpu.CompilerParams(
            collective_id=0, has_side_effects=True, vmem_limit_bytes=56 * 1024 * 1024
        ),
    )(
        layer_input[0, 0], loss_cot[0], token_weights, doc_blocks, norm_gain, qkv_weight[0], out_weight[0]
    )
    return grad_in[None, None], grad_qkv[None], grad_out[None]


def solution(mesh):
    placed = (
        P("section", None, "ctx", "tp"),
        P(None, "ctx", "tp"),
        P(None, "ctx"),
        P(),
        P("section", None),
        P("section", None, "tp"),
        P("section", None, "tp"),
    )
    return jax.shard_map(
        body,
        mesh=mesh,
        in_specs=placed,
        out_specs=(
            P("section", None, "ctx", "tp"),
            P("section", "ctx", "tp"),
            P("section", "ctx", "tp"),
        ),
        check_vma=False,
    )
```

```python
import functools

import jax
import jax.numpy as jnp
from jax import lax
from jax.experimental import pallas as pl
from jax.experimental.pallas import tpu as pltpu
from jax.sharding import PartitionSpec as P

MESH = pl.DeviceIdType.MESH
GROUP_HEADS = 4
HEAD_SIZE = 128
BLOCK = 128
MAX_DOC = 10
EPSILON = 1e-05
NEG_FILL = -1e30
F32 = jnp.float32
BF16 = jnp.bfloat16

NN = (((1,), (0,)), ((), ()))
NT = (((1,), (1,)), ((), ()))
TN = (((0,), (0,)), ((), ()))


def mm(a, b, dims=NN):
    return lax.dot_general(a, b, dims, preferred_element_type=F32)


def kernel(
    n_ctx, n_tp, window,
    x_ref, loss_ref, tw_ref, docs_ref, gain_ref, wq_hbm, wo_hbm,
    gin_ref, gqkv_ref, gout_ref,
    wq, wo, xfull, cotfull, cot_loc, inv_b,
    kv, q_s, hc_s, att_s, gq_n, gkv_n, scores, probs, peak, denom, acc,
    dkv_part, dkv_in, feat_f, feat_out, feat_in, rs_out, rs_in,
    hid_p, cot_p, hid_z, cot_z, att_z, gq_z, gkv_z, turned,
    y_out_o, y_out_q, y_out_k, y_in_o, y_in_q, y_in_k,
    w_sem, x_s, x_r, c_s, c_r, kv_s, kv_r, d_s, d_r, f_s, f_r, r_s, r_r,
    h1_s, h1_r, h2_s, h2_r, c1_s, c1_r, c2_s, c2_r, az_s, az_r, qz_s, qz_r, kz_s, kz_r, y_s, y_r, sec_s, sec_r, gate,
):
    s = lax.axis_index("section")
    c = lax.axis_index("ctx")
    t = lax.axis_index("tp")
    n_z = n_ctx // 2
    z, lo = c // 2, lax.rem(c, 2)
    part = x_ref.shape[1]
    width = part * n_tp
    half = part // 2
    heads = GROUP_HEADS * HEAD_SIZE
    cols = heads + 2 * HEAD_SIZE
    scale = HEAD_SIZE ** (-0.5)
    last = window - 1

    def remote(src, dst, ss, rs, dev):
        return pltpu.make_async_remote_copy(
            src_ref=src, dst_ref=dst, send_sem=ss, recv_sem=rs, device_id=dev, device_id_type=MESH
        )

    def tp_dev(p):
        return {"tp": p}

    def z_dev(p):
        return {"ctx": p * 2 + lo}

    def exchange(n, me, dev, src_of, slot, ss, rs):
        def copy_to(p):
            return remote(src_of(p), slot(me), ss.at[p], rs.at[me], dev(p))

        def copy_from(p):
            return remote(slot(p), slot(p), ss.at[p], rs.at[p], dev(p))

        def start():
            @pl.loop(1, n)
            def _(i):
                copy_to(lax.rem(me + i, n)).start()

        def wait_recv():
            @pl.loop(1, n)
            def _(i):
                copy_from(lax.rem(me + i, n)).wait_recv()

        def wait_send():
            @pl.loop(1, n)
            def _(i):
                copy_to(lax.rem(me + i, n)).wait_send()

        return start, wait_recv, wait_send, copy_to

    def ring(ref, ss, rs):
        up, down = z_dev(lax.rem(z + 1, n_z)), z_dev(lax.rem(z + n_z - 1, n_z))
        top = n_z // 2

        def piece(p, k, side):
            if k < top:
                return ref.at[pl.ds(p * BLOCK, BLOCK)]
            return ref.at[pl.ds(p * BLOCK + side * (BLOCK // 2), BLOCK // 2)]

        def pair(k, shift):
            below = piece(lax.rem(z - k + shift + n_z, n_z), k, 0)
            above = piece(lax.rem(z + k - shift, n_z), k, 1)
            return (
                remote(below, below, ss.at[k - 1], rs.at[k - 1], up),
                remote(above, above, ss.at[top + k - 1], rs.at[top + k - 1], down),
            )

        def arrive(k):
            for copy in pair(k, 0):
                copy.wait_recv()

        def stage(k):
            if k > top:
                return
            if k > 1:
                arrive(k - 1)
            for copy in pair(k, 1):
                copy.start()

        def wait_send():
            for k in range(1, top + 1):
                for copy in pair(k, 1):
                    copy.wait_send()

        return stage, lambda: arrive(top), wait_send

    whole = lambda ref: lambda p: ref
    share = BLOCK // n_tp
    my_rows = pl.ds(pl.multiple_of(t * share, share), share)

    x_ex = exchange(n_tp, t, tp_dev, whole(x_ref), lambda p: xfull.at[p], x_s, x_r)
    c_ex = exchange(n_tp, t, tp_dev, whole(cot_loc), lambda p: cotfull.at[p], c_s, c_r)
    f_ex = exchange(n_tp, t, tp_dev, lambda p: feat_out.at[p], lambda p: feat_in.at[p], f_s, f_r)
    r_ex = exchange(n_tp, t, tp_dev, whole(rs_out), lambda p: rs_in.at[p], r_s, r_r)
    h1_ex = exchange(n_z, z, z_dev, lambda p: xfull.at[p, my_rows], lambda p: hid_p.at[p], h1_s, h1_r)
    h2_ex = exchange(n_tp, t, tp_dev, whole(hid_p), lambda p: hid_z.at[:, p], h2_s, h2_r)
    c1_ex = exchange(n_z, z, z_dev, lambda p: cotfull.at[p, my_rows], lambda p: cot_p.at[p], c1_s, c1_r)
    c2_ex = exchange(n_tp, t, tp_dev, whole(cot_p), lambda p: cot_z.at[:, p], c2_s, c2_r)
    att_ring = ring(att_z, az_s, az_r)
    gq_ring = ring(gq_z, qz_s, qz_r)
    gkv_ring = ring(gkv_z, kz_s, kz_r)
    own_z = pl.ds(pl.multiple_of(z * BLOCK, BLOCK), BLOCK)
    wq_copy = pltpu.make_async_copy(wq_hbm, wq, w_sem.at[0])
    wo_copy = pltpu.make_async_copy(wo_hbm, wo, w_sem.at[1])

    wq_copy.start()
    wo_copy.start()
    kv[...] = jnp.zeros_like(kv)

    barrier = pltpu.get_barrier_semaphore()

    @pl.loop(1, n_tp)
    def _(i):
        pl.semaphore_signal(barrier, inc=1, device_id={"tp": lax.rem(t + i, n_tp)}, device_id_type=MESH)

    @pl.loop(1, n_ctx)
    def _(i):
        pl.semaphore_signal(barrier, inc=1, device_id={"ctx": lax.rem(c + i, n_ctx)}, device_id_type=MESH)

    pl.semaphore_signal(barrier, inc=1, device_id={"section": 1 - s}, device_id_type=MESH)
    pl.semaphore_wait(barrier, n_tp + n_ctx - 1)

    @pl.when(s == 0)
    def _():
        pl.semaphore_wait(gate, 1)

    x_ex[0]()
    xfull[t] = x_ref[...]

    @pl.when(s == 1)
    def _():
        weights = jnp.broadcast_to(tw_ref[...].astype(F32), (BLOCK, BLOCK)).T[:, :1]
        cot_loc[...] = (loss_ref[...].astype(F32) * weights).astype(BF16)
        c_ex[0]()

    x_ex[1]()

    @pl.when(s == 1)
    def _():
        pl.semaphore_signal(gate, inc=1, device_id={"section": 1 - s}, device_id_type=MESH)

    square = jnp.zeros((BLOCK, part), F32)
    for p in range(n_tp):
        wide = xfull[p].astype(F32)
        square = square + wide * wide
    inv = lax.rsqrt(jnp.sum(square, axis=1, keepdims=True) / width + EPSILON)
    inv_b[...] = jnp.broadcast_to(inv, inv_b.shape)
    for p in range(n_tp):
        gain = gain_ref[:, p * part : (p + 1) * part]
        xfull[p] = ((xfull[p].astype(F32) * inv) * gain).astype(BF16)

    def project(full, weight, lo_col, n_col):
        total = jnp.zeros((BLOCK, n_col), F32)
        for p in range(n_tp):
            total = total + mm(full[p], weight[p * part : (p + 1) * part, lo_col : lo_col + n_col])
        return total.astype(BF16)

    def slot(j):
        if isinstance(j, int):
            return pl.ds(j * BLOCK, BLOCK)
        return pl.ds(pl.multiple_of(j * BLOCK, BLOCK), BLOCK)

    wq_copy.wait()
    kv[slot(last)] = project(xfull, wq, heads, 2 * HEAD_SIZE)

    def kv_copy(d):
        return remote(
            kv.at[slot(last)], kv.at[slot(last - d)], kv_s.at[d], kv_r.at[d], {"ctx": lax.rem(c + d, n_ctx)}
        )

    @pl.loop(1, window)
    def _(d):
        @pl.when(c + d < n_ctx)
        def _():
            kv_copy(d).start()

    for j in range(0, GROUP_HEADS, 2):
        pair = project(xfull, wq, j * HEAD_SIZE, 2 * HEAD_SIZE)
        q_s[j * BLOCK : (j + 1) * BLOCK] = pair[:, :HEAD_SIZE]
        q_s[(j + 1) * BLOCK : (j + 2) * BLOCK] = pair[:, HEAD_SIZE:]
    h1_ex[0]()
    hid_p[z] = xfull[z, my_rows]

    doc_start = jnp.int32(0)
    doc_end = jnp.int32(0)
    for i in range(docs_ref.shape[1]):
        doc_end = doc_end + docs_ref[0, i]
        doc_start = jnp.where(doc_end <= c, doc_end, doc_start)
    pairs = window // 2
    wide = (GROUP_HEADS * BLOCK, 2 * BLOCK)
    query_pos = c * BLOCK + lax.broadcasted_iota(jnp.int32, wide, 0) % BLOCK
    first_key = (c - last) * BLOCK + lax.broadcasted_iota(jnp.int32, wide, 1)

    def keys(g):
        return kv[g * 2 * BLOCK : (g + 1) * 2 * BLOCK, :HEAD_SIZE]

    def values(g):
        return kv[g * 2 * BLOCK : (g + 1) * 2 * BLOCK, HEAD_SIZE:]

    for g in range(pairs - 1, -1, -1):
        for j in (2 * g + 1, 2 * g):
            if j < last:

                @pl.when(c - last + j >= 0)
                def _():
                    kv_copy(last - j).wait_recv()

        block = mm(q_s[...], keys(g), NT) * scale
        key_pos = first_key + g * 2 * BLOCK
        block = jnp.where((key_pos <= query_pos) & (key_pos >= doc_start * BLOCK), block, NEG_FILL)
        scores[g] = block
        both = jnp.maximum(block[:, :BLOCK], block[:, BLOCK:])
        peak[...] = both if g == pairs - 1 else jnp.maximum(peak[...], both)

    top = jnp.max(peak[...], axis=1, keepdims=True)
    for g in range(pairs):
        e = jnp.exp(scores[g] - top)
        scores[g] = e
        both = e[:, :BLOCK] + e[:, BLOCK:]
        denom[...] = both if g == 0 else denom[...] + both

    inverse = 1.0 / jnp.sum(denom[...], axis=1, keepdims=True)
    for g in range(pairs):
        soft = scores[g] * inverse
        low = soft.astype(BF16)
        scores[g] = soft
        probs[g] = low
        term = mm(low, values(g))
        acc[...] = term if g == 0 else acc[...] + term

    att_s[...] = acc[...].astype(BF16)
    for j in range(GROUP_HEADS):
        att_z[own_z, j * HEAD_SIZE : (j + 1) * HEAD_SIZE] = att_s[j * BLOCK : (j + 1) * BLOCK]
    att_ring[0](1)
    h1_ex[1]()
    h2_ex[0]()
    hid_z[:, t] = hid_p[...]

    sec_copy = remote(gin_ref, cot_loc, sec_s, sec_r, {"section": 1 - s})

    @pl.when(s == 0)
    def _():
        for k in range(2, n_z // 2 + 1):
            att_ring[0](k)
        sec_copy.wait_recv()
        c_ex[0]()

    cotfull[t] = cot_loc[...]
    wo_copy.wait()
    c_ex[1]()
    for j in range(0, GROUP_HEADS, 2):
        pair = project(cotfull, wo, j * HEAD_SIZE, 2 * HEAD_SIZE)
        hc_s[j * BLOCK : (j + 1) * BLOCK] = pair[:, :HEAD_SIZE]
        hc_s[(j + 1) * BLOCK : (j + 2) * BLOCK] = pair[:, HEAD_SIZE:]

    delta = jnp.sum(hc_s[...].astype(F32) * att_s[...].astype(F32), axis=1, keepdims=True)

    def dkv_copy(d):
        return remote(
            dkv_part.at[slot(last - d)], dkv_in.at[d], d_s.at[d], d_r.at[d],
            {"ctx": lax.rem(c - d + n_ctx, n_ctx)},
        )

    for g in range(pairs):
        block = slice(g * 2 * BLOCK, (g + 1) * 2 * BLOCK)
        dprobs = mm(hc_s[...], values(g), NT)
        ds = (scores[g] * (dprobs - delta)).astype(BF16)
        dkv_part[block, :HEAD_SIZE] = (mm(ds, q_s[...], TN) * scale).astype(BF16)
        dkv_part[block, HEAD_SIZE:] = mm(probs[g], hc_s[...], TN).astype(BF16)
        term = mm(ds, keys(g))
        acc[...] = term if g == 0 else acc[...] + term
        for j in (2 * g, 2 * g + 1):
            if j < last:

                @pl.when(c - last + j >= 0)
                def _():
                    dkv_copy(last - j).start()

    for j in range(GROUP_HEADS):
        gq_n[:, j * HEAD_SIZE : (j + 1) * HEAD_SIZE] = (
            acc[j * BLOCK : (j + 1) * BLOCK] * scale
        ).astype(BF16)
    c1_ex[0]()
    gq_z[own_z] = gq_n[...]
    gq_ring[0](1)
    cot_p[z] = cotfull[z, my_rows]

    @pl.loop(0, n_tp)
    def _(p):
        feat_f[p] = mm(gq_n[...], wq[pl.ds(p * part, part), :heads], NT)

    c1_ex[1]()
    c2_ex[0]()
    cot_z[:, t] = cot_p[...]

    @pl.when(s == 0)
    def _():
        gq_ring[0](2)

    acc[:BLOCK] = dkv_part[slot(last), :HEAD_SIZE].astype(F32)
    acc[BLOCK : 2 * BLOCK] = dkv_part[slot(last), HEAD_SIZE:].astype(F32)

    @pl.loop(1, window)
    def _(d):
        @pl.when(c + d < n_ctx)
        def _():
            dkv_copy(d).wait_recv()
            acc[:BLOCK] += dkv_in[d, :, :HEAD_SIZE].astype(F32)
            acc[BLOCK : 2 * BLOCK] += dkv_in[d, :, HEAD_SIZE:].astype(F32)

    gkv_n[:, :HEAD_SIZE] = acc[:BLOCK].astype(BF16)
    gkv_n[:, HEAD_SIZE:] = acc[BLOCK : 2 * BLOCK].astype(BF16)
    gkv_z[own_z] = gkv_n[...]
    gkv_ring[0](1)

    @pl.loop(1, n_tp + 1)
    def _(i):
        p = lax.rem(t + i, n_tp)
        total = feat_f[p] + mm(gkv_n[...], wq[pl.ds(p * part, part), heads:], NT)
        feat_out[p] = total.astype(BF16)

        @pl.when(i < n_tp)
        def _():
            f_ex[3](p).start()

    feat_in[t] = feat_out[t]

    mate = {"ctx": z * 2 + 1 - lo}
    y_copies = [
        remote(y_out_o, y_in_o, y_s.at[0], y_r.at[0], mate),
        remote(y_out_q, y_in_q, y_s.at[1], y_r.at[1], mate),
        remote(y_out_k, y_in_k, y_s.at[2], y_r.at[2], mate),
    ]
    positions = n_z * BLOCK
    theirs = pl.ds(pl.multiple_of((1 - lo) * half, half), half)
    mine = pl.ds(pl.multiple_of(lo * half, half), half)

    def turn(ref):
        turned[...] = ref[...].reshape(positions, part).T

    def weight_part(right, y_out, out, base, copy):
        step = min(256, heads)
        for k in range(0, right.shape[1], step):
            y_out[:, k : k + step] = mm(turned[theirs], right[:, k : k + step]).astype(BF16)
        copy.start()
        for k in range(0, right.shape[1], step):
            out[:, base + k : base + k + step] = mm(turned[mine], right[:, k : k + step])

    def grad_of_out():
        c2_ex[1]()
        att_ring[1]()
        turn(cot_z)
        weight_part(att_z, y_out_o, gout_ref, 0, y_copies[0])
        h2_ex[1]()
        turn(hid_z)

    @pl.when(s == 0)
    def _():
        gq_ring[0](3)
        gkv_ring[0](2)
        grad_of_out()
        gq_ring[0](4)
        gkv_ring[0](3)

    f_ex[1]()
    feature = jnp.zeros((BLOCK, part), F32)
    for p in range(n_tp):
        feature = feature + feat_in[p].astype(F32)
    inv = inv_b[:, :1]
    gain = gain_ref[:, pl.ds(pl.multiple_of(t * part, part), part)]
    scaled = feature * gain
    normed = x_ref[...].astype(F32) * inv
    row_sum = jnp.sum(scaled * normed, axis=1, keepdims=True)
    rs_out[...] = jnp.broadcast_to(row_sum, (BLOCK, BLOCK)).T[:8]
    r_ex[0]()
    rs_in[t] = rs_out[...]
    r_ex[1]()
    total = rs_in[0]
    for p in range(1, n_tp):
        total = total + rs_in[p]
    mean = jnp.broadcast_to(total[:1] / width, (BLOCK, BLOCK)).T[:, :1]
    gin_ref[...] = (cot_loc[...].astype(F32) + inv * (scaled - normed * mean)).astype(BF16)

    @pl.when(s == 1)
    def _():
        sec_copy.start()

    @pl.when(s == 0)
    def _():
        gkv_ring[0](4)

    @pl.when(s == 1)
    def _():
        for k in range(2, n_z // 2 + 1):
            att_ring[0](k)
            gq_ring[0](k)
            gkv_ring[0](k)
        grad_of_out()

    gq_ring[1]()
    weight_part(gq_z, y_out_q, gqkv_ref, 0, y_copies[1])
    gkv_ring[1]()
    weight_part(gkv_z, y_out_k, gqkv_ref, heads, y_copies[2])
    for y_in, out, base, copy in (
        (y_in_o, gout_ref, 0, y_copies[0]),
        (y_in_q, gqkv_ref, 0, y_copies[1]),
        (y_in_k, gqkv_ref, heads, y_copies[2]),
    ):
        copy.wait_recv()
        out[:, base : base + y_in.shape[1]] += y_in[...].astype(F32)

    for ex in (x_ex, c_ex, f_ex, r_ex, h1_ex, h2_ex, c1_ex, c2_ex, att_ring, gq_ring, gkv_ring):
        ex[2]()
    for copy in y_copies:
        copy.wait_send()

    @pl.loop(1, window)
    def _(d):
        @pl.when(c + d < n_ctx)
        def _():
            kv_copy(d).wait_send()

        @pl.when(c - d >= 0)
        def _():
            dkv_copy(d).wait_send()

    @pl.when(s == 1)
    def _():
        sec_copy.wait_send()


def settle(a_in, b_in, c_in, a_out, b_out, c_out, sem):
    copies = [
        pltpu.make_async_copy(source, target, sem.at[i])
        for i, (source, target) in enumerate(((a_in, a_out), (b_in, b_out), (c_in, c_out)))
    ]
    for copy in copies:
        copy.start()
    for copy in copies:
        copy.wait()


def body(layer_input, loss_cot, token_weights, doc_blocks, norm_gain, qkv_weight, out_weight):
    n_ctx, n_tp = lax.axis_size("ctx"), lax.axis_size("tp")
    n_z = n_ctx // 2
    part = layer_input.shape[3]
    width = part * n_tp
    cols, heads = qkv_weight.shape[2], out_weight.shape[2]
    window = min(MAX_DOC, n_ctx)
    q_rows = GROUP_HEADS * BLOCK
    kv_cols = 2 * HEAD_SIZE
    half = part // 2
    share = BLOCK // n_tp
    vmem = lambda shape, dtype=BF16: pltpu.VMEM(shape, dtype)
    dma = lambda *n: pltpu.SemaphoreType.DMA(n)
    scratch = [
        vmem((width, cols)), vmem((width, heads)),
        vmem((n_tp, BLOCK, part)), vmem((n_tp, BLOCK, part)), vmem((BLOCK, part)), vmem((BLOCK, BLOCK), F32),
        vmem((window * BLOCK, kv_cols)),
        vmem((q_rows, HEAD_SIZE)), vmem((q_rows, HEAD_SIZE)), vmem((q_rows, HEAD_SIZE)),
        vmem((BLOCK, heads)), vmem((BLOCK, kv_cols)),
        vmem((window // 2, q_rows, 2 * BLOCK), F32), vmem((window // 2, q_rows, 2 * BLOCK)),
        vmem((q_rows, BLOCK), F32), vmem((q_rows, BLOCK), F32), vmem((q_rows, HEAD_SIZE), F32),
        vmem((window * BLOCK, kv_cols)), vmem((window, BLOCK, kv_cols)),
        vmem((n_tp, BLOCK, part), F32), vmem((n_tp, BLOCK, part)), vmem((n_tp, BLOCK, part)),
        vmem((8, BLOCK), F32), vmem((n_tp, 8, BLOCK), F32),
        vmem((n_z, share, part)), vmem((n_z, share, part)),
        vmem((n_z, n_tp, share, part)), vmem((n_z, n_tp, share, part)), vmem((n_z * BLOCK, heads)),
        vmem((n_z * BLOCK, heads)), vmem((n_z * BLOCK, kv_cols)), vmem((part, n_z * BLOCK)),
        vmem((half, heads)), vmem((half, heads)), vmem((half, kv_cols)),
        vmem((half, heads)), vmem((half, heads)), vmem((half, kv_cols)),
        dma(2), dma(n_tp), dma(n_tp), dma(n_tp), dma(n_tp), dma(window), dma(window), dma(window), dma(window),
        dma(n_tp), dma(n_tp), dma(n_tp), dma(n_tp),
        dma(n_z), dma(n_z), dma(n_tp), dma(n_tp), dma(n_z), dma(n_z), dma(n_tp), dma(n_tp),
        dma(n_z), dma(n_z), dma(n_z), dma(n_z), dma(n_z), dma(n_z),
        dma(3), dma(3), pltpu.SemaphoreType.DMA, pltpu.SemaphoreType.DMA, pltpu.SemaphoreType.REGULAR,
    ]
    in_vmem = pl.BlockSpec(memory_space=pltpu.VMEM)
    anywhere = pl.BlockSpec(memory_space=pl.ANY)
    grad_in, grad_qkv, grad_out = pl.pallas_call(
        functools.partial(kernel, n_ctx, n_tp, window),
        out_shape=(
            jax.ShapeDtypeStruct((BLOCK, part), BF16),
            jax.ShapeDtypeStruct((half, cols), F32),
            jax.ShapeDtypeStruct((half, heads), F32),
        ),
        in_specs=[
            in_vmem, in_vmem, in_vmem, pl.BlockSpec(memory_space=pltpu.SMEM), in_vmem, anywhere, anywhere,
        ],
        out_specs=(in_vmem, in_vmem, in_vmem),
        scratch_shapes=scratch,
        compiler_params=pltpu.CompilerParams(
            collective_id=0, has_side_effects=True, vmem_limit_bytes=56 * 1024 * 1024
        ),
    )(
        layer_input[0, 0], loss_cot[0], token_weights, doc_blocks, norm_gain, qkv_weight[0], out_weight[0]
    )
    results = (grad_in, grad_qkv, grad_out)
    grad_in, grad_qkv, grad_out = pl.pallas_call(
        settle,
        out_shape=tuple(jax.ShapeDtypeStruct(r.shape, r.dtype) for r in results),
        in_specs=[anywhere] * 3,
        out_specs=(anywhere,) * 3,
        scratch_shapes=[dma(3)],
    )(*results)
    return grad_in[None, None], grad_qkv[None], grad_out[None]


def solution(mesh):
    placed = (
        P("section", None, "ctx", "tp"),
        P(None, "ctx", "tp"),
        P(None, "ctx"),
        P(),
        P("section", None),
        P("section", None, "tp"),
        P("section", None, "tp"),
    )
    return jax.shard_map(
        body,
        mesh=mesh,
        in_specs=placed,
        out_specs=(
            P("section", None, "ctx", "tp"),
            P("section", "ctx", "tp"),
            P("section", "ctx", "tp"),
        ),
        check_vma=False,
    )
```

```python
import functools

import jax
import jax.numpy as jnp
from jax import lax
from jax.experimental import pallas as pl
from jax.experimental.pallas import tpu as pltpu
from jax.sharding import PartitionSpec as P

MESH = pl.DeviceIdType.MESH
GROUP_HEADS = 4
HEAD_SIZE = 128
BLOCK = 128
MAX_DOC = 10
EPSILON = 1e-05
NEG_FILL = -1e30
F32 = jnp.float32
BF16 = jnp.bfloat16

NN = (((1,), (0,)), ((), ()))
NT = (((1,), (1,)), ((), ()))
TN = (((0,), (0,)), ((), ()))


def mm(a, b, dims=NN):
    return lax.dot_general(a, b, dims, preferred_element_type=F32)


def kernel(
    n_ctx, n_tp, window,
    x_ref, loss_ref, tw_ref, docs_ref, gain_ref, wq_hbm, wo_hbm,
    gin_ref, gqkv_ref, gout_ref,
    wq, wo, xfull, cotfull, cot_loc, inv_b,
    kv, q_s, hc_s, att_s, gq_n, gkv_n, scores, probs, dscores, peak, denom, acc, row_acc,
    dkv_part, dkv_in, feat_f, feat_out, feat_in, rs_out, rs_in,
    hid_p, cot_p, hid_z, cot_z, att_z, gq_z, gkv_z, turned,
    y_out_o, y_out_q, y_out_k, y_in_o, y_in_q, y_in_k,
    w_sem, x_s, x_r, c_s, c_r, kv_s, kv_r, kv_f, d_s, d_r, f_s, f_r, r_s, r_r,
    h1_s, h1_r, h2_s, h2_r, c1_s, c1_r, c2_s, c2_r, az_s, az_r, qz_s, qz_r, kz_s, kz_r, y_s, y_r, sec_s, gate,
):
    s = lax.axis_index("section")
    c = lax.axis_index("ctx")
    t = lax.axis_index("tp")
    n_z = n_ctx // 2
    z, lo = c // 2, lax.rem(c, 2)
    part = x_ref.shape[1]
    width = part * n_tp
    half = part // 2
    heads = GROUP_HEADS * HEAD_SIZE
    cols = heads + 2 * HEAD_SIZE
    scale = HEAD_SIZE ** (-0.5)
    last = window - 1

    def remote(src, dst, ss, rs, dev):
        return pltpu.make_async_remote_copy(
            src_ref=src, dst_ref=dst, send_sem=ss, recv_sem=rs, device_id=dev, device_id_type=MESH
        )

    def tp_dev(p):
        return {"tp": p}

    def z_dev(p):
        return {"ctx": p * 2 + lo}

    def exchange(n, me, dev, src_of, slot, ss, rs):
        def copy_to(p):
            return remote(src_of(p), slot(me), ss.at[p], rs.at[me], dev(p))

        def copy_from(p):
            return remote(slot(p), slot(p), ss.at[p], rs.at[p], dev(p))

        def start():
            @pl.loop(1, n)
            def _(i):
                copy_to(lax.rem(me + i, n)).start()

        def wait_recv():
            @pl.loop(1, n)
            def _(i):
                copy_from(lax.rem(me + i, n)).wait_recv()

        def wait_send():
            @pl.loop(1, n)
            def _(i):
                copy_to(lax.rem(me + i, n)).wait_send()

        return start, wait_recv, wait_send, copy_to

    def ring(ref, ss, rs):
        up, down = z_dev(lax.rem(z + 1, n_z)), z_dev(lax.rem(z + n_z - 1, n_z))
        top = n_z // 2

        def piece(p, k, side):
            if k < top:
                return ref.at[pl.ds(p * BLOCK, BLOCK)]
            return ref.at[pl.ds(p * BLOCK + side * (BLOCK // 2), BLOCK // 2)]

        def pair(k, shift):
            below = piece(lax.rem(z - k + shift + n_z, n_z), k, 0)
            above = piece(lax.rem(z + k - shift, n_z), k, 1)
            return (
                remote(below, below, ss.at[k - 1], rs.at[k - 1], up),
                remote(above, above, ss.at[top + k - 1], rs.at[top + k - 1], down),
            )

        def arrive(k):
            for copy in pair(k, 0):
                copy.wait_recv()

        def stage(k):
            if k > top:
                return
            if k > 1:
                arrive(k - 1)
            for copy in pair(k, 1):
                copy.start()

        def wait_send():
            for k in range(1, top + 1):
                for copy in pair(k, 1):
                    copy.wait_send()

        return stage, lambda: arrive(top), wait_send

    whole = lambda ref: lambda p: ref
    share = BLOCK // n_tp
    my_rows = pl.ds(pl.multiple_of(t * share, share), share)

    x_ex = exchange(n_tp, t, tp_dev, whole(x_ref), lambda p: xfull.at[p], x_s, x_r)
    c_ex = exchange(n_tp, t, tp_dev, whole(cot_loc), lambda p: cotfull.at[p], c_s, c_r)
    f_ex = exchange(n_tp, t, tp_dev, lambda p: feat_out.at[p], lambda p: feat_in.at[p], f_s, f_r)
    r_ex = exchange(n_tp, t, tp_dev, whole(rs_out), lambda p: rs_in.at[p], r_s, r_r)
    h1_ex = exchange(n_z, z, z_dev, lambda p: xfull.at[p, my_rows], lambda p: hid_p.at[p], h1_s, h1_r)
    h2_ex = exchange(n_tp, t, tp_dev, whole(hid_p), lambda p: hid_z.at[:, p], h2_s, h2_r)
    c1_ex = exchange(n_z, z, z_dev, lambda p: cotfull.at[p, my_rows], lambda p: cot_p.at[p], c1_s, c1_r)
    c2_ex = exchange(n_tp, t, tp_dev, whole(cot_p), lambda p: cot_z.at[:, p], c2_s, c2_r)
    att_ring = ring(att_z, az_s, az_r)
    gq_ring = ring(gq_z, qz_s, qz_r)
    kz_ex = exchange(n_z, z, z_dev, whole(gkv_n), lambda p: gkv_z.at[pl.ds(p * BLOCK, BLOCK)], kz_s, kz_r)
    own_z = pl.ds(pl.multiple_of(z * BLOCK, BLOCK), BLOCK)
    wq_copy = pltpu.make_async_copy(wq_hbm, wq, w_sem.at[0])
    wo_copy = pltpu.make_async_copy(wo_hbm, wo, w_sem.at[1])

    wq_copy.start()
    wo_copy.start()
    kv[...] = jnp.zeros_like(kv)

    barrier = pltpu.get_barrier_semaphore()

    @pl.loop(1, n_tp)
    def _(i):
        pl.semaphore_signal(barrier, inc=1, device_id={"tp": lax.rem(t + i, n_tp)}, device_id_type=MESH)

    @pl.loop(1, n_ctx)
    def _(i):
        pl.semaphore_signal(barrier, inc=1, device_id={"ctx": lax.rem(c + i, n_ctx)}, device_id_type=MESH)

    @pl.loop(0, n_tp)
    def _(p):
        pl.semaphore_signal(barrier, inc=1, device_id={"section": 1 - s, "tp": p}, device_id_type=MESH)

    pl.semaphore_wait(barrier, 2 * n_tp + n_ctx - 2)

    @pl.when(s == 0)
    def _():
        pl.semaphore_wait(gate, 1)

    x_ex[0]()
    xfull[t] = x_ref[...]

    @pl.when(s == 1)
    def _():
        weights = jnp.broadcast_to(tw_ref[...].astype(F32), (BLOCK, BLOCK)).T[:, :1]
        cot_loc[...] = (loss_ref[...].astype(F32) * weights).astype(BF16)
        cotfull[t] = cot_loc[...]
        c_ex[0]()

    x_ex[1]()

    @pl.when(s == 1)
    def _():
        pl.semaphore_signal(gate, inc=1, device_id={"section": 1 - s}, device_id_type=MESH)

    square = jnp.zeros((BLOCK, part), F32)
    for p in range(n_tp):
        wide = xfull[p].astype(F32)
        square = square + wide * wide
    inv = lax.rsqrt(jnp.sum(square, axis=1, keepdims=True) / width + EPSILON)
    inv_b[...] = jnp.broadcast_to(inv, inv_b.shape)
    for p in range(n_tp):
        gain = gain_ref[:, p * part : (p + 1) * part]
        xfull[p] = ((xfull[p].astype(F32) * inv) * gain).astype(BF16)

    def project(full, weight, lo_col, n_col):
        total = jnp.zeros((BLOCK, n_col), F32)
        for p in range(n_tp):
            total = total + mm(full[p], weight[p * part : (p + 1) * part, lo_col : lo_col + n_col])
        return total.astype(BF16)

    def slot(j):
        if isinstance(j, int):
            return pl.ds(j * BLOCK, BLOCK)
        return pl.ds(pl.multiple_of(j * BLOCK, BLOCK), BLOCK)

    wq_copy.wait()
    kv[slot(last)] = project(xfull, wq, heads, 2 * HEAD_SIZE)

    steps_z = (window - 1) // 2 + 1
    mate = {"ctx": z * 2 + 1 - lo}
    far = window - 1

    def kv_up(k):
        return remote(
            kv.at[slot(last)], kv.at[slot(last - 2 * k)], kv_s.at[2 * k], kv_r.at[2 * k],
            {"ctx": lax.rem(c + 2 * k, n_ctx)},
        )

    def kv_on(k):
        away = 2 * k + 1 - 2 * lo
        return remote(
            kv.at[slot(last - 2 * k)], kv.at[slot(last - away)], kv_s.at[2 * k + 1], kv_r.at[away], mate
        )

    def kv_far():
        return remote(
            kv.at[slot(last)], kv.at[slot(last - far)], kv_f.at[0], kv_r.at[far],
            {"ctx": lax.rem(c + far, n_ctx)},
        )

    def kv_arrival(d):
        return remote(
            kv.at[slot(last - d)], kv.at[slot(last - d)], kv_s.at[0], kv_r.at[d], mate
        )

    @pl.loop(1, steps_z)
    def _(i):
        k = steps_z - i

        @pl.when(z + k < n_z)
        def _():
            kv_up(k).start()

    @pl.when((lo == 1) & (c + far < n_ctx))
    def _():
        kv_far().start()

    @pl.when(lo == 0)
    def _():
        kv_on(0).start()

    for j in range(0, GROUP_HEADS, 2):
        pair = project(xfull, wq, j * HEAD_SIZE, 2 * HEAD_SIZE)
        q_s[j * BLOCK : (j + 1) * BLOCK] = pair[:, :HEAD_SIZE]
        q_s[(j + 1) * BLOCK : (j + 2) * BLOCK] = pair[:, HEAD_SIZE:]
    h1_ex[0]()
    hid_p[z] = xfull[z, my_rows]

    def pass_hidden():
        h1_ex[1]()
        h2_ex[0]()
        hid_z[:, t] = hid_p[...]

    def head_cotangent():
        wo_copy.wait()
        for j in range(0, GROUP_HEADS, 2):
            pair = project(cotfull, wo, j * HEAD_SIZE, 2 * HEAD_SIZE)
            hc_s[j * BLOCK : (j + 1) * BLOCK] = pair[:, :HEAD_SIZE]
            hc_s[(j + 1) * BLOCK : (j + 2) * BLOCK] = pair[:, HEAD_SIZE:]

    @pl.loop(1, steps_z)
    def _(k):
        @pl.when(z - k >= 0)
        def _():
            kv_up(k).wait_recv()
            kv_on(k).start()

    @pl.when(s == 0)
    def _():
        pass_hidden()

    @pl.when(s == 1)
    def _():
        c_ex[1]()
        head_cotangent()

    doc_start = jnp.int32(0)
    doc_end = jnp.int32(0)
    for i in range(docs_ref.shape[1]):
        doc_end = doc_end + docs_ref[0, i]
        doc_start = jnp.where(doc_end <= c, doc_end, doc_start)
    pairs = window // 2
    wide = (GROUP_HEADS * BLOCK, 2 * BLOCK)
    query_pos = c * BLOCK + lax.broadcasted_iota(jnp.int32, wide, 0) % BLOCK
    first_key = (c - last) * BLOCK + lax.broadcasted_iota(jnp.int32, wide, 1)

    def keys(g):
        return kv[g * 2 * BLOCK : (g + 1) * 2 * BLOCK, :HEAD_SIZE]

    def values(g):
        return kv[g * 2 * BLOCK : (g + 1) * 2 * BLOCK, HEAD_SIZE:]

    for g in range(pairs - 1, -1, -1):
        for j in (2 * g + 1, 2 * g):
            if j < last:

                if (last - j) % 2 == 1:

                    @pl.when(c - last + j >= 0)
                    def _():
                        kv_arrival(last - j).wait_recv()

        block = mm(q_s[...], keys(g), NT) * scale
        key_pos = first_key + g * 2 * BLOCK
        block = jnp.where((key_pos <= query_pos) & (key_pos >= doc_start * BLOCK), block, NEG_FILL)
        scores[g] = block
        both = jnp.maximum(block[:, :BLOCK], block[:, BLOCK:])
        peak[...] = both if g == pairs - 1 else jnp.maximum(peak[...], both)

    top = jnp.max(peak[...], axis=1, keepdims=True)
    for g in range(pairs):
        e = jnp.exp(scores[g] - top)
        scores[g] = e
        both = e[:, :BLOCK] + e[:, BLOCK:]
        denom[...] = both if g == 0 else denom[...] + both

    inverse = 1.0 / jnp.sum(denom[...], axis=1, keepdims=True)
    for g in range(pairs):
        soft = scores[g] * inverse
        low = soft.astype(BF16)
        scores[g] = soft
        probs[g] = low
        term = mm(low, values(g))
        acc[...] = term if g == 0 else acc[...] + term

    att_s[...] = acc[...].astype(BF16)
    for j in range(GROUP_HEADS):
        att_z[own_z, j * HEAD_SIZE : (j + 1) * HEAD_SIZE] = att_s[j * BLOCK : (j + 1) * BLOCK]

    def sec_copy(p):
        return remote(gin_ref, cotfull.at[t], sec_s.at[p], c_r.at[t], {"section": 1 - s, "tp": p})

    @pl.when(s == 1)
    def _():
        pass_hidden()

    @pl.when(s == 0)
    def _():
        for k in range(1, n_z // 2 + 1):
            att_ring[0](k)

        @pl.loop(0, n_tp)
        def _(p):
            remote(cotfull.at[p], cotfull.at[p], sec_s.at[p], c_r.at[p], {"section": 1 - s}).wait_recv()

        head_cotangent()

    delta = jnp.sum(hc_s[...].astype(F32) * att_s[...].astype(F32), axis=1, keepdims=True)

    def dkv_copy(d):
        return remote(
            dkv_part.at[slot(last - d)], dkv_in.at[d], d_s.at[d], d_r.at[d],
            {"ctx": lax.rem(c - d + n_ctx, n_ctx)},
        )

    for g in range(pairs):
        block = slice(g * 2 * BLOCK, (g + 1) * 2 * BLOCK)
        dprobs = mm(hc_s[...], values(g), NT)
        ds = (scores[g] * (dprobs - delta)).astype(BF16)
        dkv_part[block, :HEAD_SIZE] = (mm(ds, q_s[...], TN) * scale).astype(BF16)
        dkv_part[block, HEAD_SIZE:] = mm(probs[g], hc_s[...], TN).astype(BF16)
        dscores[g] = ds
        for j in (2 * g, 2 * g + 1):
            if j < last:

                @pl.when(c - last + j >= 0)
                def _():
                    dkv_copy(last - j).start()

    total = mm(dscores[0], keys(0))
    for g in range(1, pairs):
        total = total + mm(dscores[g], keys(g))
    acc[...] = total
    for j in range(GROUP_HEADS):
        gq_n[:, j * HEAD_SIZE : (j + 1) * HEAD_SIZE] = (
            acc[j * BLOCK : (j + 1) * BLOCK] * scale
        ).astype(BF16)
    gq_z[own_z] = gq_n[...]

    def send_cot():
        c1_ex[0]()
        cot_p[z] = cotfull[z, my_rows]

    def pass_cot():
        c1_ex[1]()
        c2_ex[0]()
        cot_z[:, t] = cot_p[...]

    @pl.when(s == 0)
    def _():
        send_cot()
        gq_ring[0](1)

    @pl.loop(0, n_tp)
    def _(p):
        feat_f[p] = mm(gq_n[...], wq[pl.ds(p * part, part), :heads], NT)

    @pl.when(s == 0)
    def _():
        pass_cot()
        gq_ring[0](2)

    acc[:BLOCK] = dkv_part[slot(last), :HEAD_SIZE].astype(F32)
    acc[BLOCK : 2 * BLOCK] = dkv_part[slot(last), HEAD_SIZE:].astype(F32)

    @pl.loop(1, window)
    def _(d):
        @pl.when(c + d < n_ctx)
        def _():
            dkv_copy(d).wait_recv()
            acc[:BLOCK] += dkv_in[d, :, :HEAD_SIZE].astype(F32)
            acc[BLOCK : 2 * BLOCK] += dkv_in[d, :, HEAD_SIZE:].astype(F32)

    gkv_n[:, :HEAD_SIZE] = acc[:BLOCK].astype(BF16)
    gkv_n[:, HEAD_SIZE:] = acc[BLOCK : 2 * BLOCK].astype(BF16)
    gkv_z[own_z] = gkv_n[...]
    kz_ex[0]()
    row_acc[...] = jnp.zeros_like(row_acc)

    @pl.loop(1, n_tp + 1)
    def _(i):
        p = lax.rem(t + i, n_tp)
        total = feat_f[p] + mm(gkv_n[...], wq[pl.ds(p * part, part), heads:], NT)
        total = total.astype(BF16)
        feat_out[p] = total
        row_acc[...] += total.astype(F32) * xfull[p].astype(F32)

        @pl.when(i < n_tp)
        def _():
            f_ex[3](p).start()

    row_sum = jnp.sum(row_acc[...], axis=1, keepdims=True)
    rs_out[...] = jnp.broadcast_to(row_sum, (BLOCK, BLOCK)).T[:8]
    r_ex[0]()
    rs_in[t] = rs_out[...]
    feat_in[t] = feat_out[t]

    y_copies = [
        remote(y_out_o, y_in_o, y_s.at[0], y_r.at[0], mate),
        remote(y_out_q, y_in_q, y_s.at[1], y_r.at[1], mate),
        remote(y_out_k, y_in_k, y_s.at[2], y_r.at[2], mate),
    ]
    positions = n_z * BLOCK
    theirs = pl.ds(pl.multiple_of((1 - lo) * half, half), half)
    mine = pl.ds(pl.multiple_of(lo * half, half), half)

    def turn(ref):
        turned[...] = ref[...].reshape(positions, part).T

    def weight_part(right, y_out, out, base, copy):
        step = min(256, heads)
        for k in range(0, right.shape[1], step):
            y_out[:, k : k + step] = mm(turned[theirs], right[:, k : k + step]).astype(BF16)
        copy.start()
        for k in range(0, right.shape[1], step):
            out[:, base + k : base + k + step] = mm(turned[mine], right[:, k : k + step])

    def grad_of_out():
        c2_ex[1]()
        att_ring[1]()
        turn(cot_z)
        weight_part(att_z, y_out_o, gout_ref, 0, y_copies[0])

    def grad_of_query():
        h2_ex[1]()
        turn(hid_z)
        gq_ring[1]()
        weight_part(gq_z, y_out_q, gqkv_ref, 0, y_copies[1])

    @pl.when(s == 0)
    def _():
        gq_ring[0](3)
        grad_of_out()
        gq_ring[0](4)
        grad_of_query()

    f_ex[1]()
    r_ex[1]()
    feature = jnp.zeros((BLOCK, part), F32)
    for p in range(n_tp):
        feature = feature + feat_in[p].astype(F32)
    inv = inv_b[:, :1]
    gain = gain_ref[:, pl.ds(pl.multiple_of(t * part, part), part)]
    scaled = feature * gain
    normed = x_ref[...].astype(F32) * inv
    total = rs_in[0]
    for p in range(1, n_tp):
        total = total + rs_in[p]
    mean = jnp.broadcast_to(total[:1] / width, (BLOCK, BLOCK)).T[:, :1]
    gin_ref[...] = (cotfull[t].astype(F32) + inv * (scaled - normed * mean)).astype(BF16)

    @pl.when(s == 1)
    def _():
        @pl.loop(0, n_tp)
        def _(i):
            sec_copy(lax.rem(t + 1 + i, n_tp)).start()

        send_cot()
        for k in range(1, n_z // 2 + 1):
            att_ring[0](k)
            gq_ring[0](k)
            if k == 2 or n_z == 2:
                pass_cot()
        grad_of_out()
        grad_of_query()

    kz_ex[1]()
    weight_part(gkv_z, y_out_k, gqkv_ref, heads, y_copies[2])
    for y_in, out, base, copy in (
        (y_in_o, gout_ref, 0, y_copies[0]),
        (y_in_q, gqkv_ref, 0, y_copies[1]),
        (y_in_k, gqkv_ref, heads, y_copies[2]),
    ):
        copy.wait_recv()
        out[:, base : base + y_in.shape[1]] += y_in[...].astype(F32)

    for ex in (x_ex, f_ex, r_ex, h1_ex, h2_ex, c1_ex, c2_ex, kz_ex, att_ring, gq_ring):
        ex[2]()
    for copy in y_copies:
        copy.wait_send()

    @pl.loop(1, steps_z)
    def _(k):
        @pl.when(z + k < n_z)
        def _():
            kv_up(k).wait_send()

        @pl.when(z - k >= 0)
        def _():
            kv_on(k).wait_send()

    @pl.when((lo == 1) & (c + far < n_ctx))
    def _():
        kv_far().wait_send()

    @pl.when(lo == 0)
    def _():
        kv_on(0).wait_send()

    @pl.loop(1, window)
    def _(d):
        @pl.when(c - d >= 0)
        def _():
            dkv_copy(d).wait_send()

    @pl.when(s == 1)
    def _():
        c_ex[2]()

        @pl.loop(0, n_tp)
        def _(p):
            sec_copy(p).wait_send()


def settle(a_in, b_in, c_in, a_out, b_out, c_out, sem):
    copies = [
        pltpu.make_async_copy(source, target, sem.at[i])
        for i, (source, target) in enumerate(((a_in, a_out), (b_in, b_out), (c_in, c_out)))
    ]
    for copy in copies:
        copy.start()
    for copy in copies:
        copy.wait()


def body(layer_input, loss_cot, token_weights, doc_blocks, norm_gain, qkv_weight, out_weight):
    n_ctx, n_tp = lax.axis_size("ctx"), lax.axis_size("tp")
    n_z = n_ctx // 2
    part = layer_input.shape[3]
    width = part * n_tp
    cols, heads = qkv_weight.shape[2], out_weight.shape[2]
    window = min(MAX_DOC, n_ctx)
    q_rows = GROUP_HEADS * BLOCK
    kv_cols = 2 * HEAD_SIZE
    half = part // 2
    share = BLOCK // n_tp
    vmem = lambda shape, dtype=BF16: pltpu.VMEM(shape, dtype)
    dma = lambda *n: pltpu.SemaphoreType.DMA(n)
    scratch = [
        vmem((width, cols)), vmem((width, heads)),
        vmem((n_tp, BLOCK, part)), vmem((n_tp, BLOCK, part)), vmem((BLOCK, part)), vmem((BLOCK, BLOCK), F32),
        vmem((window * BLOCK, kv_cols)),
        vmem((q_rows, HEAD_SIZE)), vmem((q_rows, HEAD_SIZE)), vmem((q_rows, HEAD_SIZE)),
        vmem((BLOCK, heads)), vmem((BLOCK, kv_cols)),
        vmem((window // 2, q_rows, 2 * BLOCK), F32), vmem((window // 2, q_rows, 2 * BLOCK)),
        vmem((window // 2, q_rows, 2 * BLOCK)),
        vmem((q_rows, BLOCK), F32), vmem((q_rows, BLOCK), F32), vmem((q_rows, HEAD_SIZE), F32), vmem((BLOCK, part), F32),
        vmem((window * BLOCK, kv_cols)), vmem((window, BLOCK, kv_cols)),
        vmem((n_tp, BLOCK, part), F32), vmem((n_tp, BLOCK, part)), vmem((n_tp, BLOCK, part)),
        vmem((8, BLOCK), F32), vmem((n_tp, 8, BLOCK), F32),
        vmem((n_z, share, part)), vmem((n_z, share, part)),
        vmem((n_z, n_tp, share, part)), vmem((n_z, n_tp, share, part)), vmem((n_z * BLOCK, heads)),
        vmem((n_z * BLOCK, heads)), vmem((n_z * BLOCK, kv_cols)), vmem((part, n_z * BLOCK)),
        vmem((half, heads)), vmem((half, heads)), vmem((half, kv_cols)),
        vmem((half, heads)), vmem((half, heads)), vmem((half, kv_cols)),
        dma(2), dma(n_tp), dma(n_tp), dma(n_tp), dma(n_tp), dma(window), dma(window), dma(1), dma(window), dma(window),
        dma(n_tp), dma(n_tp), dma(n_tp), dma(n_tp),
        dma(n_z), dma(n_z), dma(n_tp), dma(n_tp), dma(n_z), dma(n_z), dma(n_tp), dma(n_tp),
        dma(n_z), dma(n_z), dma(n_z), dma(n_z), dma(n_z), dma(n_z),
        dma(3), dma(3), dma(n_tp), pltpu.SemaphoreType.REGULAR,
    ]
    in_vmem = pl.BlockSpec(memory_space=pltpu.VMEM)
    anywhere = pl.BlockSpec(memory_space=pl.ANY)
    grad_in, grad_qkv, grad_out = pl.pallas_call(
        functools.partial(kernel, n_ctx, n_tp, window),
        out_shape=(
            jax.ShapeDtypeStruct((BLOCK, part), BF16),
            jax.ShapeDtypeStruct((half, cols), F32),
            jax.ShapeDtypeStruct((half, heads), F32),
        ),
        in_specs=[
            in_vmem, in_vmem, in_vmem, pl.BlockSpec(memory_space=pltpu.SMEM), in_vmem, anywhere, anywhere,
        ],
        out_specs=(in_vmem, in_vmem, in_vmem),
        scratch_shapes=scratch,
        compiler_params=pltpu.CompilerParams(
            collective_id=0, has_side_effects=True, vmem_limit_bytes=56 * 1024 * 1024
        ),
    )(
        layer_input[0, 0], loss_cot[0], token_weights, doc_blocks, norm_gain, qkv_weight[0], out_weight[0]
    )
    results = (grad_in, grad_qkv, grad_out)
    grad_in, grad_qkv, grad_out = pl.pallas_call(
        settle,
        out_shape=tuple(jax.ShapeDtypeStruct(r.shape, r.dtype) for r in results),
        in_specs=[in_vmem] * 3,
        out_specs=(anywhere,) * 3,
        scratch_shapes=[dma(3)],
    )(*results)
    return grad_in[None, None], grad_qkv[None], grad_out[None]


def solution(mesh):
    placed = (
        P("section", None, "ctx", "tp"),
        P(None, "ctx", "tp"),
        P(None, "ctx"),
        P(),
        P("section", None),
        P("section", None, "tp"),
        P("section", None, "tp"),
    )
    return jax.shard_map(
        body,
        mesh=mesh,
        in_specs=placed,
        out_specs=(
            P("section", None, "ctx", "tp"),
            P("section", "ctx", "tp"),
            P("section", "ctx", "tp"),
        ),
        check_vma=False,
    )
```

```python
import functools

import jax
import jax.numpy as jnp
from jax import lax
from jax.experimental import pallas as pl
from jax.experimental.pallas import tpu as pltpu
from jax.sharding import PartitionSpec as P

MESH = pl.DeviceIdType.MESH
GROUP_HEADS = 4
HEAD_SIZE = 128
BLOCK = 128
MAX_DOC = 10
EPSILON = 1e-05
NEG_FILL = -1e30
F32 = jnp.float32
BF16 = jnp.bfloat16

NN = (((1,), (0,)), ((), ()))
NT = (((1,), (1,)), ((), ()))
TN = (((0,), (0,)), ((), ()))


def mm(a, b, dims=NN):
    return lax.dot_general(a, b, dims, preferred_element_type=F32)


def kernel(
    n_ctx, n_tp, window,
    x_ref, loss_ref, tw_ref, docs_ref, gain_ref, wq_hbm, wo_hbm,
    gin_ref, gqkv_ref, gout_ref,
    wq, wo, xfull, cotfull, cot_loc, inv_b,
    kv, q_s, hc_s, att_s, gq_n, gkv_n, scores, probs, dscores, peak, denom, acc, kv_acc, hc_acc, sq_out, sq_in,
    dkv_part, dkv_in, feat_f, feat_out, feat_in, rs_out, rs_in,
    hid_p, cot_p, hid_z, cot_z, att_z, gq_z, gkv_z, turned,
    y_out_o, y_out_q, y_out_k, y_in_o, y_in_q, y_in_k,
    w_sem, x_s, x_r, c_s, c_r, kv_s, kv_r, kv_f, d_s, d_r, f_s, f_r, r_s, r_r,
    h1_s, h1_r, h2_s, h2_r, c1_s, c1_r, c2_s, c2_r, az_s, az_r, qz_s, qz_r, kz_s, kz_r, y_s, y_r, sec_s, q_sem, q_rcv, gate,
):
    s = lax.axis_index("section")
    c = lax.axis_index("ctx")
    t = lax.axis_index("tp")
    n_z = n_ctx // 2
    z, lo = c // 2, lax.rem(c, 2)
    part = x_ref.shape[1]
    width = part * n_tp
    half = part // 2
    heads = GROUP_HEADS * HEAD_SIZE
    cols = heads + 2 * HEAD_SIZE
    scale = HEAD_SIZE ** (-0.5)
    last = window - 1

    def remote(src, dst, ss, rs, dev):
        return pltpu.make_async_remote_copy(
            src_ref=src, dst_ref=dst, send_sem=ss, recv_sem=rs, device_id=dev, device_id_type=MESH
        )

    def tp_dev(p):
        return {"tp": p}

    def z_dev(p):
        return {"ctx": p * 2 + lo}

    def exchange(n, me, dev, src_of, slot, ss, rs):
        def copy_to(p):
            return remote(src_of(p), slot(me), ss.at[p], rs.at[me], dev(p))

        def copy_from(p):
            return remote(slot(p), slot(p), ss.at[p], rs.at[p], dev(p))

        def start():
            @pl.loop(1, n)
            def _(i):
                copy_to(lax.rem(me + i, n)).start()

        def wait_recv():
            @pl.loop(1, n)
            def _(i):
                copy_from(lax.rem(me + i, n)).wait_recv()

        def wait_send():
            @pl.loop(1, n)
            def _(i):
                copy_to(lax.rem(me + i, n)).wait_send()

        return start, wait_recv, wait_send, copy_to, copy_from

    def ring(ref, ss, rs):
        up, down = z_dev(lax.rem(z + 1, n_z)), z_dev(lax.rem(z + n_z - 1, n_z))
        top = n_z // 2

        def piece(p, k, side):
            if k < top:
                return ref.at[pl.ds(p * BLOCK, BLOCK)]
            return ref.at[pl.ds(p * BLOCK + side * (BLOCK // 2), BLOCK // 2)]

        def pair(k, shift):
            below = piece(lax.rem(z - k + shift + n_z, n_z), k, 0)
            above = piece(lax.rem(z + k - shift, n_z), k, 1)
            return (
                remote(below, below, ss.at[k - 1], rs.at[k - 1], up),
                remote(above, above, ss.at[top + k - 1], rs.at[top + k - 1], down),
            )

        def arrive(k):
            for copy in pair(k, 0):
                copy.wait_recv()

        def stage(k):
            if k > top:
                return
            if k > 1:
                arrive(k - 1)
            for copy in pair(k, 1):
                copy.start()

        def wait_send():
            for k in range(1, top + 1):
                for copy in pair(k, 1):
                    copy.wait_send()

        return stage, lambda: arrive(top), wait_send

    whole = lambda ref: lambda p: ref
    share = BLOCK // n_tp
    my_rows = pl.ds(pl.multiple_of(t * share, share), share)

    x_ex = exchange(n_tp, t, tp_dev, whole(x_ref), lambda p: xfull.at[p], x_s, x_r)
    c_ex = exchange(n_tp, t, tp_dev, whole(cot_loc), lambda p: cotfull.at[p], c_s, c_r)
    f_ex = exchange(n_tp, t, tp_dev, lambda p: feat_out.at[p], lambda p: feat_in.at[p], f_s, f_r)
    q_ex = exchange(n_tp, t, tp_dev, whole(sq_out), lambda p: sq_in.at[p], q_sem, q_rcv)
    r_ex = exchange(n_tp, t, tp_dev, whole(rs_out), lambda p: rs_in.at[p], r_s, r_r)
    h1_ex = exchange(n_z, z, z_dev, lambda p: xfull.at[p, my_rows], lambda p: hid_p.at[p], h1_s, h1_r)
    h2_ex = exchange(n_tp, t, tp_dev, whole(hid_p), lambda p: hid_z.at[:, p], h2_s, h2_r)
    c1_ex = exchange(n_z, z, z_dev, lambda p: cotfull.at[p, my_rows], lambda p: cot_p.at[p], c1_s, c1_r)
    c2_ex = exchange(n_tp, t, tp_dev, whole(cot_p), lambda p: cot_z.at[:, p], c2_s, c2_r)
    att_ring = ring(att_z, az_s, az_r)
    gq_ring = ring(gq_z, qz_s, qz_r)
    kz_ex = exchange(n_z, z, z_dev, whole(gkv_n), lambda p: gkv_z.at[pl.ds(p * BLOCK, BLOCK)], kz_s, kz_r)
    own_z = pl.ds(pl.multiple_of(z * BLOCK, BLOCK), BLOCK)
    wq_copy = pltpu.make_async_copy(wq_hbm, wq, w_sem.at[0])
    wo_copy = pltpu.make_async_copy(wo_hbm, wo, w_sem.at[1])

    wq_copy.start()
    wo_copy.start()
    kv[...] = jnp.zeros_like(kv)
    own_x = x_ref[...].astype(F32)
    square_sum = jnp.sum(own_x * own_x, axis=1, keepdims=True)
    sq_out[...] = jnp.broadcast_to(square_sum, (BLOCK, BLOCK)).T[:8]

    barrier = pltpu.get_barrier_semaphore()

    @pl.loop(1, n_tp)
    def _(i):
        pl.semaphore_signal(barrier, inc=1, device_id={"tp": lax.rem(t + i, n_tp)}, device_id_type=MESH)

    @pl.loop(1, n_ctx)
    def _(i):
        pl.semaphore_signal(barrier, inc=1, device_id={"ctx": lax.rem(c + i, n_ctx)}, device_id_type=MESH)

    @pl.loop(0, n_tp)
    def _(p):
        pl.semaphore_signal(barrier, inc=1, device_id={"section": 1 - s, "tp": p}, device_id_type=MESH)

    pl.semaphore_wait(barrier, 2 * n_tp + n_ctx - 2)

    @pl.when(s == 0)
    def _():
        pl.semaphore_wait(gate, 1)

    q_ex[0]()
    x_ex[0]()
    sq_in[t] = sq_out[...]
    xfull[t] = x_ref[...]

    def total_of(ref):
        total = ref[0]
        for p in range(1, n_tp):
            total = total + ref[p]
        return jnp.broadcast_to(total[:1], (BLOCK, BLOCK)).T

    q_ex[1]()
    inv_b[...] = lax.rsqrt(total_of(sq_in) / width + EPSILON)
    kv_acc[...] = jnp.zeros_like(kv_acc)
    wq_copy.wait()

    @pl.loop(0, n_tp)
    def _(i):
        p = lax.rem(t - i + n_tp, n_tp)

        @pl.when(i > 0)
        def _():
            x_ex[4](p).wait_recv()

        gain = gain_ref[:, pl.ds(pl.multiple_of(p * part, part), part)]
        hidden = ((xfull[p].astype(F32) * inv_b[:, :1]) * gain).astype(BF16)
        xfull[p] = hidden
        kv_acc[...] += mm(hidden, wq[pl.ds(pl.multiple_of(p * part, part), part), heads:])

    @pl.when(s == 1)
    def _():
        weights = jnp.broadcast_to(tw_ref[...].astype(F32), (BLOCK, BLOCK)).T[:, :1]
        cot_loc[...] = (loss_ref[...].astype(F32) * weights).astype(BF16)
        cotfull[t] = cot_loc[...]
        c_ex[0]()

    def project(full, weight, lo_col, n_col):
        total = jnp.zeros((BLOCK, n_col), F32)
        for p in range(n_tp):
            total = total + mm(full[p], weight[p * part : (p + 1) * part, lo_col : lo_col + n_col])
        return total.astype(BF16)

    def slot(j):
        if isinstance(j, int):
            return pl.ds(j * BLOCK, BLOCK)
        return pl.ds(pl.multiple_of(j * BLOCK, BLOCK), BLOCK)

    kv[slot(last)] = kv_acc[...].astype(BF16)

    steps_z = (window - 1) // 2 + 1
    mate = {"ctx": z * 2 + 1 - lo}
    far = window - 1

    def kv_up(k):
        return remote(
            kv.at[slot(last)], kv.at[slot(last - 2 * k)], kv_s.at[2 * k], kv_r.at[2 * k],
            {"ctx": lax.rem(c + 2 * k, n_ctx)},
        )

    def kv_on(k):
        away = 2 * k + 1 - 2 * lo
        return remote(
            kv.at[slot(last - 2 * k)], kv.at[slot(last - away)], kv_s.at[2 * k + 1], kv_r.at[away], mate
        )

    def kv_far():
        return remote(
            kv.at[slot(last)], kv.at[slot(last - far)], kv_f.at[0], kv_r.at[far],
            {"ctx": lax.rem(c + far, n_ctx)},
        )

    def kv_arrival(d):
        return remote(
            kv.at[slot(last - d)], kv.at[slot(last - d)], kv_s.at[0], kv_r.at[d], mate
        )

    @pl.loop(1, steps_z)
    def _(i):
        k = steps_z - i

        @pl.when(z + k < n_z)
        def _():
            kv_up(k).start()

    @pl.when((lo == 1) & (c + far < n_ctx))
    def _():
        kv_far().start()

    @pl.when(lo == 0)
    def _():
        kv_on(0).start()

    for j in range(0, GROUP_HEADS, 2):
        pair = project(xfull, wq, j * HEAD_SIZE, 2 * HEAD_SIZE)
        q_s[j * BLOCK : (j + 1) * BLOCK] = pair[:, :HEAD_SIZE]
        q_s[(j + 1) * BLOCK : (j + 2) * BLOCK] = pair[:, HEAD_SIZE:]
    h1_ex[0]()
    hid_p[z] = xfull[z, my_rows]

    def pass_hidden():
        h1_ex[1]()
        h2_ex[0]()
        hid_z[:, t] = hid_p[...]

    def head_cotangent(arrival):
        wo_copy.wait()
        hc_acc[...] = jnp.zeros_like(hc_acc)

        @pl.loop(0, n_tp)
        def _(i):
            p = lax.rem(t - i + n_tp, n_tp)
            arrival(i, p)
            hc_acc[...] += mm(cotfull[p], wo[pl.ds(pl.multiple_of(p * part, part), part)])

        for j in range(GROUP_HEADS):
            hc_s[j * BLOCK : (j + 1) * BLOCK] = hc_acc[:, j * HEAD_SIZE : (j + 1) * HEAD_SIZE].astype(BF16)

    @pl.loop(1, steps_z)
    def _(k):
        @pl.when(z - k >= 0)
        def _():
            kv_up(k).wait_recv()
            kv_on(k).start()

    @pl.when(s == 0)
    def _():
        pass_hidden()

    @pl.when(s == 1)
    def _():
        c_ex[1]()
        pl.semaphore_signal(gate, inc=1, device_id={"section": 1 - s}, device_id_type=MESH)
        head_cotangent(lambda i, p: None)

    doc_start = jnp.int32(0)
    doc_end = jnp.int32(0)
    for i in range(docs_ref.shape[1]):
        doc_end = doc_end + docs_ref[0, i]
        doc_start = jnp.where(doc_end <= c, doc_end, doc_start)
    pairs = window // 2
    wide = (GROUP_HEADS * BLOCK, 2 * BLOCK)
    query_pos = c * BLOCK + lax.broadcasted_iota(jnp.int32, wide, 0) % BLOCK
    first_key = (c - last) * BLOCK + lax.broadcasted_iota(jnp.int32, wide, 1)

    def keys(g):
        return kv[g * 2 * BLOCK : (g + 1) * 2 * BLOCK, :HEAD_SIZE]

    def values(g):
        return kv[g * 2 * BLOCK : (g + 1) * 2 * BLOCK, HEAD_SIZE:]

    for g in range(pairs - 1, -1, -1):
        for j in (2 * g + 1, 2 * g):
            if j < last:

                if (last - j) % 2 == 1:

                    @pl.when(c - last + j >= 0)
                    def _():
                        kv_arrival(last - j).wait_recv()

        block = mm(q_s[...], keys(g), NT) * scale
        key_pos = first_key + g * 2 * BLOCK
        block = jnp.where((key_pos <= query_pos) & (key_pos >= doc_start * BLOCK), block, NEG_FILL)
        scores[g] = block
        both = jnp.maximum(block[:, :BLOCK], block[:, BLOCK:])
        peak[...] = both if g == pairs - 1 else jnp.maximum(peak[...], both)

    top = jnp.max(peak[...], axis=1, keepdims=True)
    for g in range(pairs):
        e = jnp.exp(scores[g] - top)
        scores[g] = e
        both = e[:, :BLOCK] + e[:, BLOCK:]
        denom[...] = both if g == 0 else denom[...] + both

    inverse = 1.0 / jnp.sum(denom[...], axis=1, keepdims=True)
    for g in range(pairs):
        soft = scores[g] * inverse
        low = soft.astype(BF16)
        scores[g] = soft
        probs[g] = low
        term = mm(low, values(g))
        acc[...] = term if g == 0 else acc[...] + term

    att_s[...] = acc[...].astype(BF16)
    for j in range(GROUP_HEADS):
        att_z[own_z, j * HEAD_SIZE : (j + 1) * HEAD_SIZE] = att_s[j * BLOCK : (j + 1) * BLOCK]

    def sec_copy(p):
        return remote(gin_ref, cotfull.at[t], sec_s.at[p], c_r.at[t], {"section": 1 - s, "tp": p})

    @pl.when(s == 1)
    def _():
        pass_hidden()

    @pl.when(s == 0)
    def _():
        for k in range(1, n_z // 2 + 1):
            att_ring[0](k)

        def arrival(i, p):
            remote(cotfull.at[p], cotfull.at[p], sec_s.at[p], c_r.at[p], {"section": 1 - s}).wait_recv()

        head_cotangent(arrival)

    delta = jnp.sum(hc_s[...].astype(F32) * att_s[...].astype(F32), axis=1, keepdims=True)

    def dkv_copy(d):
        return remote(
            dkv_part.at[slot(last - d)], dkv_in.at[d], d_s.at[d], d_r.at[d],
            {"ctx": lax.rem(c - d + n_ctx, n_ctx)},
        )

    for g in range(pairs):
        block = slice(g * 2 * BLOCK, (g + 1) * 2 * BLOCK)
        dprobs = mm(hc_s[...], values(g), NT)
        ds = (scores[g] * (dprobs - delta)).astype(BF16)
        dkv_part[block, :HEAD_SIZE] = (mm(ds, q_s[...], TN) * scale).astype(BF16)
        dkv_part[block, HEAD_SIZE:] = mm(probs[g], hc_s[...], TN).astype(BF16)
        dscores[g] = ds
        for j in (2 * g, 2 * g + 1):
            if j < last:

                @pl.when(c - last + j >= 0)
                def _():
                    dkv_copy(last - j).start()

    total = mm(dscores[0], keys(0))
    for g in range(1, pairs):
        total = total + mm(dscores[g], keys(g))
    acc[...] = total
    for j in range(GROUP_HEADS):
        gq_n[:, j * HEAD_SIZE : (j + 1) * HEAD_SIZE] = (
            acc[j * BLOCK : (j + 1) * BLOCK] * scale
        ).astype(BF16)
    gq_z[own_z] = gq_n[...]

    def send_cot():
        c1_ex[0]()
        cot_p[z] = cotfull[z, my_rows]

    def pass_cot():
        c1_ex[1]()
        c2_ex[0]()
        cot_z[:, t] = cot_p[...]

    @pl.when(s == 0)
    def _():
        send_cot()
        gq_ring[0](1)

    @pl.loop(0, n_tp)
    def _(p):
        feat_f[p] = mm(gq_n[...], wq[pl.ds(p * part, part), :heads], NT)

    @pl.when(s == 0)
    def _():
        pass_cot()
        gq_ring[0](2)

    acc[:BLOCK] = dkv_part[slot(last), :HEAD_SIZE].astype(F32)
    acc[BLOCK : 2 * BLOCK] = dkv_part[slot(last), HEAD_SIZE:].astype(F32)

    @pl.loop(1, window)
    def _(d):
        @pl.when(c + d < n_ctx)
        def _():
            dkv_copy(d).wait_recv()
            acc[:BLOCK] += dkv_in[d, :, :HEAD_SIZE].astype(F32)
            acc[BLOCK : 2 * BLOCK] += dkv_in[d, :, HEAD_SIZE:].astype(F32)

    gkv_n[:, :HEAD_SIZE] = acc[:BLOCK].astype(BF16)
    gkv_n[:, HEAD_SIZE:] = acc[BLOCK : 2 * BLOCK].astype(BF16)
    gkv_z[own_z] = gkv_n[...]
    kz_ex[0]()

    row_sum = gkv_n[:, :HEAD_SIZE].astype(F32) * kv[slot(last), :HEAD_SIZE].astype(F32)
    row_sum = row_sum + gkv_n[:, HEAD_SIZE:].astype(F32) * kv[slot(last), HEAD_SIZE:].astype(F32)
    for j in range(GROUP_HEADS):
        row_sum = row_sum + gq_n[:, j * HEAD_SIZE : (j + 1) * HEAD_SIZE].astype(F32) * q_s[
            j * BLOCK : (j + 1) * BLOCK
        ].astype(F32)
    row_sum = jnp.sum(row_sum, axis=1, keepdims=True)
    rs_out[...] = jnp.broadcast_to(row_sum, (BLOCK, BLOCK)).T[:8]
    r_ex[0]()
    rs_in[t] = rs_out[...]

    @pl.loop(1, n_tp + 1)
    def _(i):
        p = lax.rem(t + i, n_tp)
        total = feat_f[p] + mm(gkv_n[...], wq[pl.ds(p * part, part), heads:], NT)
        feat_out[p] = total.astype(BF16)

        @pl.when(i < n_tp)
        def _():
            f_ex[3](p).start()

    feat_in[t] = feat_out[t]

    y_copies = [
        remote(y_out_o, y_in_o, y_s.at[0], y_r.at[0], mate),
        remote(y_out_q, y_in_q, y_s.at[1], y_r.at[1], mate),
        remote(y_out_k, y_in_k, y_s.at[2], y_r.at[2], mate),
    ]
    positions = n_z * BLOCK
    theirs = pl.ds(pl.multiple_of((1 - lo) * half, half), half)
    mine = pl.ds(pl.multiple_of(lo * half, half), half)

    def turn(ref):
        turned[...] = ref[...].reshape(positions, part).T

    def weight_part(right, y_out, out, base, copy):
        step = min(256, heads)
        for k in range(0, right.shape[1], step):
            y_out[:, k : k + step] = mm(turned[theirs], right[:, k : k + step]).astype(BF16)
        copy.start()
        for k in range(0, right.shape[1], step):
            out[:, base + k : base + k + step] = mm(turned[mine], right[:, k : k + step])

    def grad_of_out():
        c2_ex[1]()
        att_ring[1]()
        turn(cot_z)
        weight_part(att_z, y_out_o, gout_ref, 0, y_copies[0])

    def grad_of_query():
        h2_ex[1]()
        turn(hid_z)
        gq_ring[1]()
        weight_part(gq_z, y_out_q, gqkv_ref, 0, y_copies[1])

    @pl.when(s == 0)
    def _():
        gq_ring[0](3)
        grad_of_out()
        gq_ring[0](4)
        grad_of_query()

    f_ex[1]()
    r_ex[1]()
    feature = jnp.zeros((BLOCK, part), F32)
    for p in range(n_tp):
        feature = feature + feat_in[p].astype(F32)
    inv = inv_b[:, :1]
    gain = gain_ref[:, pl.ds(pl.multiple_of(t * part, part), part)]
    scaled = feature * gain
    normed = x_ref[...].astype(F32) * inv
    mean = total_of(rs_in)[:, :1] / width
    gin_ref[...] = (cotfull[t].astype(F32) + inv * (scaled - normed * mean)).astype(BF16)

    @pl.when(s == 1)
    def _():
        @pl.loop(0, n_tp)
        def _(i):
            sec_copy(lax.rem(t + i, n_tp)).start()

        send_cot()
        for k in range(1, n_z // 2 + 1):
            att_ring[0](k)
            gq_ring[0](k)
            if k == 2 or n_z == 2:
                pass_cot()
        grad_of_out()
        grad_of_query()

    kz_ex[1]()
    weight_part(gkv_z, y_out_k, gqkv_ref, heads, y_copies[2])
    for y_in, out, base, copy in (
        (y_in_o, gout_ref, 0, y_copies[0]),
        (y_in_q, gqkv_ref, 0, y_copies[1]),
        (y_in_k, gqkv_ref, heads, y_copies[2]),
    ):
        copy.wait_recv()
        out[:, base : base + y_in.shape[1]] += y_in[...].astype(F32)

    for ex in (x_ex, q_ex, f_ex, r_ex, h1_ex, h2_ex, c1_ex, c2_ex, kz_ex, att_ring, gq_ring):
        ex[2]()
    for copy in y_copies:
        copy.wait_send()

    @pl.loop(1, steps_z)
    def _(k):
        @pl.when(z + k < n_z)
        def _():
            kv_up(k).wait_send()

        @pl.when(z - k >= 0)
        def _():
            kv_on(k).wait_send()

    @pl.when((lo == 1) & (c + far < n_ctx))
    def _():
        kv_far().wait_send()

    @pl.when(lo == 0)
    def _():
        kv_on(0).wait_send()

    @pl.loop(1, window)
    def _(d):
        @pl.when(c - d >= 0)
        def _():
            dkv_copy(d).wait_send()

    @pl.when(s == 1)
    def _():
        c_ex[2]()

        @pl.loop(0, n_tp)
        def _(p):
            sec_copy(p).wait_send()


def settle(a_in, b_in, c_in, a_out, b_out, c_out, sem):
    copies = [
        pltpu.make_async_copy(source, target, sem.at[i])
        for i, (source, target) in enumerate(((a_in, a_out), (b_in, b_out), (c_in, c_out)))
    ]
    for copy in copies:
        copy.start()
    for copy in copies:
        copy.wait()


def body(layer_input, loss_cot, token_weights, doc_blocks, norm_gain, qkv_weight, out_weight):
    n_ctx, n_tp = lax.axis_size("ctx"), lax.axis_size("tp")
    n_z = n_ctx // 2
    part = layer_input.shape[3]
    width = part * n_tp
    cols, heads = qkv_weight.shape[2], out_weight.shape[2]
    window = min(MAX_DOC, n_ctx)
    q_rows = GROUP_HEADS * BLOCK
    kv_cols = 2 * HEAD_SIZE
    half = part // 2
    share = BLOCK // n_tp
    vmem = lambda shape, dtype=BF16: pltpu.VMEM(shape, dtype)
    dma = lambda *n: pltpu.SemaphoreType.DMA(n)
    scratch = [
        vmem((width, cols)), vmem((width, heads)),
        vmem((n_tp, BLOCK, part)), vmem((n_tp, BLOCK, part)), vmem((BLOCK, part)), vmem((BLOCK, BLOCK), F32),
        vmem((window * BLOCK, kv_cols)),
        vmem((q_rows, HEAD_SIZE)), vmem((q_rows, HEAD_SIZE)), vmem((q_rows, HEAD_SIZE)),
        vmem((BLOCK, heads)), vmem((BLOCK, kv_cols)),
        vmem((window // 2, q_rows, 2 * BLOCK), F32), vmem((window // 2, q_rows, 2 * BLOCK)),
        vmem((window // 2, q_rows, 2 * BLOCK)),
        vmem((q_rows, BLOCK), F32), vmem((q_rows, BLOCK), F32), vmem((q_rows, HEAD_SIZE), F32),
        vmem((BLOCK, kv_cols), F32), vmem((BLOCK, heads), F32), vmem((8, BLOCK), F32), vmem((n_tp, 8, BLOCK), F32),
        vmem((window * BLOCK, kv_cols)), vmem((window, BLOCK, kv_cols)),
        vmem((n_tp, BLOCK, part), F32), vmem((n_tp, BLOCK, part)), vmem((n_tp, BLOCK, part)),
        vmem((8, BLOCK), F32), vmem((n_tp, 8, BLOCK), F32),
        vmem((n_z, share, part)), vmem((n_z, share, part)),
        vmem((n_z, n_tp, share, part)), vmem((n_z, n_tp, share, part)), vmem((n_z * BLOCK, heads)),
        vmem((n_z * BLOCK, heads)), vmem((n_z * BLOCK, kv_cols)), vmem((part, n_z * BLOCK)),
        vmem((half, heads)), vmem((half, heads)), vmem((half, kv_cols)),
        vmem((half, heads)), vmem((half, heads)), vmem((half, kv_cols)),
        dma(2), dma(n_tp), dma(n_tp), dma(n_tp), dma(n_tp), dma(window), dma(window), dma(1), dma(window), dma(window),
        dma(n_tp), dma(n_tp), dma(n_tp), dma(n_tp),
        dma(n_z), dma(n_z), dma(n_tp), dma(n_tp), dma(n_z), dma(n_z), dma(n_tp), dma(n_tp),
        dma(n_z), dma(n_z), dma(n_z), dma(n_z), dma(n_z), dma(n_z),
        dma(3), dma(3), dma(n_tp), dma(n_tp), dma(n_tp), pltpu.SemaphoreType.REGULAR,
    ]
    in_vmem = pl.BlockSpec(memory_space=pltpu.VMEM)
    anywhere = pl.BlockSpec(memory_space=pl.ANY)
    grad_in, grad_qkv, grad_out = pl.pallas_call(
        functools.partial(kernel, n_ctx, n_tp, window),
        out_shape=(
            jax.ShapeDtypeStruct((BLOCK, part), BF16),
            jax.ShapeDtypeStruct((half, cols), F32),
            jax.ShapeDtypeStruct((half, heads), F32),
        ),
        in_specs=[
            in_vmem, in_vmem, in_vmem, pl.BlockSpec(memory_space=pltpu.SMEM), in_vmem, anywhere, anywhere,
        ],
        out_specs=(in_vmem, in_vmem, in_vmem),
        scratch_shapes=scratch,
        compiler_params=pltpu.CompilerParams(
            collective_id=0, has_side_effects=True, vmem_limit_bytes=56 * 1024 * 1024
        ),
    )(
        layer_input[0, 0], loss_cot[0], token_weights, doc_blocks, norm_gain, qkv_weight[0], out_weight[0]
    )
    results = (grad_in, grad_qkv, grad_out)
    grad_in, grad_qkv, grad_out = pl.pallas_call(
        settle,
        out_shape=tuple(jax.ShapeDtypeStruct(r.shape, r.dtype) for r in results),
        in_specs=[in_vmem] * 3,
        out_specs=(anywhere,) * 3,
        scratch_shapes=[dma(3)],
    )(*results)
    return grad_in[None, None], grad_qkv[None], grad_out[None]


def solution(mesh):
    placed = (
        P("section", None, "ctx", "tp"),
        P(None, "ctx", "tp"),
        P(None, "ctx"),
        P(),
        P("section", None),
        P("section", None, "tp"),
        P("section", None, "tp"),
    )
    return jax.shard_map(
        body,
        mesh=mesh,
        in_specs=placed,
        out_specs=(
            P("section", None, "ctx", "tp"),
            P("section", "ctx", "tp"),
            P("section", "ctx", "tp"),
        ),
        check_vma=False,
    )
```

```python
import functools

import jax
import jax.numpy as jnp
from jax import lax
from jax.experimental import pallas as pl
from jax.experimental.pallas import tpu as pltpu
from jax.sharding import PartitionSpec as P

MESH = pl.DeviceIdType.MESH
GROUP_HEADS = 4
HEAD_SIZE = 128
BLOCK = 128
MAX_DOC = 10
EPSILON = 1e-05
NEG_FILL = -1e30
F32 = jnp.float32
BF16 = jnp.bfloat16

NN = (((1,), (0,)), ((), ()))
NT = (((1,), (1,)), ((), ()))
TN = (((0,), (0,)), ((), ()))


def mm(a, b, dims=NN):
    return lax.dot_general(a, b, dims, preferred_element_type=F32)


def kernel(
    n_ctx, n_tp, window,
    x_ref, loss_ref, tw_ref, docs_ref, gain_ref, wq_hbm, wo_hbm,
    gin_ref, gqkv_ref, gout_ref,
    wq, wo, xfull, cotfull, cot_loc, inv_b,
    kv, q_s, hc_s, att_s, gq_n, gkv_n, scores, probs, dscores, peak, denom, acc, kv_acc, hc_acc, sq_out, sq_in,
    dkv_part, dkv_in, feat_f, feat_out, feat_in, rs_out, rs_in,
    hid_p, cot_p, hid_z, cot_z, att_z, gq_z, gkv_z, turned,
    y_out_o, y_out_q, y_out_k, y_in_o, y_in_q, y_in_k,
    w_sem, x_s, x_r, c_s, c_r, kv_s, kv_r, kv_f, d_s, d_r, f_s, f_r, r_s, r_r,
    h1_s, h1_r, h2_s, h2_r, c1_s, c1_r, c2_s, c2_r, az_s, az_r, qz_s, qz_r, kz_s, kz_r, y_s, y_r, sec_s, q_sem, q_rcv, gate,
):
    s = lax.axis_index("section")
    c = lax.axis_index("ctx")
    t = lax.axis_index("tp")
    n_z = n_ctx // 2
    z, lo = c // 2, lax.rem(c, 2)
    part = x_ref.shape[1]
    width = part * n_tp
    half = part // 2
    heads = GROUP_HEADS * HEAD_SIZE
    cols = heads + 2 * HEAD_SIZE
    scale = HEAD_SIZE ** (-0.5)
    last = window - 1

    def remote(src, dst, ss, rs, dev):
        return pltpu.make_async_remote_copy(
            src_ref=src, dst_ref=dst, send_sem=ss, recv_sem=rs, device_id=dev, device_id_type=MESH
        )

    def tp_dev(p):
        return {"tp": p}

    def z_dev(p):
        return {"ctx": p * 2 + lo}

    def exchange(n, me, dev, src_of, slot, ss, rs):
        def copy_to(p):
            return remote(src_of(p), slot(me), ss.at[p], rs.at[me], dev(p))

        def copy_from(p):
            return remote(slot(p), slot(p), ss.at[p], rs.at[p], dev(p))

        def start():
            @pl.loop(1, n)
            def _(i):
                copy_to(lax.rem(me + i, n)).start()

        def wait_recv():
            @pl.loop(1, n)
            def _(i):
                copy_from(lax.rem(me + i, n)).wait_recv()

        def wait_send():
            @pl.loop(1, n)
            def _(i):
                copy_to(lax.rem(me + i, n)).wait_send()

        return start, wait_recv, wait_send, copy_to, copy_from

    def ring(ref, ss, rs):
        up, down = z_dev(lax.rem(z + 1, n_z)), z_dev(lax.rem(z + n_z - 1, n_z))
        top = n_z // 2

        def piece(p, k, side):
            if k < top:
                return ref.at[pl.ds(p * BLOCK, BLOCK)]
            return ref.at[pl.ds(p * BLOCK + side * (BLOCK // 2), BLOCK // 2)]

        def pair(k, shift):
            below = piece(lax.rem(z - k + shift + n_z, n_z), k, 0)
            above = piece(lax.rem(z + k - shift, n_z), k, 1)
            return (
                remote(below, below, ss.at[k - 1], rs.at[k - 1], up),
                remote(above, above, ss.at[top + k - 1], rs.at[top + k - 1], down),
            )

        def arrive(k):
            for copy in pair(k, 0):
                copy.wait_recv()

        def stage(k):
            if k > top:
                return
            if k > 1:
                arrive(k - 1)
            for copy in pair(k, 1):
                copy.start()

        def wait_send():
            for k in range(1, top + 1):
                for copy in pair(k, 1):
                    copy.wait_send()

        return stage, lambda: arrive(top), wait_send

    whole = lambda ref: lambda p: ref
    share = BLOCK // n_tp
    my_rows = pl.ds(pl.multiple_of(t * share, share), share)

    x_ex = exchange(n_tp, t, tp_dev, whole(x_ref), lambda p: xfull.at[p], x_s, x_r)
    c_ex = exchange(n_tp, t, tp_dev, whole(cot_loc), lambda p: cotfull.at[p], c_s, c_r)
    f_ex = exchange(n_tp, t, tp_dev, lambda p: feat_out.at[p], lambda p: feat_in.at[p], f_s, f_r)
    q_ex = exchange(n_tp, t, tp_dev, whole(sq_out), lambda p: sq_in.at[p], q_sem, q_rcv)
    r_ex = exchange(n_tp, t, tp_dev, whole(rs_out), lambda p: rs_in.at[p], r_s, r_r)
    h1_ex = exchange(n_z, z, z_dev, lambda p: xfull.at[p, my_rows], lambda p: hid_p.at[p], h1_s, h1_r)
    h2_ex = exchange(n_tp, t, tp_dev, whole(hid_p), lambda p: hid_z.at[:, p], h2_s, h2_r)
    c1_ex = exchange(n_z, z, z_dev, lambda p: cotfull.at[p, my_rows], lambda p: cot_p.at[p], c1_s, c1_r)
    c2_ex = exchange(n_tp, t, tp_dev, whole(cot_p), lambda p: cot_z.at[:, p], c2_s, c2_r)
    att_ring = ring(att_z, az_s, az_r)
    gq_ring = ring(gq_z, qz_s, qz_r)
    kz_ex = exchange(n_z, z, z_dev, whole(gkv_n), lambda p: gkv_z.at[pl.ds(p * BLOCK, BLOCK)], kz_s, kz_r)
    own_z = pl.ds(pl.multiple_of(z * BLOCK, BLOCK), BLOCK)
    wq_copy = pltpu.make_async_copy(wq_hbm, wq, w_sem.at[0])
    wo_copy = pltpu.make_async_copy(wo_hbm, wo, w_sem.at[1])

    wq_copy.start()
    wo_copy.start()
    kv[...] = jnp.zeros_like(kv)
    own_x = x_ref[...].astype(F32)
    square_sum = jnp.sum(own_x * own_x, axis=1, keepdims=True)
    sq_out[...] = jnp.broadcast_to(square_sum, (BLOCK, BLOCK)).T[:8]

    barrier = pltpu.get_barrier_semaphore()

    @pl.loop(1, n_tp)
    def _(i):
        pl.semaphore_signal(barrier, inc=1, device_id={"tp": lax.rem(t + i, n_tp)}, device_id_type=MESH)

    @pl.loop(1, n_ctx)
    def _(i):
        pl.semaphore_signal(barrier, inc=1, device_id={"ctx": lax.rem(c + i, n_ctx)}, device_id_type=MESH)

    @pl.loop(0, n_tp)
    def _(p):
        pl.semaphore_signal(barrier, inc=1, device_id={"section": 1 - s, "tp": p}, device_id_type=MESH)

    pl.semaphore_wait(barrier, 2 * n_tp + n_ctx - 2)

    @pl.when(s == 0)
    def _():
        pl.semaphore_wait(gate, 1)

    q_ex[0]()
    x_ex[0]()
    sq_in[t] = sq_out[...]
    xfull[t] = x_ref[...]

    def total_of(ref):
        total = ref[0]
        for p in range(1, n_tp):
            total = total + ref[p]
        return jnp.broadcast_to(total[:1], (BLOCK, BLOCK)).T

    q_ex[1]()
    inv_b[...] = lax.rsqrt(total_of(sq_in) / width + EPSILON)
    kv_acc[...] = jnp.zeros_like(kv_acc)
    wq_copy.wait()

    @pl.loop(0, n_tp)
    def _(i):
        p = lax.rem(t - i + n_tp, n_tp)

        @pl.when(i > 0)
        def _():
            x_ex[4](p).wait_recv()

        gain = gain_ref[:, pl.ds(pl.multiple_of(p * part, part), part)]
        hidden = ((xfull[p].astype(F32) * inv_b[:, :1]) * gain).astype(BF16)
        xfull[p] = hidden
        kv_acc[...] += mm(hidden, wq[pl.ds(pl.multiple_of(p * part, part), part), heads:])

    @pl.when(s == 1)
    def _():
        weights = jnp.broadcast_to(tw_ref[...].astype(F32), (BLOCK, BLOCK)).T[:, :1]
        cot_loc[...] = (loss_ref[...].astype(F32) * weights).astype(BF16)
        cotfull[t] = cot_loc[...]
        c_ex[0]()
        pl.semaphore_signal(gate, inc=1, device_id={"section": 1 - s}, device_id_type=MESH)

    def project(full, weight, lo_col, n_col):
        total = jnp.zeros((BLOCK, n_col), F32)
        for p in range(n_tp):
            total = total + mm(full[p], weight[p * part : (p + 1) * part, lo_col : lo_col + n_col])
        return total.astype(BF16)

    def slot(j):
        if isinstance(j, int):
            return pl.ds(j * BLOCK, BLOCK)
        return pl.ds(pl.multiple_of(j * BLOCK, BLOCK), BLOCK)

    kv[slot(last)] = kv_acc[...].astype(BF16)

    steps_z = (window - 1) // 2 + 1
    mate = {"ctx": z * 2 + 1 - lo}
    far = window - 1

    def kv_up(k):
        return remote(
            kv.at[slot(last)], kv.at[slot(last - 2 * k)], kv_s.at[2 * k], kv_r.at[2 * k],
            {"ctx": lax.rem(c + 2 * k, n_ctx)},
        )

    def kv_on(k):
        away = 2 * k + 1 - 2 * lo
        return remote(
            kv.at[slot(last - 2 * k)], kv.at[slot(last - away)], kv_s.at[2 * k + 1], kv_r.at[away], mate
        )

    def kv_far():
        return remote(
            kv.at[slot(last)], kv.at[slot(last - far)], kv_f.at[0], kv_r.at[far],
            {"ctx": lax.rem(c + far, n_ctx)},
        )

    def kv_arrival(d):
        return remote(
            kv.at[slot(last - d)], kv.at[slot(last - d)], kv_s.at[0], kv_r.at[d], mate
        )

    @pl.loop(1, steps_z)
    def _(i):
        k = steps_z - i

        @pl.when(z + k < n_z)
        def _():
            kv_up(k).start()

    @pl.when((lo == 1) & (c + far < n_ctx))
    def _():
        kv_far().start()

    @pl.when(lo == 0)
    def _():
        kv_on(0).start()

    for j in range(0, GROUP_HEADS, 2):
        pair = project(xfull, wq, j * HEAD_SIZE, 2 * HEAD_SIZE)
        q_s[j * BLOCK : (j + 1) * BLOCK] = pair[:, :HEAD_SIZE]
        q_s[(j + 1) * BLOCK : (j + 2) * BLOCK] = pair[:, HEAD_SIZE:]
    h1_ex[0]()
    hid_p[z] = xfull[z, my_rows]

    def pass_hidden():
        h1_ex[1]()
        h2_ex[0]()
        hid_z[:, t] = hid_p[...]

    def head_cotangent(arrival):
        wo_copy.wait()
        hc_acc[...] = jnp.zeros_like(hc_acc)

        @pl.loop(0, n_tp)
        def _(i):
            p = lax.rem(t - i + n_tp, n_tp)
            arrival(i, p)
            hc_acc[...] += mm(cotfull[p], wo[pl.ds(pl.multiple_of(p * part, part), part)])

        for j in range(GROUP_HEADS):
            hc_s[j * BLOCK : (j + 1) * BLOCK] = hc_acc[:, j * HEAD_SIZE : (j + 1) * HEAD_SIZE].astype(BF16)

    @pl.loop(1, steps_z)
    def _(k):
        @pl.when(z - k >= 0)
        def _():
            kv_up(k).wait_recv()
            kv_on(k).start()

    @pl.when(s == 0)
    def _():
        pass_hidden()

    @pl.when(s == 1)
    def _():
        c_ex[1]()
        head_cotangent(lambda i, p: None)

    doc_start = jnp.int32(0)
    doc_end = jnp.int32(0)
    for i in range(docs_ref.shape[1]):
        doc_end = doc_end + docs_ref[0, i]
        doc_start = jnp.where(doc_end <= c, doc_end, doc_start)
    pairs = window // 2
    wide = (GROUP_HEADS * BLOCK, 2 * BLOCK)
    query_pos = c * BLOCK + lax.broadcasted_iota(jnp.int32, wide, 0) % BLOCK
    first_key = (c - last) * BLOCK + lax.broadcasted_iota(jnp.int32, wide, 1)

    def keys(g):
        return kv[g * 2 * BLOCK : (g + 1) * 2 * BLOCK, :HEAD_SIZE]

    def values(g):
        return kv[g * 2 * BLOCK : (g + 1) * 2 * BLOCK, HEAD_SIZE:]

    for g in range(pairs - 1, -1, -1):
        for j in (2 * g + 1, 2 * g):
            if j < last:

                if (last - j) % 2 == 1:

                    @pl.when(c - last + j >= 0)
                    def _():
                        kv_arrival(last - j).wait_recv()

        block = mm(q_s[...], keys(g), NT) * scale
        key_pos = first_key + g * 2 * BLOCK
        block = jnp.where((key_pos <= query_pos) & (key_pos >= doc_start * BLOCK), block, NEG_FILL)
        scores[g] = block
        both = jnp.maximum(block[:, :BLOCK], block[:, BLOCK:])
        peak[...] = both if g == pairs - 1 else jnp.maximum(peak[...], both)

    top = jnp.max(peak[...], axis=1, keepdims=True)
    for g in range(pairs):
        e = jnp.exp(scores[g] - top)
        scores[g] = e
        both = e[:, :BLOCK] + e[:, BLOCK:]
        denom[...] = both if g == 0 else denom[...] + both

    inverse = 1.0 / jnp.sum(denom[...], axis=1, keepdims=True)
    for g in range(pairs):
        soft = scores[g] * inverse
        low = soft.astype(BF16)
        scores[g] = soft
        probs[g] = low
        term = mm(low, values(g))
        acc[...] = term if g == 0 else acc[...] + term

    att_s[...] = acc[...].astype(BF16)
    for j in range(GROUP_HEADS):
        att_z[own_z, j * HEAD_SIZE : (j + 1) * HEAD_SIZE] = att_s[j * BLOCK : (j + 1) * BLOCK]

    def sec_copy(p):
        return remote(gin_ref, cotfull.at[t], sec_s.at[p], c_r.at[t], {"section": 1 - s, "tp": p})

    @pl.when(s == 1)
    def _():
        pass_hidden()

    @pl.when(s == 0)
    def _():
        att_ring[0](1)

        def arrival(i, p):
            remote(cotfull.at[p], cotfull.at[p], sec_s.at[p], c_r.at[p], {"section": 1 - s}).wait_recv()

        head_cotangent(arrival)
        att_ring[0](2)

    delta = jnp.sum(hc_s[...].astype(F32) * att_s[...].astype(F32), axis=1, keepdims=True)

    def dkv_copy(d):
        return remote(
            dkv_part.at[slot(last - d)], dkv_in.at[d], d_s.at[d], d_r.at[d],
            {"ctx": lax.rem(c - d + n_ctx, n_ctx)},
        )

    for g in range(pairs):
        block = slice(g * 2 * BLOCK, (g + 1) * 2 * BLOCK)
        dprobs = mm(hc_s[...], values(g), NT)
        ds = (scores[g] * (dprobs - delta)).astype(BF16)
        dkv_part[block, :HEAD_SIZE] = (mm(ds, q_s[...], TN) * scale).astype(BF16)
        dkv_part[block, HEAD_SIZE:] = mm(probs[g], hc_s[...], TN).astype(BF16)
        dscores[g] = ds
        for j in (2 * g, 2 * g + 1):
            if j < last:

                @pl.when(c - last + j >= 0)
                def _():
                    dkv_copy(last - j).start()

    total = mm(dscores[0], keys(0))
    for g in range(1, pairs):
        total = total + mm(dscores[g], keys(g))
    acc[...] = total
    for j in range(GROUP_HEADS):
        gq_n[:, j * HEAD_SIZE : (j + 1) * HEAD_SIZE] = (
            acc[j * BLOCK : (j + 1) * BLOCK] * scale
        ).astype(BF16)
    gq_z[own_z] = gq_n[...]

    def send_cot():
        c1_ex[0]()
        cot_p[z] = cotfull[z, my_rows]

    def pass_cot():
        c1_ex[1]()
        c2_ex[0]()
        cot_z[:, t] = cot_p[...]

    @pl.when(s == 0)
    def _():
        send_cot()
        gq_ring[0](1)
        att_ring[0](3)

    @pl.loop(0, n_tp)
    def _(p):
        feat_f[p] = mm(gq_n[...], wq[pl.ds(p * part, part), :heads], NT)

    @pl.when(s == 0)
    def _():
        pass_cot()
        gq_ring[0](2)
        att_ring[0](4)

    acc[:BLOCK] = dkv_part[slot(last), :HEAD_SIZE].astype(F32)
    acc[BLOCK : 2 * BLOCK] = dkv_part[slot(last), HEAD_SIZE:].astype(F32)

    @pl.loop(1, window)
    def _(d):
        @pl.when(c + d < n_ctx)
        def _():
            dkv_copy(d).wait_recv()
            acc[:BLOCK] += dkv_in[d, :, :HEAD_SIZE].astype(F32)
            acc[BLOCK : 2 * BLOCK] += dkv_in[d, :, HEAD_SIZE:].astype(F32)

    gkv_n[:, :HEAD_SIZE] = acc[:BLOCK].astype(BF16)
    gkv_n[:, HEAD_SIZE:] = acc[BLOCK : 2 * BLOCK].astype(BF16)
    gkv_z[own_z] = gkv_n[...]
    kz_ex[0]()

    row_sum = gkv_n[:, :HEAD_SIZE].astype(F32) * kv[slot(last), :HEAD_SIZE].astype(F32)
    row_sum = row_sum + gkv_n[:, HEAD_SIZE:].astype(F32) * kv[slot(last), HEAD_SIZE:].astype(F32)
    for j in range(GROUP_HEADS):
        row_sum = row_sum + gq_n[:, j * HEAD_SIZE : (j + 1) * HEAD_SIZE].astype(F32) * q_s[
            j * BLOCK : (j + 1) * BLOCK
        ].astype(F32)
    row_sum = jnp.sum(row_sum, axis=1, keepdims=True)
    rs_out[...] = jnp.broadcast_to(row_sum, (BLOCK, BLOCK)).T[:8]
    r_ex[0]()
    rs_in[t] = rs_out[...]

    @pl.loop(1, n_tp + 1)
    def _(i):
        p = lax.rem(t + i, n_tp)
        total = feat_f[p] + mm(gkv_n[...], wq[pl.ds(p * part, part), heads:], NT)
        feat_out[p] = total.astype(BF16)

        @pl.when(i < n_tp)
        def _():
            f_ex[3](p).start()

    feat_in[t] = feat_out[t]

    y_copies = [
        remote(y_out_o, y_in_o, y_s.at[0], y_r.at[0], mate),
        remote(y_out_q, y_in_q, y_s.at[1], y_r.at[1], mate),
        remote(y_out_k, y_in_k, y_s.at[2], y_r.at[2], mate),
    ]
    positions = n_z * BLOCK
    theirs = pl.ds(pl.multiple_of((1 - lo) * half, half), half)
    mine = pl.ds(pl.multiple_of(lo * half, half), half)

    def turn(ref):
        turned[...] = ref[...].reshape(positions, part).T

    def weight_part(right, y_out, out, base, copy):
        step = min(256, heads)
        for k in range(0, right.shape[1], step):
            y_out[:, k : k + step] = mm(turned[theirs], right[:, k : k + step]).astype(BF16)
        copy.start()
        for k in range(0, right.shape[1], step):
            out[:, base + k : base + k + step] = mm(turned[mine], right[:, k : k + step])

    def grad_of_out():
        c2_ex[1]()
        att_ring[1]()
        turn(cot_z)
        weight_part(att_z, y_out_o, gout_ref, 0, y_copies[0])

    def grad_of_query():
        h2_ex[1]()
        turn(hid_z)
        gq_ring[1]()
        weight_part(gq_z, y_out_q, gqkv_ref, 0, y_copies[1])

    @pl.when(s == 0)
    def _():
        gq_ring[0](3)
        grad_of_out()
        gq_ring[0](4)
        grad_of_query()

    f_ex[1]()
    r_ex[1]()
    feature = jnp.zeros((BLOCK, part), F32)
    for p in range(n_tp):
        feature = feature + feat_in[p].astype(F32)
    inv = inv_b[:, :1]
    gain = gain_ref[:, pl.ds(pl.multiple_of(t * part, part), part)]
    scaled = feature * gain
    normed = x_ref[...].astype(F32) * inv
    mean = total_of(rs_in)[:, :1] / width
    gin_ref[...] = (cotfull[t].astype(F32) + inv * (scaled - normed * mean)).astype(BF16)

    @pl.when(s == 1)
    def _():
        @pl.loop(0, n_tp)
        def _(i):
            sec_copy(lax.rem(t + i, n_tp)).start()

        send_cot()
        for k in range(1, n_z // 2 + 1):
            att_ring[0](k)
            gq_ring[0](k)
            if k == 2 or n_z == 2:
                pass_cot()
        grad_of_out()
        grad_of_query()

    kz_ex[1]()
    weight_part(gkv_z, y_out_k, gqkv_ref, heads, y_copies[2])
    for y_in, out, base, copy in (
        (y_in_o, gout_ref, 0, y_copies[0]),
        (y_in_q, gqkv_ref, 0, y_copies[1]),
        (y_in_k, gqkv_ref, heads, y_copies[2]),
    ):
        copy.wait_recv()
        out[:, base : base + y_in.shape[1]] += y_in[...].astype(F32)

    for ex in (x_ex, q_ex, f_ex, r_ex, h1_ex, h2_ex, c1_ex, c2_ex, kz_ex, att_ring, gq_ring):
        ex[2]()
    for copy in y_copies:
        copy.wait_send()

    @pl.loop(1, steps_z)
    def _(k):
        @pl.when(z + k < n_z)
        def _():
            kv_up(k).wait_send()

        @pl.when(z - k >= 0)
        def _():
            kv_on(k).wait_send()

    @pl.when((lo == 1) & (c + far < n_ctx))
    def _():
        kv_far().wait_send()

    @pl.when(lo == 0)
    def _():
        kv_on(0).wait_send()

    @pl.loop(1, window)
    def _(d):
        @pl.when(c - d >= 0)
        def _():
            dkv_copy(d).wait_send()

    @pl.when(s == 1)
    def _():
        c_ex[2]()

        @pl.loop(0, n_tp)
        def _(p):
            sec_copy(p).wait_send()


def settle(a_in, b_in, c_in, a_out, b_out, c_out, sem):
    copies = [
        pltpu.make_async_copy(source, target, sem.at[i])
        for i, (source, target) in enumerate(((a_in, a_out), (b_in, b_out), (c_in, c_out)))
    ]
    for copy in copies:
        copy.start()
    for copy in copies:
        copy.wait()


def body(layer_input, loss_cot, token_weights, doc_blocks, norm_gain, qkv_weight, out_weight):
    n_ctx, n_tp = lax.axis_size("ctx"), lax.axis_size("tp")
    n_z = n_ctx // 2
    part = layer_input.shape[3]
    width = part * n_tp
    cols, heads = qkv_weight.shape[2], out_weight.shape[2]
    window = min(MAX_DOC, n_ctx)
    q_rows = GROUP_HEADS * BLOCK
    kv_cols = 2 * HEAD_SIZE
    half = part // 2
    share = BLOCK // n_tp
    vmem = lambda shape, dtype=BF16: pltpu.VMEM(shape, dtype)
    dma = lambda *n: pltpu.SemaphoreType.DMA(n)
    scratch = [
        vmem((width, cols)), vmem((width, heads)),
        vmem((n_tp, BLOCK, part)), vmem((n_tp, BLOCK, part)), vmem((BLOCK, part)), vmem((BLOCK, BLOCK), F32),
        vmem((window * BLOCK, kv_cols)),
        vmem((q_rows, HEAD_SIZE)), vmem((q_rows, HEAD_SIZE)), vmem((q_rows, HEAD_SIZE)),
        vmem((BLOCK, heads)), vmem((BLOCK, kv_cols)),
        vmem((window // 2, q_rows, 2 * BLOCK), F32), vmem((window // 2, q_rows, 2 * BLOCK)),
        vmem((window // 2, q_rows, 2 * BLOCK)),
        vmem((q_rows, BLOCK), F32), vmem((q_rows, BLOCK), F32), vmem((q_rows, HEAD_SIZE), F32),
        vmem((BLOCK, kv_cols), F32), vmem((BLOCK, heads), F32), vmem((8, BLOCK), F32), vmem((n_tp, 8, BLOCK), F32),
        vmem((window * BLOCK, kv_cols)), vmem((window, BLOCK, kv_cols)),
        vmem((n_tp, BLOCK, part), F32), vmem((n_tp, BLOCK, part)), vmem((n_tp, BLOCK, part)),
        vmem((8, BLOCK), F32), vmem((n_tp, 8, BLOCK), F32),
        vmem((n_z, share, part)), vmem((n_z, share, part)),
        vmem((n_z, n_tp, share, part)), vmem((n_z, n_tp, share, part)), vmem((n_z * BLOCK, heads)),
        vmem((n_z * BLOCK, heads)), vmem((n_z * BLOCK, kv_cols)), vmem((part, n_z * BLOCK)),
        vmem((half, heads)), vmem((half, heads)), vmem((half, kv_cols)),
        vmem((half, heads)), vmem((half, heads)), vmem((half, kv_cols)),
        dma(2), dma(n_tp), dma(n_tp), dma(n_tp), dma(n_tp), dma(window), dma(window), dma(1), dma(window), dma(window),
        dma(n_tp), dma(n_tp), dma(n_tp), dma(n_tp),
        dma(n_z), dma(n_z), dma(n_tp), dma(n_tp), dma(n_z), dma(n_z), dma(n_tp), dma(n_tp),
        dma(n_z), dma(n_z), dma(n_z), dma(n_z), dma(n_z), dma(n_z),
        dma(3), dma(3), dma(n_tp), dma(n_tp), dma(n_tp), pltpu.SemaphoreType.REGULAR,
    ]
    in_vmem = pl.BlockSpec(memory_space=pltpu.VMEM)
    anywhere = pl.BlockSpec(memory_space=pl.ANY)
    grad_in, grad_qkv, grad_out = pl.pallas_call(
        functools.partial(kernel, n_ctx, n_tp, window),
        out_shape=(
            jax.ShapeDtypeStruct((BLOCK, part), BF16),
            jax.ShapeDtypeStruct((half, cols), F32),
            jax.ShapeDtypeStruct((half, heads), F32),
        ),
        in_specs=[
            in_vmem, in_vmem, in_vmem, pl.BlockSpec(memory_space=pltpu.SMEM), in_vmem, anywhere, anywhere,
        ],
        out_specs=(in_vmem, in_vmem, in_vmem),
        scratch_shapes=scratch,
        compiler_params=pltpu.CompilerParams(
            collective_id=0, has_side_effects=True, vmem_limit_bytes=56 * 1024 * 1024
        ),
    )(
        layer_input[0, 0], loss_cot[0], token_weights, doc_blocks, norm_gain, qkv_weight[0], out_weight[0]
    )
    results = (grad_in, grad_qkv, grad_out)
    grad_in, grad_qkv, grad_out = pl.pallas_call(
        settle,
        out_shape=tuple(jax.ShapeDtypeStruct(r.shape, r.dtype) for r in results),
        in_specs=[in_vmem] * 3,
        out_specs=(anywhere,) * 3,
        scratch_shapes=[dma(3)],
    )(*results)
    return grad_in[None, None], grad_qkv[None], grad_out[None]


def solution(mesh):
    placed = (
        P("section", None, "ctx", "tp"),
        P(None, "ctx", "tp"),
        P(None, "ctx"),
        P(),
        P("section", None),
        P("section", None, "tp"),
        P("section", None, "tp"),
    )
    return jax.shard_map(
        body,
        mesh=mesh,
        in_specs=placed,
        out_specs=(
            P("section", None, "ctx", "tp"),
            P("section", "ctx", "tp"),
            P("section", "ctx", "tp"),
        ),
        check_vma=False,
    )
```

```python
import functools

import jax
import jax.numpy as jnp
from jax import lax
from jax.experimental import pallas as pl
from jax.experimental.pallas import tpu as pltpu
from jax.sharding import PartitionSpec as P

MESH = pl.DeviceIdType.MESH
GROUP_HEADS = 4
HEAD_SIZE = 128
BLOCK = 128
MAX_DOC = 10
EPSILON = 1e-05
NEG_FILL = -1e30
F32 = jnp.float32
BF16 = jnp.bfloat16

NN = (((1,), (0,)), ((), ()))
NT = (((1,), (1,)), ((), ()))
TN = (((0,), (0,)), ((), ()))


def mm(a, b, dims=NN):
    return lax.dot_general(a, b, dims, preferred_element_type=F32)


def kernel(
    n_ctx, n_tp, window,
    x_ref, loss_ref, tw_ref, docs_ref, gain_ref, wq_hbm, wo_hbm,
    gin_ref, gqkv_ref, gout_ref,
    wq, wo, xfull, hfull, cotfull, inv_b,
    kv, q_s, hc_s, att_s, gq_n, gkv_n, scores, probs, dscores, peak, denom, acc, kv_acc, hc_acc, sq_out, sq_in,
    dkv_part, dkv_in, feat_f, feat_out, feat_in, rs_out, rs_in,
    hid_p, cot_p, hid_z, cot_z, att_z, gq_z, gkv_z, turned,
    y_out_o, y_out_q, y_out_k, y_in_o, y_in_q, y_in_k,
    w_sem, x_s, x_r, c_s, c_r, kv_s, kv_r, kv_f, d_s, d_r, f_s, f_r, r_s, r_r,
    h1_s, h1_r, h2_s, h2_r, c1_s, c1_r, c2_s, c2_r, az_s, az_r, qz_s, qz_r, kz_s, kz_r, y_s, y_r, sec_s, q_sem, q_rcv, gate,
):
    s = lax.axis_index("section")
    c = lax.axis_index("ctx")
    t = lax.axis_index("tp")
    n_z = n_ctx // 2
    z, lo = c // 2, lax.rem(c, 2)
    part = x_ref.shape[1]
    width = part * n_tp
    half = part // 2
    heads = GROUP_HEADS * HEAD_SIZE
    cols = heads + 2 * HEAD_SIZE
    scale = HEAD_SIZE ** (-0.5)
    last = window - 1

    def remote(src, dst, ss, rs, dev):
        return pltpu.make_async_remote_copy(
            src_ref=src, dst_ref=dst, send_sem=ss, recv_sem=rs, device_id=dev, device_id_type=MESH
        )

    def tp_dev(p):
        return {"tp": p}

    def z_dev(p):
        return {"ctx": p * 2 + lo}

    def exchange(n, me, dev, src_of, slot, ss, rs):
        def copy_to(p):
            return remote(src_of(p), slot(me), ss.at[p], rs.at[me], dev(p))

        def copy_from(p):
            return remote(slot(p), slot(p), ss.at[p], rs.at[p], dev(p))

        def start():
            @pl.loop(1, n)
            def _(i):
                copy_to(lax.rem(me + i, n)).start()

        def wait_recv():
            @pl.loop(1, n)
            def _(i):
                copy_from(lax.rem(me + i, n)).wait_recv()

        def wait_send():
            @pl.loop(1, n)
            def _(i):
                copy_to(lax.rem(me + i, n)).wait_send()

        return start, wait_recv, wait_send, copy_to, copy_from

    def ring(ref, ss, rs):
        up, down = z_dev(lax.rem(z + 1, n_z)), z_dev(lax.rem(z + n_z - 1, n_z))
        top = n_z // 2

        def piece(p, k, side):
            if k < top:
                return ref.at[pl.ds(p * BLOCK, BLOCK)]
            return ref.at[pl.ds(p * BLOCK + side * (BLOCK // 2), BLOCK // 2)]

        def pair(k, shift):
            below = piece(lax.rem(z - k + shift + n_z, n_z), k, 0)
            above = piece(lax.rem(z + k - shift, n_z), k, 1)
            return (
                remote(below, below, ss.at[k - 1], rs.at[k - 1], up),
                remote(above, above, ss.at[top + k - 1], rs.at[top + k - 1], down),
            )

        def arrive(k):
            for copy in pair(k, 0):
                copy.wait_recv()

        def stage(k):
            if k > top:
                return
            if k > 1:
                arrive(k - 1)
            for copy in pair(k, 1):
                copy.start()

        def wait_send():
            for k in range(1, top + 1):
                for copy in pair(k, 1):
                    copy.wait_send()

        return stage, lambda: arrive(top), wait_send

    n_x = n_tp // 2
    ty, tx = t // n_x, lax.rem(t, n_x)

    def at(dy, dx):
        return (ty if dy == 0 else 1 - ty) * n_x + lax.rem(tx + dx + n_x, n_x)

    near = [at(0, -1), at(0, 1)] if n_x > 1 else []
    mate_t = at(1, 0)
    order = [t] + near + [mate_t]
    if n_x > 1:
        order = order + [at(1, -1), at(1, 1), at(0, 2), at(1, 2)]

    class Spread:
        def __init__(self, piece, ss, rs):
            self.piece, self.ss, self.rs = piece, ss, rs
            self.sends = [self.move(t, None, 0, t, mate_t)]
            if n_x > 1:
                left, right = near
                self.sends += [
                    self.move(t, None, 1, t, right),
                    self.move(t, None, 2, t, left),
                    self.move(left, 0, 3, left, right),
                    self.move(right, 1, 4, n_tp, left),
                    self.move(mate_t, None, 5, mate_t, right),
                    self.move(mate_t, None, 6, mate_t, left),
                    self.move(at(1, -1), 0, 7, at(1, -1), right),
                    self.move(at(1, 1), 1, 8, n_tp + 1, left),
                ]

        def move(self, p, side, i, r, to):
            return remote(self.piece(p, side), self.piece(p, side), self.ss.at[i], self.rs.at[r], {"tp": to})

        def arrive(self, p, side=None, r=None):
            self.move(p, side, 0, p if r is None else r, mate_t).wait_recv()

        def start(self):
            for copy in self.sends[:3]:
                copy.start()

        def relay(self):
            if n_x > 1:
                for p, copy in zip(near, self.sends[3:5]):
                    self.arrive(p)
                    copy.start()
            self.arrive(mate_t)
            for copy in self.sends[5:7]:
                copy.start()

        def relay_far(self):
            for p, copy in zip((at(1, -1), at(1, 1)), self.sends[7:]):
                self.arrive(p)
                copy.start()

        def finish(self):
            if n_x > 1:
                for i, p in enumerate((at(0, 2), at(1, 2))):
                    self.arrive(p, 0)
                    self.arrive(p, 1, n_tp + i)

        def wait_send(self, first=0):
            for copy in self.sends[first:]:
                copy.wait_send()

    def block_of(ref):
        part_rows = BLOCK // 2

        def piece(p, side):
            return ref.at[p] if side is None else ref.at[p, pl.ds(side * part_rows, part_rows)]

        return piece

    def slice_of(ref):
        depth = n_z // 2

        def piece(p, side):
            return ref.at[:, p] if side is None else ref.at[pl.ds(side * depth, depth), p]

        return piece

    whole = lambda ref: lambda p: ref
    share = BLOCK // n_tp
    my_rows = pl.ds(pl.multiple_of(t * share, share), share)

    x_ag = Spread(block_of(xfull), x_s, x_r)
    c_ag = Spread(block_of(cotfull), c_s, c_r)
    h2_ag = Spread(slice_of(hid_z), h2_s, h2_r)
    c2_ag = Spread(slice_of(cot_z), c2_s, c2_r)
    f_ex = exchange(n_tp, t, tp_dev, lambda p: feat_out.at[p], lambda p: feat_in.at[p], f_s, f_r)
    q_ex = exchange(n_tp, t, tp_dev, whole(sq_out), lambda p: sq_in.at[p], q_sem, q_rcv)
    r_ex = exchange(n_tp, t, tp_dev, whole(rs_out), lambda p: rs_in.at[p], r_s, r_r)
    h1_ex = exchange(n_z, z, z_dev, lambda p: hfull.at[p, my_rows], lambda p: hid_p.at[p], h1_s, h1_r)
    c1_ex = exchange(n_z, z, z_dev, lambda p: cotfull.at[p, my_rows], lambda p: cot_p.at[p], c1_s, c1_r)
    att_ring = ring(att_z, az_s, az_r)
    gq_ring = ring(gq_z, qz_s, qz_r)
    kz_ex = exchange(n_z, z, z_dev, whole(gkv_n), lambda p: gkv_z.at[pl.ds(p * BLOCK, BLOCK)], kz_s, kz_r)
    own_z = pl.ds(pl.multiple_of(z * BLOCK, BLOCK), BLOCK)
    wq_copy = pltpu.make_async_copy(wq_hbm, wq, w_sem.at[0])
    wo_copy = pltpu.make_async_copy(wo_hbm, wo, w_sem.at[1])

    wq_copy.start()
    wo_copy.start()
    kv[...] = jnp.zeros_like(kv)
    own_x = x_ref[...].astype(F32)
    square_sum = jnp.sum(own_x * own_x, axis=1, keepdims=True)
    sq_out[...] = jnp.broadcast_to(square_sum, (BLOCK, BLOCK)).T[:8]

    barrier = pltpu.get_barrier_semaphore()

    @pl.loop(1, n_tp)
    def _(i):
        pl.semaphore_signal(barrier, inc=1, device_id={"tp": lax.rem(t + i, n_tp)}, device_id_type=MESH)

    @pl.loop(1, n_ctx)
    def _(i):
        pl.semaphore_signal(barrier, inc=1, device_id={"ctx": lax.rem(c + i, n_ctx)}, device_id_type=MESH)

    @pl.loop(0, n_tp)
    def _(p):
        pl.semaphore_signal(barrier, inc=1, device_id={"section": 1 - s, "tp": p}, device_id_type=MESH)

    pl.semaphore_wait(barrier, 2 * n_tp + n_ctx - 2)

    @pl.when(s == 0)
    def _():
        pl.semaphore_wait(gate, 1)

    xfull[t] = x_ref[...]
    q_ex[0]()
    x_ag.start()
    sq_in[t] = sq_out[...]

    def total_of(ref):
        total = ref[0]
        for p in range(1, n_tp):
            total = total + ref[p]
        return jnp.broadcast_to(total[:1], (BLOCK, BLOCK)).T

    q_ex[1]()
    inv_b[...] = lax.rsqrt(total_of(sq_in) / width + EPSILON)
    kv_acc[...] = jnp.zeros_like(kv_acc)
    wq_copy.wait()

    def norm_block(p):
        cols_p = pl.ds(pl.multiple_of(p * part, part), part)
        hidden = ((xfull[p].astype(F32) * inv_b[:, :1]) * gain_ref[:, cols_p]).astype(BF16)
        hfull[p] = hidden
        kv_acc[...] += mm(hidden, wq[cols_p, heads:])

    norm_block(t)
    x_ag.relay()
    for p in order[1:4]:
        norm_block(p)
    if n_x > 1:
        x_ag.relay_far()
    x_ag.finish()

    @pl.when(s == 1)
    def _():
        weights = jnp.broadcast_to(tw_ref[...].astype(F32), (BLOCK, BLOCK)).T[:, :1]
        cotfull[t] = (loss_ref[...].astype(F32) * weights).astype(BF16)
        c_ag.start()

    for p in order[4:]:
        norm_block(p)

    def project(full, weight, lo_col, n_col):
        total = jnp.zeros((BLOCK, n_col), F32)
        for p in range(n_tp):
            total = total + mm(full[p], weight[p * part : (p + 1) * part, lo_col : lo_col + n_col])
        return total.astype(BF16)

    def slot(j):
        if isinstance(j, int):
            return pl.ds(j * BLOCK, BLOCK)
        return pl.ds(pl.multiple_of(j * BLOCK, BLOCK), BLOCK)

    kv[slot(last)] = kv_acc[...].astype(BF16)

    steps_z = (window - 1) // 2 + 1
    mate = {"ctx": z * 2 + 1 - lo}
    far = window - 1

    def kv_up(k):
        return remote(
            kv.at[slot(last)], kv.at[slot(last - 2 * k)], kv_s.at[2 * k], kv_r.at[2 * k],
            {"ctx": lax.rem(c + 2 * k, n_ctx)},
        )

    def kv_on(k):
        away = 2 * k + 1 - 2 * lo
        return remote(
            kv.at[slot(last - 2 * k)], kv.at[slot(last - away)], kv_s.at[2 * k + 1], kv_r.at[away], mate
        )

    def kv_far():
        return remote(
            kv.at[slot(last)], kv.at[slot(last - far)], kv_f.at[0], kv_r.at[far],
            {"ctx": lax.rem(c + far, n_ctx)},
        )

    def kv_arrival(d):
        return remote(
            kv.at[slot(last - d)], kv.at[slot(last - d)], kv_s.at[0], kv_r.at[d], mate
        )

    @pl.loop(1, steps_z)
    def _(i):
        k = steps_z - i

        @pl.when(z + k < n_z)
        def _():
            kv_up(k).start()

    @pl.when((lo == 1) & (c + far < n_ctx))
    def _():
        kv_far().start()

    @pl.when(lo == 0)
    def _():
        kv_on(0).start()

    for j in range(0, GROUP_HEADS, 2):
        pair = project(hfull, wq, j * HEAD_SIZE, 2 * HEAD_SIZE)
        q_s[j * BLOCK : (j + 1) * BLOCK] = pair[:, :HEAD_SIZE]
        q_s[(j + 1) * BLOCK : (j + 2) * BLOCK] = pair[:, HEAD_SIZE:]
    h1_ex[0]()
    hid_p[z] = hfull[z, my_rows]

    @pl.when(s == 1)
    def _():
        c_ag.relay()
        pl.semaphore_signal(gate, inc=1, device_id={"section": 1 - s}, device_id_type=MESH)

    def pass_hidden():
        h1_ex[1]()
        hid_z[:, t] = hid_p[...]
        h2_ag.start()

    def relay_rest(ag):
        if n_x > 1:
            ag.relay_far()
        ag.finish()

    def head_cotangent(arrival):
        wo_copy.wait()
        hc_acc[...] = jnp.zeros_like(hc_acc)

        def add(p):
            hc_acc[...] += mm(cotfull[p], wo[pl.ds(pl.multiple_of(p * part, part), part)])

        if arrival is not None:
            arrival()
            add(t)
            c_ag.relay()
            for p in order[1:4]:
                add(p)
            relay_rest(c_ag)
        else:
            for p in order[:4]:
                add(p)
        for p in order[4:]:
            add(p)

        for j in range(GROUP_HEADS):
            hc_s[j * BLOCK : (j + 1) * BLOCK] = hc_acc[:, j * HEAD_SIZE : (j + 1) * HEAD_SIZE].astype(BF16)

    @pl.loop(1, steps_z)
    def _(k):
        @pl.when(z - k >= 0)
        def _():
            kv_up(k).wait_recv()
            kv_on(k).start()

    @pl.when(s == 0)
    def _():
        pass_hidden()

    @pl.when(s == 1)
    def _():
        relay_rest(c_ag)
        head_cotangent(None)

    doc_start = jnp.int32(0)
    doc_end = jnp.int32(0)
    for i in range(docs_ref.shape[1]):
        doc_end = doc_end + docs_ref[0, i]
        doc_start = jnp.where(doc_end <= c, doc_end, doc_start)
    pairs = window // 2
    wide = (GROUP_HEADS * BLOCK, 2 * BLOCK)
    query_pos = c * BLOCK + lax.broadcasted_iota(jnp.int32, wide, 0) % BLOCK
    first_key = (c - last) * BLOCK + lax.broadcasted_iota(jnp.int32, wide, 1)

    def keys(g):
        return kv[g * 2 * BLOCK : (g + 1) * 2 * BLOCK, :HEAD_SIZE]

    def values(g):
        return kv[g * 2 * BLOCK : (g + 1) * 2 * BLOCK, HEAD_SIZE:]

    for g in range(pairs - 1, -1, -1):
        for j in (2 * g + 1, 2 * g):
            if j < last:

                if (last - j) % 2 == 1:

                    @pl.when(c - last + j >= 0)
                    def _():
                        kv_arrival(last - j).wait_recv()

        block = mm(q_s[...], keys(g), NT) * scale
        key_pos = first_key + g * 2 * BLOCK
        block = jnp.where((key_pos <= query_pos) & (key_pos >= doc_start * BLOCK), block, NEG_FILL)
        scores[g] = block
        both = jnp.maximum(block[:, :BLOCK], block[:, BLOCK:])
        peak[...] = both if g == pairs - 1 else jnp.maximum(peak[...], both)

    top = jnp.max(peak[...], axis=1, keepdims=True)
    for g in range(pairs):
        e = jnp.exp(scores[g] - top)
        scores[g] = e
        both = e[:, :BLOCK] + e[:, BLOCK:]
        denom[...] = both if g == 0 else denom[...] + both

    inverse = 1.0 / jnp.sum(denom[...], axis=1, keepdims=True)
    for g in range(pairs):
        soft = scores[g] * inverse
        low = soft.astype(BF16)
        scores[g] = soft
        probs[g] = low
        term = mm(low, values(g))
        acc[...] = term if g == 0 else acc[...] + term

    att_s[...] = acc[...].astype(BF16)
    for j in range(GROUP_HEADS):
        att_z[own_z, j * HEAD_SIZE : (j + 1) * HEAD_SIZE] = att_s[j * BLOCK : (j + 1) * BLOCK]

    def sec_copy(i):
        return remote(gin_ref, cotfull.at[t], sec_s.at[i], c_r.at[t], {"section": 1 - s, "tp": order[i]})

    targets = min(4, len(order))

    @pl.when(s == 0)
    def _():
        h2_ag.relay()
        att_ring[0](1)
        relay_rest(h2_ag)

        def arrival():
            remote(cotfull.at[t], cotfull.at[t], sec_s.at[0], c_r.at[t], {"section": 1 - s}).wait_recv()

        head_cotangent(arrival)
        att_ring[0](2)

    delta = jnp.sum(hc_s[...].astype(F32) * att_s[...].astype(F32), axis=1, keepdims=True)

    def dkv_copy(d):
        return remote(
            dkv_part.at[slot(last - d)], dkv_in.at[d], d_s.at[d], d_r.at[d],
            {"ctx": lax.rem(c - d + n_ctx, n_ctx)},
        )

    for g in range(pairs):
        block = slice(g * 2 * BLOCK, (g + 1) * 2 * BLOCK)
        dprobs = mm(hc_s[...], values(g), NT)
        ds = (scores[g] * (dprobs - delta)).astype(BF16)
        dkv_part[block, :HEAD_SIZE] = (mm(ds, q_s[...], TN) * scale).astype(BF16)
        dkv_part[block, HEAD_SIZE:] = mm(probs[g], hc_s[...], TN).astype(BF16)
        dscores[g] = ds
        for j in (2 * g, 2 * g + 1):
            if j < last:

                @pl.when(c - last + j >= 0)
                def _():
                    dkv_copy(last - j).start()

    total = mm(dscores[0], keys(0))
    for g in range(1, pairs):
        total = total + mm(dscores[g], keys(g))
    acc[...] = total
    for j in range(GROUP_HEADS):
        gq_n[:, j * HEAD_SIZE : (j + 1) * HEAD_SIZE] = (
            acc[j * BLOCK : (j + 1) * BLOCK] * scale
        ).astype(BF16)
    gq_z[own_z] = gq_n[...]

    def send_cot():
        c1_ex[0]()
        cot_p[z] = cotfull[z, my_rows]

    def pass_cot():
        c1_ex[1]()
        cot_z[:, t] = cot_p[...]
        c2_ag.start()

    @pl.when(s == 0)
    def _():
        send_cot()
        gq_ring[0](1)
        att_ring[0](3)

    @pl.loop(0, n_tp)
    def _(p):
        feat_f[p] = mm(gq_n[...], wq[pl.ds(p * part, part), :heads], NT)

    @pl.when(s == 0)
    def _():
        pass_cot()
        gq_ring[0](2)
        att_ring[0](4)

    acc[:BLOCK] = dkv_part[slot(last), :HEAD_SIZE].astype(F32)
    acc[BLOCK : 2 * BLOCK] = dkv_part[slot(last), HEAD_SIZE:].astype(F32)

    @pl.loop(1, window)
    def _(d):
        @pl.when(c + d < n_ctx)
        def _():
            dkv_copy(d).wait_recv()
            acc[:BLOCK] += dkv_in[d, :, :HEAD_SIZE].astype(F32)
            acc[BLOCK : 2 * BLOCK] += dkv_in[d, :, HEAD_SIZE:].astype(F32)

    gkv_n[:, :HEAD_SIZE] = acc[:BLOCK].astype(BF16)
    gkv_n[:, HEAD_SIZE:] = acc[BLOCK : 2 * BLOCK].astype(BF16)
    gkv_z[own_z] = gkv_n[...]
    kz_ex[0]()

    @pl.when(s == 0)
    def _():
        c2_ag.relay()

    row_sum = gkv_n[:, :HEAD_SIZE].astype(F32) * kv[slot(last), :HEAD_SIZE].astype(F32)
    row_sum = row_sum + gkv_n[:, HEAD_SIZE:].astype(F32) * kv[slot(last), HEAD_SIZE:].astype(F32)
    for j in range(GROUP_HEADS):
        row_sum = row_sum + gq_n[:, j * HEAD_SIZE : (j + 1) * HEAD_SIZE].astype(F32) * q_s[
            j * BLOCK : (j + 1) * BLOCK
        ].astype(F32)
    row_sum = jnp.sum(row_sum, axis=1, keepdims=True)
    rs_out[...] = jnp.broadcast_to(row_sum, (BLOCK, BLOCK)).T[:8]
    r_ex[0]()
    rs_in[t] = rs_out[...]

    @pl.loop(1, n_tp + 1)
    def _(i):
        p = lax.rem(t + i, n_tp)
        total = feat_f[p] + mm(gkv_n[...], wq[pl.ds(p * part, part), heads:], NT)
        feat_out[p] = total.astype(BF16)

        @pl.when(i < n_tp)
        def _():
            f_ex[3](p).start()

    feat_in[t] = feat_out[t]

    y_copies = [
        remote(y_out_o, y_in_o, y_s.at[0], y_r.at[0], mate),
        remote(y_out_q, y_in_q, y_s.at[1], y_r.at[1], mate),
        remote(y_out_k, y_in_k, y_s.at[2], y_r.at[2], mate),
    ]
    positions = n_z * BLOCK
    theirs = pl.ds(pl.multiple_of((1 - lo) * half, half), half)
    mine = pl.ds(pl.multiple_of(lo * half, half), half)

    def turn(ref):
        turned[...] = ref[...].reshape(positions, part).T

    def weight_part(right, y_out, out, base, copy):
        step = min(256, heads)
        for k in range(0, right.shape[1], step):
            y_out[:, k : k + step] = mm(turned[theirs], right[:, k : k + step]).astype(BF16)
        copy.start()
        for k in range(0, right.shape[1], step):
            out[:, base + k : base + k + step] = mm(turned[mine], right[:, k : k + step])

    def grad_of_out():
        att_ring[1]()
        turn(cot_z)
        weight_part(att_z, y_out_o, gout_ref, 0, y_copies[0])

    def grad_of_query():
        turn(hid_z)
        gq_ring[1]()
        weight_part(gq_z, y_out_q, gqkv_ref, 0, y_copies[1])

    @pl.when(s == 0)
    def _():
        relay_rest(c2_ag)
        gq_ring[0](3)
        grad_of_out()
        gq_ring[0](4)
        grad_of_query()

    f_ex[1]()
    r_ex[1]()
    feature = jnp.zeros((BLOCK, part), F32)
    for p in range(n_tp):
        feature = feature + feat_in[p].astype(F32)
    inv = inv_b[:, :1]
    gain = gain_ref[:, pl.ds(pl.multiple_of(t * part, part), part)]
    scaled = feature * gain
    normed = x_ref[...].astype(F32) * inv
    mean = total_of(rs_in)[:, :1] / width
    gin_ref[...] = (cotfull[t].astype(F32) + inv * (scaled - normed * mean)).astype(BF16)

    @pl.when(s == 1)
    def _():
        for i in range(targets):
            sec_copy(i).start()
        send_cot()
        for k in (1, 2):
            att_ring[0](k)
            gq_ring[0](k)
        pass_hidden()
        pass_cot()
        h2_ag.relay()
        c2_ag.relay()
        att_ring[0](3)
        gq_ring[0](3)
        relay_rest(h2_ag)
        relay_rest(c2_ag)
        att_ring[0](4)
        gq_ring[0](4)
        grad_of_out()
        grad_of_query()

    kz_ex[1]()
    weight_part(gkv_z, y_out_k, gqkv_ref, heads, y_copies[2])
    for y_in, out, base, copy in (
        (y_in_o, gout_ref, 0, y_copies[0]),
        (y_in_q, gqkv_ref, 0, y_copies[1]),
        (y_in_k, gqkv_ref, heads, y_copies[2]),
    ):
        copy.wait_recv()
        out[:, base : base + y_in.shape[1]] += y_in[...].astype(F32)

    for ex in (q_ex, f_ex, r_ex, h1_ex, c1_ex, kz_ex, att_ring, gq_ring):
        ex[2]()
    for ag in (x_ag, h2_ag, c2_ag):
        ag.wait_send()
    c_ag.wait_send(3)
    for copy in y_copies:
        copy.wait_send()

    @pl.loop(1, steps_z)
    def _(k):
        @pl.when(z + k < n_z)
        def _():
            kv_up(k).wait_send()

        @pl.when(z - k >= 0)
        def _():
            kv_on(k).wait_send()

    @pl.when((lo == 1) & (c + far < n_ctx))
    def _():
        kv_far().wait_send()

    @pl.when(lo == 0)
    def _():
        kv_on(0).wait_send()

    @pl.loop(1, window)
    def _(d):
        @pl.when(c - d >= 0)
        def _():
            dkv_copy(d).wait_send()

    @pl.when(s == 1)
    def _():
        for copy in c_ag.sends[:3]:
            copy.wait_send()
        for i in range(targets):
            sec_copy(i).wait_send()


def settle(a_in, b_in, c_in, a_out, b_out, c_out, sem):
    copies = [
        pltpu.make_async_copy(source, target, sem.at[i])
        for i, (source, target) in enumerate(((a_in, a_out), (b_in, b_out), (c_in, c_out)))
    ]
    for copy in copies:
        copy.start()
    for copy in copies:
        copy.wait()


def body(layer_input, loss_cot, token_weights, doc_blocks, norm_gain, qkv_weight, out_weight):
    n_ctx, n_tp = lax.axis_size("ctx"), lax.axis_size("tp")
    n_z = n_ctx // 2
    part = layer_input.shape[3]
    width = part * n_tp
    cols, heads = qkv_weight.shape[2], out_weight.shape[2]
    window = min(MAX_DOC, n_ctx)
    q_rows = GROUP_HEADS * BLOCK
    kv_cols = 2 * HEAD_SIZE
    half = part // 2
    share = BLOCK // n_tp
    vmem = lambda shape, dtype=BF16: pltpu.VMEM(shape, dtype)
    dma = lambda *n: pltpu.SemaphoreType.DMA(n)
    scratch = [
        vmem((width, cols)), vmem((width, heads)),
        vmem((n_tp, BLOCK, part)), vmem((n_tp, BLOCK, part)), vmem((n_tp, BLOCK, part)), vmem((BLOCK, BLOCK), F32),
        vmem((window * BLOCK, kv_cols)),
        vmem((q_rows, HEAD_SIZE)), vmem((q_rows, HEAD_SIZE)), vmem((q_rows, HEAD_SIZE)),
        vmem((BLOCK, heads)), vmem((BLOCK, kv_cols)),
        vmem((window // 2, q_rows, 2 * BLOCK), F32), vmem((window // 2, q_rows, 2 * BLOCK)),
        vmem((window // 2, q_rows, 2 * BLOCK)),
        vmem((q_rows, BLOCK), F32), vmem((q_rows, BLOCK), F32), vmem((q_rows, HEAD_SIZE), F32),
        vmem((BLOCK, kv_cols), F32), vmem((BLOCK, heads), F32), vmem((8, BLOCK), F32), vmem((n_tp, 8, BLOCK), F32),
        vmem((window * BLOCK, kv_cols)), vmem((window, BLOCK, kv_cols)),
        vmem((n_tp, BLOCK, part), F32), vmem((n_tp, BLOCK, part)), vmem((n_tp, BLOCK, part)),
        vmem((8, BLOCK), F32), vmem((n_tp, 8, BLOCK), F32),
        vmem((n_z, share, part)), vmem((n_z, share, part)),
        vmem((n_z, n_tp, share, part)), vmem((n_z, n_tp, share, part)), vmem((n_z * BLOCK, heads)),
        vmem((n_z * BLOCK, heads)), vmem((n_z * BLOCK, kv_cols)), vmem((part, n_z * BLOCK)),
        vmem((half, heads)), vmem((half, heads)), vmem((half, kv_cols)),
        vmem((half, heads)), vmem((half, heads)), vmem((half, kv_cols)),
        dma(2), dma(9), dma(n_tp + 2), dma(9), dma(n_tp + 2), dma(window), dma(window), dma(1), dma(window), dma(window),
        dma(n_tp), dma(n_tp), dma(n_tp), dma(n_tp),
        dma(n_z), dma(n_z), dma(9), dma(n_tp + 2), dma(n_z), dma(n_z), dma(9), dma(n_tp + 2),
        dma(n_z), dma(n_z), dma(n_z), dma(n_z), dma(n_z), dma(n_z),
        dma(3), dma(3), dma(4), dma(n_tp), dma(n_tp), pltpu.SemaphoreType.REGULAR,
    ]
    in_vmem = pl.BlockSpec(memory_space=pltpu.VMEM)
    anywhere = pl.BlockSpec(memory_space=pl.ANY)
    grad_in, grad_qkv, grad_out = pl.pallas_call(
        functools.partial(kernel, n_ctx, n_tp, window),
        out_shape=(
            jax.ShapeDtypeStruct((BLOCK, part), BF16),
            jax.ShapeDtypeStruct((half, cols), F32),
            jax.ShapeDtypeStruct((half, heads), F32),
        ),
        in_specs=[
            in_vmem, in_vmem, in_vmem, pl.BlockSpec(memory_space=pltpu.SMEM), in_vmem, anywhere, anywhere,
        ],
        out_specs=(in_vmem, in_vmem, in_vmem),
        scratch_shapes=scratch,
        compiler_params=pltpu.CompilerParams(
            collective_id=0, has_side_effects=True, vmem_limit_bytes=56 * 1024 * 1024
        ),
    )(
        layer_input[0, 0], loss_cot[0], token_weights, doc_blocks, norm_gain, qkv_weight[0], out_weight[0]
    )
    results = (grad_in, grad_qkv, grad_out)
    grad_in, grad_qkv, grad_out = pl.pallas_call(
        settle,
        out_shape=tuple(jax.ShapeDtypeStruct(r.shape, r.dtype) for r in results),
        in_specs=[in_vmem] * 3,
        out_specs=(anywhere,) * 3,
        scratch_shapes=[dma(3)],
    )(*results)
    return grad_in[None, None], grad_qkv[None], grad_out[None]


def solution(mesh):
    placed = (
        P("section", None, "ctx", "tp"),
        P(None, "ctx", "tp"),
        P(None, "ctx"),
        P(),
        P("section", None),
        P("section", None, "tp"),
        P("section", None, "tp"),
    )
    return jax.shard_map(
        body,
        mesh=mesh,
        in_specs=placed,
        out_specs=(
            P("section", None, "ctx", "tp"),
            P("section", "ctx", "tp"),
            P("section", "ctx", "tp"),
        ),
        check_vma=False,
    )
```

```python
import functools

import jax
import jax.numpy as jnp
from jax import lax
from jax.experimental import pallas as pl
from jax.experimental.pallas import tpu as pltpu
from jax.sharding import PartitionSpec as P

MESH = pl.DeviceIdType.MESH
GROUP_HEADS = 4
HEAD_SIZE = 128
BLOCK = 128
MAX_DOC = 10
EPSILON = 1e-05
NEG_FILL = -1e30
F32 = jnp.float32
BF16 = jnp.bfloat16

NN = (((1,), (0,)), ((), ()))
NT = (((1,), (1,)), ((), ()))
TN = (((0,), (0,)), ((), ()))


def mm(a, b, dims=NN):
    return lax.dot_general(a, b, dims, preferred_element_type=F32)


def kernel(
    n_ctx, n_tp, window,
    x_ref, loss_ref, tw_ref, docs_ref, gain_ref, wq_hbm, wo_hbm,
    gin_ref, gqkv_ref, gout_ref,
    wq, wo, xfull, cotfull, cot_loc, inv_b,
    kv, q_s, hc_s, att_s, gq_n, gkv_n, scores, probs, dscores, peak, denom, acc,
    dkv_part, dkv_in, feat_f, feat_out, feat_in, rs_out, rs_in,
    hid_p, cot_p, hid_z, cot_z, att_z, gq_z, gkv_z, turned,
    y_out_o, y_out_q, y_out_k, y_in_o, y_in_q, y_in_k,
    w_sem, x_s, x_r, c_s, c_r, kv_s, kv_r, kv_f, d_s, d_r, f_s, f_r, r_s, r_r,
    h1_s, h1_r, h2_s, h2_r, c1_s, c1_r, c2_s, c2_r, az_s, az_r, qz_s, qz_r, kz_s, kz_r, y_s, y_r, sec_s, gate,
):
    s = lax.axis_index("section")
    c = lax.axis_index("ctx")
    t = lax.axis_index("tp")
    n_z = n_ctx // 2
    z, lo = c // 2, lax.rem(c, 2)
    part = x_ref.shape[1]
    width = part * n_tp
    half = part // 2
    heads = GROUP_HEADS * HEAD_SIZE
    cols = heads + 2 * HEAD_SIZE
    scale = HEAD_SIZE ** (-0.5)
    last = window - 1

    def remote(src, dst, ss, rs, dev):
        return pltpu.make_async_remote_copy(
            src_ref=src, dst_ref=dst, send_sem=ss, recv_sem=rs, device_id=dev, device_id_type=MESH
        )

    def tp_dev(p):
        return {"tp": p}

    def z_dev(p):
        return {"ctx": p * 2 + lo}

    def exchange(n, me, dev, src_of, slot, ss, rs):
        def copy_to(p):
            return remote(src_of(p), slot(me), ss.at[p], rs.at[me], dev(p))

        def copy_from(p):
            return remote(slot(p), slot(p), ss.at[p], rs.at[p], dev(p))

        def start():
            @pl.loop(1, n)
            def _(i):
                copy_to(lax.rem(me + i, n)).start()

        def wait_recv():
            @pl.loop(1, n)
            def _(i):
                copy_from(lax.rem(me + i, n)).wait_recv()

        def wait_send():
            @pl.loop(1, n)
            def _(i):
                copy_to(lax.rem(me + i, n)).wait_send()

        return start, wait_recv, wait_send, copy_to

    def ring(ref, ss, rs):
        up, down = z_dev(lax.rem(z + 1, n_z)), z_dev(lax.rem(z + n_z - 1, n_z))
        top = n_z // 2

        def piece(p, k, side):
            if k < top:
                return ref.at[pl.ds(p * BLOCK, BLOCK)]
            return ref.at[pl.ds(p * BLOCK + side * (BLOCK // 2), BLOCK // 2)]

        def pair(k, shift):
            below = piece(lax.rem(z - k + shift + n_z, n_z), k, 0)
            above = piece(lax.rem(z + k - shift, n_z), k, 1)
            return (
                remote(below, below, ss.at[k - 1], rs.at[k - 1], up),
                remote(above, above, ss.at[top + k - 1], rs.at[top + k - 1], down),
            )

        def arrive(k):
            for copy in pair(k, 0):
                copy.wait_recv()

        def stage(k):
            if k > top:
                return
            if k > 1:
                arrive(k - 1)
            for copy in pair(k, 1):
                copy.start()

        def wait_send():
            for k in range(1, top + 1):
                for copy in pair(k, 1):
                    copy.wait_send()

        return stage, lambda: arrive(top), wait_send

    whole = lambda ref: lambda p: ref
    share = BLOCK // n_tp
    my_rows = pl.ds(pl.multiple_of(t * share, share), share)

    x_ex = exchange(n_tp, t, tp_dev, whole(x_ref), lambda p: xfull.at[p], x_s, x_r)
    c_ex = exchange(n_tp, t, tp_dev, whole(cot_loc), lambda p: cotfull.at[p], c_s, c_r)
    f_ex = exchange(n_tp, t, tp_dev, lambda p: feat_out.at[p], lambda p: feat_in.at[p], f_s, f_r)
    r_ex = exchange(n_tp, t, tp_dev, whole(rs_out), lambda p: rs_in.at[p], r_s, r_r)
    h1_ex = exchange(n_z, z, z_dev, lambda p: xfull.at[p, my_rows], lambda p: hid_p.at[p], h1_s, h1_r)
    h2_ex = exchange(n_tp, t, tp_dev, whole(hid_p), lambda p: hid_z.at[:, p], h2_s, h2_r)
    c1_ex = exchange(n_z, z, z_dev, lambda p: cotfull.at[p, my_rows], lambda p: cot_p.at[p], c1_s, c1_r)
    c2_ex = exchange(n_tp, t, tp_dev, whole(cot_p), lambda p: cot_z.at[:, p], c2_s, c2_r)
    att_ring = ring(att_z, az_s, az_r)
    gq_ring = ring(gq_z, qz_s, qz_r)
    kz_ex = exchange(n_z, z, z_dev, whole(gkv_n), lambda p: gkv_z.at[pl.ds(p * BLOCK, BLOCK)], kz_s, kz_r)
    own_z = pl.ds(pl.multiple_of(z * BLOCK, BLOCK), BLOCK)
    wq_copy = pltpu.make_async_copy(wq_hbm, wq, w_sem.at[0])
    wo_copy = pltpu.make_async_copy(wo_hbm, wo, w_sem.at[1])

    wq_copy.start()
    wo_copy.start()
    kv[...] = jnp.zeros_like(kv)

    barrier = pltpu.get_barrier_semaphore()

    @pl.loop(1, n_tp)
    def _(i):
        pl.semaphore_signal(barrier, inc=1, device_id={"tp": lax.rem(t + i, n_tp)}, device_id_type=MESH)

    @pl.loop(1, n_ctx)
    def _(i):
        pl.semaphore_signal(barrier, inc=1, device_id={"ctx": lax.rem(c + i, n_ctx)}, device_id_type=MESH)

    @pl.loop(0, n_tp)
    def _(p):
        pl.semaphore_signal(barrier, inc=1, device_id={"section": 1 - s, "tp": p}, device_id_type=MESH)

    pl.semaphore_wait(barrier, 2 * n_tp + n_ctx - 2)

    @pl.when(s == 0)
    def _():
        pl.semaphore_wait(gate, 1)

    x_ex[0]()
    xfull[t] = x_ref[...]

    x_ex[1]()

    @pl.when(s == 1)
    def _():
        weights = jnp.broadcast_to(tw_ref[...].astype(F32), (BLOCK, BLOCK)).T[:, :1]
        cot_loc[...] = (loss_ref[...].astype(F32) * weights).astype(BF16)
        cotfull[t] = cot_loc[...]
        c_ex[0]()

    square = jnp.zeros((BLOCK, part), F32)
    for p in range(n_tp):
        wide = xfull[p].astype(F32)
        square = square + wide * wide
    inv = lax.rsqrt(jnp.sum(square, axis=1, keepdims=True) / width + EPSILON)
    inv_b[...] = jnp.broadcast_to(inv, inv_b.shape)
    for p in range(n_tp):
        gain = gain_ref[:, p * part : (p + 1) * part]
        xfull[p] = ((xfull[p].astype(F32) * inv) * gain).astype(BF16)

    def project(full, weight, lo_col, n_col):
        total = jnp.zeros((BLOCK, n_col), F32)
        for p in range(n_tp):
            total = total + mm(full[p], weight[p * part : (p + 1) * part, lo_col : lo_col + n_col])
        return total.astype(BF16)

    def slot(j):
        if isinstance(j, int):
            return pl.ds(j * BLOCK, BLOCK)
        return pl.ds(pl.multiple_of(j * BLOCK, BLOCK), BLOCK)

    wq_copy.wait()
    kv[slot(last)] = project(xfull, wq, heads, 2 * HEAD_SIZE)

    steps_z = (window - 1) // 2 + 1
    mate = {"ctx": z * 2 + 1 - lo}
    far = window - 1

    def kv_up(k):
        return remote(
            kv.at[slot(last)], kv.at[slot(last - 2 * k)], kv_s.at[2 * k], kv_r.at[2 * k],
            {"ctx": lax.rem(c + 2 * k, n_ctx)},
        )

    def kv_on(k):
        away = 2 * k + 1 - 2 * lo
        return remote(
            kv.at[slot(last - 2 * k)], kv.at[slot(last - away)], kv_s.at[2 * k + 1], kv_r.at[away], mate
        )

    def kv_far():
        return remote(
            kv.at[slot(last)], kv.at[slot(last - far)], kv_f.at[0], kv_r.at[far],
            {"ctx": lax.rem(c + far, n_ctx)},
        )

    def kv_arrival(d):
        return remote(
            kv.at[slot(last - d)], kv.at[slot(last - d)], kv_s.at[0], kv_r.at[d], mate
        )

    @pl.loop(1, steps_z)
    def _(i):
        k = steps_z - i

        @pl.when(z + k < n_z)
        def _():
            kv_up(k).start()

    @pl.when((lo == 1) & (c + far < n_ctx))
    def _():
        kv_far().start()

    @pl.when(lo == 0)
    def _():
        kv_on(0).start()

    @pl.when(s == 1)
    def _():
        pl.semaphore_signal(gate, inc=1, device_id={"section": 1 - s}, device_id_type=MESH)

    for j in range(0, GROUP_HEADS, 2):
        pair = project(xfull, wq, j * HEAD_SIZE, 2 * HEAD_SIZE)
        q_s[j * BLOCK : (j + 1) * BLOCK] = pair[:, :HEAD_SIZE]
        q_s[(j + 1) * BLOCK : (j + 2) * BLOCK] = pair[:, HEAD_SIZE:]
    h1_ex[0]()
    hid_p[z] = xfull[z, my_rows]

    def pass_hidden():
        h1_ex[1]()
        h2_ex[0]()
        hid_z[:, t] = hid_p[...]

    def head_cotangent():
        wo_copy.wait()
        for j in range(0, GROUP_HEADS, 2):
            pair = project(cotfull, wo, j * HEAD_SIZE, 2 * HEAD_SIZE)
            hc_s[j * BLOCK : (j + 1) * BLOCK] = pair[:, :HEAD_SIZE]
            hc_s[(j + 1) * BLOCK : (j + 2) * BLOCK] = pair[:, HEAD_SIZE:]

    @pl.loop(1, steps_z)
    def _(k):
        @pl.when(z - k >= 0)
        def _():
            kv_up(k).wait_recv()
            kv_on(k).start()

    @pl.when(s == 0)
    def _():
        pass_hidden()

    @pl.when(s == 1)
    def _():
        c_ex[1]()
        head_cotangent()

    doc_start = jnp.int32(0)
    doc_end = jnp.int32(0)
    for i in range(docs_ref.shape[1]):
        doc_end = doc_end + docs_ref[0, i]
        doc_start = jnp.where(doc_end <= c, doc_end, doc_start)
    pairs = window // 2
    wide = (GROUP_HEADS * BLOCK, 2 * BLOCK)
    query_pos = c * BLOCK + lax.broadcasted_iota(jnp.int32, wide, 0) % BLOCK
    first_key = (c - last) * BLOCK + lax.broadcasted_iota(jnp.int32, wide, 1)

    def keys(g):
        return kv[g * 2 * BLOCK : (g + 1) * 2 * BLOCK, :HEAD_SIZE]

    def values(g):
        return kv[g * 2 * BLOCK : (g + 1) * 2 * BLOCK, HEAD_SIZE:]

    for g in range(pairs - 1, -1, -1):
        for j in (2 * g + 1, 2 * g):
            if j < last:

                if (last - j) % 2 == 1:

                    @pl.when(c - last + j >= 0)
                    def _():
                        kv_arrival(last - j).wait_recv()

        block = mm(q_s[...], keys(g), NT) * scale
        key_pos = first_key + g * 2 * BLOCK
        block = jnp.where((key_pos <= query_pos) & (key_pos >= doc_start * BLOCK), block, NEG_FILL)
        scores[g] = block
        both = jnp.maximum(block[:, :BLOCK], block[:, BLOCK:])
        peak[...] = both if g == pairs - 1 else jnp.maximum(peak[...], both)

    top = jnp.max(peak[...], axis=1, keepdims=True)
    for g in range(pairs):
        e = jnp.exp(scores[g] - top)
        scores[g] = e
        both = e[:, :BLOCK] + e[:, BLOCK:]
        denom[...] = both if g == 0 else denom[...] + both

    inverse = 1.0 / jnp.sum(denom[...], axis=1, keepdims=True)
    for g in range(pairs):
        soft = scores[g] * inverse
        low = soft.astype(BF16)
        scores[g] = soft
        probs[g] = low
        term = mm(low, values(g))
        acc[...] = term if g == 0 else acc[...] + term

    att_s[...] = acc[...].astype(BF16)
    for j in range(GROUP_HEADS):
        att_z[own_z, j * HEAD_SIZE : (j + 1) * HEAD_SIZE] = att_s[j * BLOCK : (j + 1) * BLOCK]

    def sec_copy(p):
        return remote(gin_ref, cotfull.at[t], sec_s.at[p], c_r.at[t], {"section": 1 - s, "tp": p})

    @pl.when(s == 1)
    def _():
        pass_hidden()

    @pl.when(s == 0)
    def _():
        for k in range(1, min(3, n_z // 2) + 1):
            att_ring[0](k)

        @pl.loop(0, n_tp)
        def _(p):
            remote(cotfull.at[p], cotfull.at[p], sec_s.at[p], c_r.at[p], {"section": 1 - s}).wait_recv()

        head_cotangent()
        att_ring[0](4)

    delta = jnp.sum(hc_s[...].astype(F32) * att_s[...].astype(F32), axis=1, keepdims=True)

    def dkv_copy(d):
        return remote(
            dkv_part.at[slot(last - d)], dkv_in.at[d], d_s.at[d], d_r.at[d],
            {"ctx": lax.rem(c - d + n_ctx, n_ctx)},
        )

    for g in range(pairs):
        block = slice(g * 2 * BLOCK, (g + 1) * 2 * BLOCK)
        dprobs = mm(hc_s[...], values(g), NT)
        ds = (scores[g] * (dprobs - delta)).astype(BF16)
        dkv_part[block, :HEAD_SIZE] = (mm(ds, q_s[...], TN) * scale).astype(BF16)
        dkv_part[block, HEAD_SIZE:] = mm(probs[g], hc_s[...], TN).astype(BF16)
        dscores[g] = ds
        for j in (2 * g, 2 * g + 1):
            if j < last:

                @pl.when(c - last + j >= 0)
                def _():
                    dkv_copy(last - j).start()

    total = mm(dscores[0], keys(0))
    for g in range(1, pairs):
        total = total + mm(dscores[g], keys(g))
    acc[...] = total
    for j in range(GROUP_HEADS):
        gq_n[:, j * HEAD_SIZE : (j + 1) * HEAD_SIZE] = (
            acc[j * BLOCK : (j + 1) * BLOCK] * scale
        ).astype(BF16)
    gq_z[own_z] = gq_n[...]

    def send_cot():
        c1_ex[0]()
        cot_p[z] = cotfull[z, my_rows]

    def pass_cot():
        c1_ex[1]()
        c2_ex[0]()
        cot_z[:, t] = cot_p[...]

    @pl.when(s == 0)
    def _():
        send_cot()
        gq_ring[0](1)

    @pl.loop(0, n_tp)
    def _(p):
        feat_f[p] = mm(gq_n[...], wq[pl.ds(p * part, part), :heads], NT)

    @pl.when(s == 0)
    def _():
        pass_cot()
        gq_ring[0](2)

    acc[:BLOCK] = dkv_part[slot(last), :HEAD_SIZE].astype(F32)
    acc[BLOCK : 2 * BLOCK] = dkv_part[slot(last), HEAD_SIZE:].astype(F32)

    @pl.loop(1, window)
    def _(d):
        @pl.when(c + d < n_ctx)
        def _():
            dkv_copy(d).wait_recv()
            acc[:BLOCK] += dkv_in[d, :, :HEAD_SIZE].astype(F32)
            acc[BLOCK : 2 * BLOCK] += dkv_in[d, :, HEAD_SIZE:].astype(F32)

    gkv_n[:, :HEAD_SIZE] = acc[:BLOCK].astype(BF16)
    gkv_n[:, HEAD_SIZE:] = acc[BLOCK : 2 * BLOCK].astype(BF16)
    gkv_z[own_z] = gkv_n[...]
    kz_ex[0]()

    row_sum = gkv_n[:, :HEAD_SIZE].astype(F32) * kv[slot(last), :HEAD_SIZE].astype(F32)
    row_sum = row_sum + gkv_n[:, HEAD_SIZE:].astype(F32) * kv[slot(last), HEAD_SIZE:].astype(F32)
    for j in range(GROUP_HEADS):
        row_sum = row_sum + gq_n[:, j * HEAD_SIZE : (j + 1) * HEAD_SIZE].astype(F32) * q_s[
            j * BLOCK : (j + 1) * BLOCK
        ].astype(F32)
    row_sum = jnp.sum(row_sum, axis=1, keepdims=True)
    rs_out[...] = jnp.broadcast_to(row_sum, (BLOCK, BLOCK)).T[:8]
    r_ex[0]()
    rs_in[t] = rs_out[...]

    @pl.loop(1, n_tp + 1)
    def _(i):
        p = lax.rem(t + i, n_tp)
        total = feat_f[p] + mm(gkv_n[...], wq[pl.ds(p * part, part), heads:], NT)
        feat_out[p] = total.astype(BF16)

        @pl.when(i < n_tp)
        def _():
            f_ex[3](p).start()

    feat_in[t] = feat_out[t]

    y_copies = [
        remote(y_out_o, y_in_o, y_s.at[0], y_r.at[0], mate),
        remote(y_out_q, y_in_q, y_s.at[1], y_r.at[1], mate),
        remote(y_out_k, y_in_k, y_s.at[2], y_r.at[2], mate),
    ]
    positions = n_z * BLOCK
    theirs = pl.ds(pl.multiple_of((1 - lo) * half, half), half)
    mine = pl.ds(pl.multiple_of(lo * half, half), half)

    def turn(ref):
        turned[...] = ref[...].reshape(positions, part).T

    def weight_part(right, y_out, out, base, copy):
        step = min(256, heads)
        for k in range(0, right.shape[1], step):
            y_out[:, k : k + step] = mm(turned[theirs], right[:, k : k + step]).astype(BF16)
        copy.start()
        for k in range(0, right.shape[1], step):
            out[:, base + k : base + k + step] = mm(turned[mine], right[:, k : k + step])

    def grad_of_out():
        c2_ex[1]()
        att_ring[1]()
        turn(cot_z)
        weight_part(att_z, y_out_o, gout_ref, 0, y_copies[0])

    def grad_of_query():
        h2_ex[1]()
        turn(hid_z)
        gq_ring[1]()
        weight_part(gq_z, y_out_q, gqkv_ref, 0, y_copies[1])

    @pl.when(s == 0)
    def _():
        gq_ring[0](3)
        grad_of_out()
        gq_ring[0](4)
        grad_of_query()

    f_ex[1]()
    r_ex[1]()
    feature = jnp.zeros((BLOCK, part), F32)
    for p in range(n_tp):
        feature = feature + feat_in[p].astype(F32)
    inv = inv_b[:, :1]
    gain = gain_ref[:, pl.ds(pl.multiple_of(t * part, part), part)]
    scaled = feature * gain
    normed = x_ref[...].astype(F32) * inv
    total = rs_in[0]
    for p in range(1, n_tp):
        total = total + rs_in[p]
    mean = jnp.broadcast_to(total[:1] / width, (BLOCK, BLOCK)).T[:, :1]
    gin_ref[...] = (cotfull[t].astype(F32) + inv * (scaled - normed * mean)).astype(BF16)

    @pl.when(s == 1)
    def _():
        @pl.loop(0, n_tp)
        def _(i):
            sec_copy(lax.rem(t + i, n_tp)).start()

        send_cot()
        for k in range(1, n_z // 2 + 1):
            att_ring[0](k)
            gq_ring[0](k)
            if k == 2 or n_z == 2:
                pass_cot()
        grad_of_out()
        grad_of_query()

    kz_ex[1]()
    weight_part(gkv_z, y_out_k, gqkv_ref, heads, y_copies[2])
    for y_in, out, base, copy in (
        (y_in_o, gout_ref, 0, y_copies[0]),
        (y_in_q, gqkv_ref, 0, y_copies[1]),
        (y_in_k, gqkv_ref, heads, y_copies[2]),
    ):
        copy.wait_recv()
        out[:, base : base + y_in.shape[1]] += y_in[...].astype(F32)

    for ex in (x_ex, f_ex, r_ex, h1_ex, h2_ex, c1_ex, c2_ex, kz_ex, att_ring, gq_ring):
        ex[2]()
    for copy in y_copies:
        copy.wait_send()

    @pl.loop(1, steps_z)
    def _(k):
        @pl.when(z + k < n_z)
        def _():
            kv_up(k).wait_send()

        @pl.when(z - k >= 0)
        def _():
            kv_on(k).wait_send()

    @pl.when((lo == 1) & (c + far < n_ctx))
    def _():
        kv_far().wait_send()

    @pl.when(lo == 0)
    def _():
        kv_on(0).wait_send()

    @pl.loop(1, window)
    def _(d):
        @pl.when(c - d >= 0)
        def _():
            dkv_copy(d).wait_send()

    @pl.when(s == 1)
    def _():
        c_ex[2]()

        @pl.loop(0, n_tp)
        def _(p):
            sec_copy(p).wait_send()


def settle(a_in, b_in, c_in, a_out, b_out, c_out, sem):
    copies = [
        pltpu.make_async_copy(source, target, sem.at[i])
        for i, (source, target) in enumerate(((a_in, a_out), (b_in, b_out), (c_in, c_out)))
    ]
    for copy in copies:
        copy.start()
    for copy in copies:
        copy.wait()


def body(layer_input, loss_cot, token_weights, doc_blocks, norm_gain, qkv_weight, out_weight):
    n_ctx, n_tp = lax.axis_size("ctx"), lax.axis_size("tp")
    n_z = n_ctx // 2
    part = layer_input.shape[3]
    width = part * n_tp
    cols, heads = qkv_weight.shape[2], out_weight.shape[2]
    window = min(MAX_DOC, n_ctx)
    q_rows = GROUP_HEADS * BLOCK
    kv_cols = 2 * HEAD_SIZE
    half = part // 2
    share = BLOCK // n_tp
    vmem = lambda shape, dtype=BF16: pltpu.VMEM(shape, dtype)
    dma = lambda *n: pltpu.SemaphoreType.DMA(n)
    scratch = [
        vmem((width, cols)), vmem((width, heads)),
        vmem((n_tp, BLOCK, part)), vmem((n_tp, BLOCK, part)), vmem((BLOCK, part)), vmem((BLOCK, BLOCK), F32),
        vmem((window * BLOCK, kv_cols)),
        vmem((q_rows, HEAD_SIZE)), vmem((q_rows, HEAD_SIZE)), vmem((q_rows, HEAD_SIZE)),
        vmem((BLOCK, heads)), vmem((BLOCK, kv_cols)),
        vmem((window // 2, q_rows, 2 * BLOCK), F32), vmem((window // 2, q_rows, 2 * BLOCK)),
        vmem((window // 2, q_rows, 2 * BLOCK)),
        vmem((q_rows, BLOCK), F32), vmem((q_rows, BLOCK), F32), vmem((q_rows, HEAD_SIZE), F32),
        vmem((window * BLOCK, kv_cols)), vmem((window, BLOCK, kv_cols)),
        vmem((n_tp, BLOCK, part), F32), vmem((n_tp, BLOCK, part)), vmem((n_tp, BLOCK, part)),
        vmem((8, BLOCK), F32), vmem((n_tp, 8, BLOCK), F32),
        vmem((n_z, share, part)), vmem((n_z, share, part)),
        vmem((n_z, n_tp, share, part)), vmem((n_z, n_tp, share, part)), vmem((n_z * BLOCK, heads)),
        vmem((n_z * BLOCK, heads)), vmem((n_z * BLOCK, kv_cols)), vmem((part, n_z * BLOCK)),
        vmem((half, heads)), vmem((half, heads)), vmem((half, kv_cols)),
        vmem((half, heads)), vmem((half, heads)), vmem((half, kv_cols)),
        dma(2), dma(n_tp), dma(n_tp), dma(n_tp), dma(n_tp), dma(window), dma(window), dma(1), dma(window), dma(window),
        dma(n_tp), dma(n_tp), dma(n_tp), dma(n_tp),
        dma(n_z), dma(n_z), dma(n_tp), dma(n_tp), dma(n_z), dma(n_z), dma(n_tp), dma(n_tp),
        dma(n_z), dma(n_z), dma(n_z), dma(n_z), dma(n_z), dma(n_z),
        dma(3), dma(3), dma(n_tp), pltpu.SemaphoreType.REGULAR,
    ]
    in_vmem = pl.BlockSpec(memory_space=pltpu.VMEM)
    anywhere = pl.BlockSpec(memory_space=pl.ANY)
    grad_in, grad_qkv, grad_out = pl.pallas_call(
        functools.partial(kernel, n_ctx, n_tp, window),
        out_shape=(
            jax.ShapeDtypeStruct((BLOCK, part), BF16),
            jax.ShapeDtypeStruct((half, cols), F32),
            jax.ShapeDtypeStruct((half, heads), F32),
        ),
        in_specs=[
            in_vmem, in_vmem, in_vmem, pl.BlockSpec(memory_space=pltpu.SMEM), in_vmem, anywhere, anywhere,
        ],
        out_specs=(in_vmem, in_vmem, in_vmem),
        scratch_shapes=scratch,
        compiler_params=pltpu.CompilerParams(
            collective_id=0, has_side_effects=True, vmem_limit_bytes=56 * 1024 * 1024
        ),
    )(
        layer_input[0, 0], loss_cot[0], token_weights, doc_blocks, norm_gain, qkv_weight[0], out_weight[0]
    )
    results = (grad_in, grad_qkv, grad_out)
    grad_in, grad_qkv, grad_out = pl.pallas_call(
        settle,
        out_shape=tuple(jax.ShapeDtypeStruct(r.shape, r.dtype) for r in results),
        in_specs=[in_vmem] * 3,
        out_specs=(anywhere,) * 3,
        scratch_shapes=[dma(3)],
    )(*results)
    return grad_in[None, None], grad_qkv[None], grad_out[None]


def solution(mesh):
    placed = (
        P("section", None, "ctx", "tp"),
        P(None, "ctx", "tp"),
        P(None, "ctx"),
        P(),
        P("section", None),
        P("section", None, "tp"),
        P("section", None, "tp"),
    )
    return jax.shard_map(
        body,
        mesh=mesh,
        in_specs=placed,
        out_specs=(
            P("section", None, "ctx", "tp"),
            P("section", "ctx", "tp"),
            P("section", "ctx", "tp"),
        ),
        check_vma=False,
    )
```

```python
import functools

import jax
import jax.numpy as jnp
from jax import lax
from jax.experimental import pallas as pl
from jax.experimental.pallas import tpu as pltpu
from jax.sharding import PartitionSpec as P

MESH = pl.DeviceIdType.MESH
GROUP_HEADS = 4
HEAD_SIZE = 128
BLOCK = 128
MAX_DOC = 10
EPSILON = 1e-05
NEG_FILL = -1e30
F32 = jnp.float32
BF16 = jnp.bfloat16

NN = (((1,), (0,)), ((), ()))
NT = (((1,), (1,)), ((), ()))
TN = (((0,), (0,)), ((), ()))


def mm(a, b, dims=NN):
    return lax.dot_general(a, b, dims, preferred_element_type=F32)


def kernel(
    n_ctx, n_tp, window,
    x_ref, loss_ref, tw_ref, docs_ref, gain_ref, wq_hbm, wo_hbm,
    gin_ref, gqkv_ref, gout_ref,
    wq, wo, xfull, cotfull, cot_loc, inv_b,
    kv, q_s, hc_s, att_s, gq_n, gkv_n, scores, probs, dscores, peak, denom, acc,
    dkv_part, dkv_in, feat_f, feat_out, feat_in, rs_out, rs_in,
    hid_p, cot_p, hid_z, cot_z, att_z, gq_z, gkv_z, turned,
    y_out_o, y_out_q, y_out_k, y_in_o, y_in_q, y_in_k,
    w_sem, x_s, x_r, c_s, c_r, kv_s, kv_r, kv_f, d_s, d_r, f_s, f_r, r_s, r_r,
    h1_s, h1_r, h2_s, h2_r, c1_s, c1_r, c2_s, c2_r, az_s, az_r, qz_s, qz_r, kz_s, kz_r, y_s, y_r, sec_s, gate,
):
    s = lax.axis_index("section")
    c = lax.axis_index("ctx")
    t = lax.axis_index("tp")
    n_z = n_ctx // 2
    z, lo = c // 2, lax.rem(c, 2)
    part = x_ref.shape[1]
    width = part * n_tp
    half = part // 2
    heads = GROUP_HEADS * HEAD_SIZE
    cols = heads + 2 * HEAD_SIZE
    scale = HEAD_SIZE ** (-0.5)
    last = window - 1

    def remote(src, dst, ss, rs, dev):
        return pltpu.make_async_remote_copy(
            src_ref=src, dst_ref=dst, send_sem=ss, recv_sem=rs, device_id=dev, device_id_type=MESH
        )

    def tp_dev(p):
        return {"tp": p}

    def z_dev(p):
        return {"ctx": p * 2 + lo}

    def exchange(n, me, dev, src_of, slot, ss, rs):
        def copy_to(p):
            return remote(src_of(p), slot(me), ss.at[p], rs.at[me], dev(p))

        def copy_from(p):
            return remote(slot(p), slot(p), ss.at[p], rs.at[p], dev(p))

        def start():
            @pl.loop(1, n)
            def _(i):
                copy_to(lax.rem(me + i, n)).start()

        def wait_recv():
            @pl.loop(1, n)
            def _(i):
                copy_from(lax.rem(me + i, n)).wait_recv()

        def wait_send():
            @pl.loop(1, n)
            def _(i):
                copy_to(lax.rem(me + i, n)).wait_send()

        return start, wait_recv, wait_send, copy_to

    def ring(ref, ss, rs):
        up, down = z_dev(lax.rem(z + 1, n_z)), z_dev(lax.rem(z + n_z - 1, n_z))
        top = n_z // 2

        def piece(p, k, side):
            if k < top:
                return ref.at[pl.ds(p * BLOCK, BLOCK)]
            return ref.at[pl.ds(p * BLOCK + side * (BLOCK // 2), BLOCK // 2)]

        def pair(k, shift):
            below = piece(lax.rem(z - k + shift + n_z, n_z), k, 0)
            above = piece(lax.rem(z + k - shift, n_z), k, 1)
            return (
                remote(below, below, ss.at[k - 1], rs.at[k - 1], up),
                remote(above, above, ss.at[top + k - 1], rs.at[top + k - 1], down),
            )

        def arrive(k):
            for copy in pair(k, 0):
                copy.wait_recv()

        def stage(k):
            if k > top:
                return
            if k > 1:
                arrive(k - 1)
            for copy in pair(k, 1):
                copy.start()

        def wait_send():
            for k in range(1, top + 1):
                for copy in pair(k, 1):
                    copy.wait_send()

        return stage, lambda: arrive(top), wait_send

    n_x = n_tp // 2
    ty, tx = t // n_x, lax.rem(t, n_x)

    def at(dy, dx):
        return (ty if dy == 0 else 1 - ty) * n_x + lax.rem(tx + dx + n_x, n_x)

    near = [at(0, -1), at(0, 1)] if n_x > 1 else []
    mate_t = at(1, 0)

    class Spread:
        def __init__(self, piece, ss, rs):
            self.piece, self.ss, self.rs = piece, ss, rs
            self.sends = [self.move(t, None, 0, t, mate_t)]
            if n_x > 1:
                left, right = near
                self.sends += [
                    self.move(t, None, 1, t, right),
                    self.move(t, None, 2, t, left),
                    self.move(left, 0, 3, left, right),
                    self.move(right, 1, 4, n_tp, left),
                    self.move(mate_t, None, 5, mate_t, right),
                    self.move(mate_t, None, 6, mate_t, left),
                    self.move(at(1, -1), 0, 7, at(1, -1), right),
                    self.move(at(1, 1), 1, 8, n_tp + 1, left),
                ]

        def move(self, p, side, i, r, to):
            return remote(self.piece(p, side), self.piece(p, side), self.ss.at[i], self.rs.at[r], {"tp": to})

        def arrive(self, p, side=None, r=None):
            self.move(p, side, 0, p if r is None else r, mate_t).wait_recv()

        def start(self):
            for copy in self.sends[:3]:
                copy.start()

        def relay(self):
            if n_x > 1:
                for p, copy in zip(near, self.sends[3:5]):
                    self.arrive(p)
                    copy.start()
            self.arrive(mate_t)
            for copy in self.sends[5:7]:
                copy.start()

        def relay_far(self):
            for p, copy in zip((at(1, -1), at(1, 1)), self.sends[7:]):
                self.arrive(p)
                copy.start()

        def finish(self):
            if n_x > 1:
                for i, p in enumerate((at(0, 2), at(1, 2))):
                    self.arrive(p, 0)
                    self.arrive(p, 1, n_tp + i)

        def wait_send(self):
            for copy in self.sends:
                copy.wait_send()

        def rest(self):
            if n_x > 1:
                self.relay_far()
            self.finish()

    def slice_of(ref):
        depth = n_z // 2

        def piece(p, side):
            return ref.at[:, p] if side is None else ref.at[pl.ds(side * depth, depth), p]

        return piece

    whole = lambda ref: lambda p: ref
    share = BLOCK // n_tp
    my_rows = pl.ds(pl.multiple_of(t * share, share), share)

    x_ex = exchange(n_tp, t, tp_dev, whole(x_ref), lambda p: xfull.at[p], x_s, x_r)
    c_ex = exchange(n_tp, t, tp_dev, whole(cot_loc), lambda p: cotfull.at[p], c_s, c_r)
    f_ex = exchange(n_tp, t, tp_dev, lambda p: feat_out.at[p], lambda p: feat_in.at[p], f_s, f_r)
    r_ex = exchange(n_tp, t, tp_dev, whole(rs_out), lambda p: rs_in.at[p], r_s, r_r)
    h1_ex = exchange(n_z, z, z_dev, lambda p: xfull.at[p, my_rows], lambda p: hid_p.at[p], h1_s, h1_r)
    h2_ag = Spread(slice_of(hid_z), h2_s, h2_r)
    c1_ex = exchange(n_z, z, z_dev, lambda p: cotfull.at[p, my_rows], lambda p: cot_p.at[p], c1_s, c1_r)
    c2_ag = Spread(slice_of(cot_z), c2_s, c2_r)
    att_ring = ring(att_z, az_s, az_r)
    gq_ring = ring(gq_z, qz_s, qz_r)
    kz_ex = exchange(n_z, z, z_dev, whole(gkv_n), lambda p: gkv_z.at[pl.ds(p * BLOCK, BLOCK)], kz_s, kz_r)
    own_z = pl.ds(pl.multiple_of(z * BLOCK, BLOCK), BLOCK)
    wq_copy = pltpu.make_async_copy(wq_hbm, wq, w_sem.at[0])
    wo_copy = pltpu.make_async_copy(wo_hbm, wo, w_sem.at[1])

    wq_copy.start()
    wo_copy.start()
    kv[...] = jnp.zeros_like(kv)

    barrier = pltpu.get_barrier_semaphore()

    @pl.loop(1, n_tp)
    def _(i):
        pl.semaphore_signal(barrier, inc=1, device_id={"tp": lax.rem(t + i, n_tp)}, device_id_type=MESH)

    @pl.loop(1, n_ctx)
    def _(i):
        pl.semaphore_signal(barrier, inc=1, device_id={"ctx": lax.rem(c + i, n_ctx)}, device_id_type=MESH)

    @pl.loop(0, n_tp)
    def _(p):
        pl.semaphore_signal(barrier, inc=1, device_id={"section": 1 - s, "tp": p}, device_id_type=MESH)

    pl.semaphore_wait(barrier, 2 * n_tp + n_ctx - 2)

    @pl.when(s == 0)
    def _():
        pl.semaphore_wait(gate, 1)

    x_ex[0]()
    xfull[t] = x_ref[...]

    x_ex[1]()

    @pl.when(s == 1)
    def _():
        weights = jnp.broadcast_to(tw_ref[...].astype(F32), (BLOCK, BLOCK)).T[:, :1]
        cot_loc[...] = (loss_ref[...].astype(F32) * weights).astype(BF16)
        cotfull[t] = cot_loc[...]
        c_ex[0]()

    square = jnp.zeros((BLOCK, part), F32)
    for p in range(n_tp):
        wide = xfull[p].astype(F32)
        square = square + wide * wide
    inv = lax.rsqrt(jnp.sum(square, axis=1, keepdims=True) / width + EPSILON)
    inv_b[...] = jnp.broadcast_to(inv, inv_b.shape)
    for p in range(n_tp):
        gain = gain_ref[:, p * part : (p + 1) * part]
        xfull[p] = ((xfull[p].astype(F32) * inv) * gain).astype(BF16)

    def project(full, weight, lo_col, n_col):
        total = jnp.zeros((BLOCK, n_col), F32)
        for p in range(n_tp):
            total = total + mm(full[p], weight[p * part : (p + 1) * part, lo_col : lo_col + n_col])
        return total.astype(BF16)

    def slot(j):
        if isinstance(j, int):
            return pl.ds(j * BLOCK, BLOCK)
        return pl.ds(pl.multiple_of(j * BLOCK, BLOCK), BLOCK)

    wq_copy.wait()
    kv[slot(last)] = project(xfull, wq, heads, 2 * HEAD_SIZE)

    steps_z = (window - 1) // 2 + 1
    mate = {"ctx": z * 2 + 1 - lo}
    far = window - 1

    def kv_up(k):
        return remote(
            kv.at[slot(last)], kv.at[slot(last - 2 * k)], kv_s.at[2 * k], kv_r.at[2 * k],
            {"ctx": lax.rem(c + 2 * k, n_ctx)},
        )

    def kv_on(k):
        away = 2 * k + 1 - 2 * lo
        return remote(
            kv.at[slot(last - 2 * k)], kv.at[slot(last - away)], kv_s.at[2 * k + 1], kv_r.at[away], mate
        )

    def kv_far():
        return remote(
            kv.at[slot(last)], kv.at[slot(last - far)], kv_f.at[0], kv_r.at[far],
            {"ctx": lax.rem(c + far, n_ctx)},
        )

    def kv_arrival(d):
        return remote(
            kv.at[slot(last - d)], kv.at[slot(last - d)], kv_s.at[0], kv_r.at[d], mate
        )

    @pl.loop(1, steps_z)
    def _(i):
        k = steps_z - i

        @pl.when(z + k < n_z)
        def _():
            kv_up(k).start()

    @pl.when((lo == 1) & (c + far < n_ctx))
    def _():
        kv_far().start()

    @pl.when(lo == 0)
    def _():
        kv_on(0).start()


    for j in range(0, GROUP_HEADS, 2):
        pair = project(xfull, wq, j * HEAD_SIZE, 2 * HEAD_SIZE)
        q_s[j * BLOCK : (j + 1) * BLOCK] = pair[:, :HEAD_SIZE]
        q_s[(j + 1) * BLOCK : (j + 2) * BLOCK] = pair[:, HEAD_SIZE:]
    h1_ex[0]()
    hid_p[z] = xfull[z, my_rows]

    def pass_hidden():
        h1_ex[1]()
        hid_z[:, t] = hid_p[...]
        h2_ag.start()

    def head_cotangent():
        wo_copy.wait()
        for j in range(0, GROUP_HEADS, 2):
            pair = project(cotfull, wo, j * HEAD_SIZE, 2 * HEAD_SIZE)
            hc_s[j * BLOCK : (j + 1) * BLOCK] = pair[:, :HEAD_SIZE]
            hc_s[(j + 1) * BLOCK : (j + 2) * BLOCK] = pair[:, HEAD_SIZE:]

    @pl.loop(1, steps_z)
    def _(k):
        @pl.when(z - k >= 0)
        def _():
            kv_up(k).wait_recv()
            kv_on(k).start()

    @pl.when(s == 0)
    def _():
        pass_hidden()

    @pl.when(s == 1)
    def _():
        c_ex[1]()
        pl.semaphore_signal(gate, inc=1, device_id={"section": 1 - s}, device_id_type=MESH)
        head_cotangent()

    doc_start = jnp.int32(0)
    doc_end = jnp.int32(0)
    for i in range(docs_ref.shape[1]):
        doc_end = doc_end + docs_ref[0, i]
        doc_start = jnp.where(doc_end <= c, doc_end, doc_start)
    pairs = window // 2
    wide = (GROUP_HEADS * BLOCK, 2 * BLOCK)
    query_pos = c * BLOCK + lax.broadcasted_iota(jnp.int32, wide, 0) % BLOCK
    first_key = (c - last) * BLOCK + lax.broadcasted_iota(jnp.int32, wide, 1)

    def keys(g):
        return kv[g * 2 * BLOCK : (g + 1) * 2 * BLOCK, :HEAD_SIZE]

    def values(g):
        return kv[g * 2 * BLOCK : (g + 1) * 2 * BLOCK, HEAD_SIZE:]

    for g in range(pairs - 1, -1, -1):
        for j in (2 * g + 1, 2 * g):
            if j < last:

                if (last - j) % 2 == 1:

                    @pl.when(c - last + j >= 0)
                    def _():
                        kv_arrival(last - j).wait_recv()

        block = mm(q_s[...], keys(g), NT) * scale
        key_pos = first_key + g * 2 * BLOCK
        block = jnp.where((key_pos <= query_pos) & (key_pos >= doc_start * BLOCK), block, NEG_FILL)
        scores[g] = block
        both = jnp.maximum(block[:, :BLOCK], block[:, BLOCK:])
        peak[...] = both if g == pairs - 1 else jnp.maximum(peak[...], both)

    top = jnp.max(peak[...], axis=1, keepdims=True)
    for g in range(pairs):
        e = jnp.exp(scores[g] - top)
        scores[g] = e
        both = e[:, :BLOCK] + e[:, BLOCK:]
        denom[...] = both if g == 0 else denom[...] + both

    inverse = 1.0 / jnp.sum(denom[...], axis=1, keepdims=True)
    for g in range(pairs):
        soft = scores[g] * inverse
        low = soft.astype(BF16)
        scores[g] = soft
        probs[g] = low
        term = mm(low, values(g))
        acc[...] = term if g == 0 else acc[...] + term

    att_s[...] = acc[...].astype(BF16)
    for j in range(GROUP_HEADS):
        att_z[own_z, j * HEAD_SIZE : (j + 1) * HEAD_SIZE] = att_s[j * BLOCK : (j + 1) * BLOCK]

    def sec_copy(p):
        return remote(gin_ref, cotfull.at[t], sec_s.at[p], c_r.at[t], {"section": 1 - s, "tp": p})

    @pl.when(s == 1)
    def _():
        pass_hidden()

    @pl.when(s == 0)
    def _():
        h2_ag.relay()
        att_ring[0](1)
        h2_ag.rest()

        @pl.loop(0, n_tp)
        def _(p):
            remote(cotfull.at[p], cotfull.at[p], sec_s.at[p], c_r.at[p], {"section": 1 - s}).wait_recv()

        head_cotangent()
        att_ring[0](2)

    delta = jnp.sum(hc_s[...].astype(F32) * att_s[...].astype(F32), axis=1, keepdims=True)

    def dkv_copy(d):
        return remote(
            dkv_part.at[slot(last - d)], dkv_in.at[d], d_s.at[d], d_r.at[d],
            {"ctx": lax.rem(c - d + n_ctx, n_ctx)},
        )

    for g in range(pairs):
        block = slice(g * 2 * BLOCK, (g + 1) * 2 * BLOCK)
        dprobs = mm(hc_s[...], values(g), NT)
        ds = (scores[g] * (dprobs - delta)).astype(BF16)
        dkv_part[block, :HEAD_SIZE] = (mm(ds, q_s[...], TN) * scale).astype(BF16)
        dkv_part[block, HEAD_SIZE:] = mm(probs[g], hc_s[...], TN).astype(BF16)
        dscores[g] = ds
        for j in (2 * g, 2 * g + 1):
            if j < last:

                @pl.when(c - last + j >= 0)
                def _():
                    dkv_copy(last - j).start()

    total = mm(dscores[0], keys(0))
    for g in range(1, pairs):
        total = total + mm(dscores[g], keys(g))
    acc[...] = total
    for j in range(GROUP_HEADS):
        gq_n[:, j * HEAD_SIZE : (j + 1) * HEAD_SIZE] = (
            acc[j * BLOCK : (j + 1) * BLOCK] * scale
        ).astype(BF16)
    gq_z[own_z] = gq_n[...]

    def send_cot():
        c1_ex[0]()
        cot_p[z] = cotfull[z, my_rows]

    def pass_cot():
        c1_ex[1]()
        cot_z[:, t] = cot_p[...]
        c2_ag.start()

    @pl.when(s == 0)
    def _():
        send_cot()
        gq_ring[0](1)
        att_ring[0](3)

    @pl.when(s == 1)
    def _():
        h2_ag.relay()

    @pl.loop(0, n_tp)
    def _(p):
        feat_f[p] = mm(gq_n[...], wq[pl.ds(p * part, part), :heads], NT)

    @pl.when(s == 0)
    def _():
        pass_cot()
        gq_ring[0](2)
        att_ring[0](4)
        c2_ag.relay()
        c2_ag.rest()

    acc[:BLOCK] = dkv_part[slot(last), :HEAD_SIZE].astype(F32)
    acc[BLOCK : 2 * BLOCK] = dkv_part[slot(last), HEAD_SIZE:].astype(F32)

    @pl.loop(1, window)
    def _(d):
        @pl.when(c + d < n_ctx)
        def _():
            dkv_copy(d).wait_recv()
            acc[:BLOCK] += dkv_in[d, :, :HEAD_SIZE].astype(F32)
            acc[BLOCK : 2 * BLOCK] += dkv_in[d, :, HEAD_SIZE:].astype(F32)

    gkv_n[:, :HEAD_SIZE] = acc[:BLOCK].astype(BF16)
    gkv_n[:, HEAD_SIZE:] = acc[BLOCK : 2 * BLOCK].astype(BF16)
    gkv_z[own_z] = gkv_n[...]
    kz_ex[0]()

    row_sum = gkv_n[:, :HEAD_SIZE].astype(F32) * kv[slot(last), :HEAD_SIZE].astype(F32)
    row_sum = row_sum + gkv_n[:, HEAD_SIZE:].astype(F32) * kv[slot(last), HEAD_SIZE:].astype(F32)
    for j in range(GROUP_HEADS):
        row_sum = row_sum + gq_n[:, j * HEAD_SIZE : (j + 1) * HEAD_SIZE].astype(F32) * q_s[
            j * BLOCK : (j + 1) * BLOCK
        ].astype(F32)
    row_sum = jnp.sum(row_sum, axis=1, keepdims=True)
    rs_out[...] = jnp.broadcast_to(row_sum, (BLOCK, BLOCK)).T[:8]
    r_ex[0]()
    rs_in[t] = rs_out[...]

    @pl.loop(1, n_tp + 1)
    def _(i):
        p = lax.rem(t + i, n_tp)
        total = feat_f[p] + mm(gkv_n[...], wq[pl.ds(p * part, part), heads:], NT)
        feat_out[p] = total.astype(BF16)

        @pl.when(i < n_tp)
        def _():
            f_ex[3](p).start()

    feat_in[t] = feat_out[t]

    y_copies = [
        remote(y_out_o, y_in_o, y_s.at[0], y_r.at[0], mate),
        remote(y_out_q, y_in_q, y_s.at[1], y_r.at[1], mate),
        remote(y_out_k, y_in_k, y_s.at[2], y_r.at[2], mate),
    ]
    positions = n_z * BLOCK
    theirs = pl.ds(pl.multiple_of((1 - lo) * half, half), half)
    mine = pl.ds(pl.multiple_of(lo * half, half), half)

    def turn(ref):
        turned[...] = ref[...].reshape(positions, part).T

    def weight_part(right, y_out, out, base, copy):
        step = min(256, heads)
        for k in range(0, right.shape[1], step):
            y_out[:, k : k + step] = mm(turned[theirs], right[:, k : k + step]).astype(BF16)
        copy.start()
        for k in range(0, right.shape[1], step):
            out[:, base + k : base + k + step] = mm(turned[mine], right[:, k : k + step])

    def grad_of_out():
        att_ring[1]()
        turn(cot_z)
        weight_part(att_z, y_out_o, gout_ref, 0, y_copies[0])

    def grad_of_query():
        turn(hid_z)
        gq_ring[1]()
        weight_part(gq_z, y_out_q, gqkv_ref, 0, y_copies[1])

    @pl.when(s == 0)
    def _():
        gq_ring[0](3)
        grad_of_out()
        gq_ring[0](4)
        grad_of_query()

    f_ex[1]()
    r_ex[1]()
    feature = jnp.zeros((BLOCK, part), F32)
    for p in range(n_tp):
        feature = feature + feat_in[p].astype(F32)
    inv = inv_b[:, :1]
    gain = gain_ref[:, pl.ds(pl.multiple_of(t * part, part), part)]
    scaled = feature * gain
    normed = x_ref[...].astype(F32) * inv
    total = rs_in[0]
    for p in range(1, n_tp):
        total = total + rs_in[p]
    mean = jnp.broadcast_to(total[:1] / width, (BLOCK, BLOCK)).T[:, :1]
    gin_ref[...] = (cotfull[t].astype(F32) + inv * (scaled - normed * mean)).astype(BF16)

    @pl.when(s == 1)
    def _():
        @pl.loop(0, n_tp)
        def _(i):
            sec_copy(lax.rem(t + i, n_tp)).start()

        send_cot()
        for k in (1, 2):
            att_ring[0](k)
            gq_ring[0](k)
        h2_ag.rest()
        pass_cot()
        att_ring[0](3)
        gq_ring[0](3)
        c2_ag.relay()
        att_ring[0](4)
        gq_ring[0](4)
        c2_ag.rest()
        grad_of_out()
        grad_of_query()

    kz_ex[1]()
    weight_part(gkv_z, y_out_k, gqkv_ref, heads, y_copies[2])
    for y_in, out, base, copy in (
        (y_in_o, gout_ref, 0, y_copies[0]),
        (y_in_q, gqkv_ref, 0, y_copies[1]),
        (y_in_k, gqkv_ref, heads, y_copies[2]),
    ):
        copy.wait_recv()
        out[:, base : base + y_in.shape[1]] += y_in[...].astype(F32)

    for ex in (x_ex, f_ex, r_ex, h1_ex, c1_ex, kz_ex, att_ring, gq_ring):
        ex[2]()
    for ag in (h2_ag, c2_ag):
        ag.wait_send()
    for copy in y_copies:
        copy.wait_send()

    @pl.loop(1, steps_z)
    def _(k):
        @pl.when(z + k < n_z)
        def _():
            kv_up(k).wait_send()

        @pl.when(z - k >= 0)
        def _():
            kv_on(k).wait_send()

    @pl.when((lo == 1) & (c + far < n_ctx))
    def _():
        kv_far().wait_send()

    @pl.when(lo == 0)
    def _():
        kv_on(0).wait_send()

    @pl.loop(1, window)
    def _(d):
        @pl.when(c - d >= 0)
        def _():
            dkv_copy(d).wait_send()

    @pl.when(s == 1)
    def _():
        c_ex[2]()

        @pl.loop(0, n_tp)
        def _(p):
            sec_copy(p).wait_send()


def settle(a_in, b_in, c_in, a_out, b_out, c_out, sem):
    copies = [
        pltpu.make_async_copy(source, target, sem.at[i])
        for i, (source, target) in enumerate(((a_in, a_out), (b_in, b_out), (c_in, c_out)))
    ]
    for copy in copies:
        copy.start()
    for copy in copies:
        copy.wait()


def body(layer_input, loss_cot, token_weights, doc_blocks, norm_gain, qkv_weight, out_weight):
    n_ctx, n_tp = lax.axis_size("ctx"), lax.axis_size("tp")
    n_z = n_ctx // 2
    part = layer_input.shape[3]
    width = part * n_tp
    cols, heads = qkv_weight.shape[2], out_weight.shape[2]
    window = min(MAX_DOC, n_ctx)
    q_rows = GROUP_HEADS * BLOCK
    kv_cols = 2 * HEAD_SIZE
    half = part // 2
    share = BLOCK // n_tp
    vmem = lambda shape, dtype=BF16: pltpu.VMEM(shape, dtype)
    dma = lambda *n: pltpu.SemaphoreType.DMA(n)
    scratch = [
        vmem((width, cols)), vmem((width, heads)),
        vmem((n_tp, BLOCK, part)), vmem((n_tp, BLOCK, part)), vmem((BLOCK, part)), vmem((BLOCK, BLOCK), F32),
        vmem((window * BLOCK, kv_cols)),
        vmem((q_rows, HEAD_SIZE)), vmem((q_rows, HEAD_SIZE)), vmem((q_rows, HEAD_SIZE)),
        vmem((BLOCK, heads)), vmem((BLOCK, kv_cols)),
        vmem((window // 2, q_rows, 2 * BLOCK), F32), vmem((window // 2, q_rows, 2 * BLOCK)),
        vmem((window // 2, q_rows, 2 * BLOCK)),
        vmem((q_rows, BLOCK), F32), vmem((q_rows, BLOCK), F32), vmem((q_rows, HEAD_SIZE), F32),
        vmem((window * BLOCK, kv_cols)), vmem((window, BLOCK, kv_cols)),
        vmem((n_tp, BLOCK, part), F32), vmem((n_tp, BLOCK, part)), vmem((n_tp, BLOCK, part)),
        vmem((8, BLOCK), F32), vmem((n_tp, 8, BLOCK), F32),
        vmem((n_z, share, part)), vmem((n_z, share, part)),
        vmem((n_z, n_tp, share, part)), vmem((n_z, n_tp, share, part)), vmem((n_z * BLOCK, heads)),
        vmem((n_z * BLOCK, heads)), vmem((n_z * BLOCK, kv_cols)), vmem((part, n_z * BLOCK)),
        vmem((half, heads)), vmem((half, heads)), vmem((half, kv_cols)),
        vmem((half, heads)), vmem((half, heads)), vmem((half, kv_cols)),
        dma(2), dma(n_tp), dma(n_tp), dma(n_tp), dma(n_tp), dma(window), dma(window), dma(1), dma(window), dma(window),
        dma(n_tp), dma(n_tp), dma(n_tp), dma(n_tp),
        dma(n_z), dma(n_z), dma(9), dma(n_tp + 2), dma(n_z), dma(n_z), dma(9), dma(n_tp + 2),
        dma(n_z), dma(n_z), dma(n_z), dma(n_z), dma(n_z), dma(n_z),
        dma(3), dma(3), dma(n_tp), pltpu.SemaphoreType.REGULAR,
    ]
    in_vmem = pl.BlockSpec(memory_space=pltpu.VMEM)
    anywhere = pl.BlockSpec(memory_space=pl.ANY)
    grad_in, grad_qkv, grad_out = pl.pallas_call(
        functools.partial(kernel, n_ctx, n_tp, window),
        out_shape=(
            jax.ShapeDtypeStruct((BLOCK, part), BF16),
            jax.ShapeDtypeStruct((half, cols), F32),
            jax.ShapeDtypeStruct((half, heads), F32),
        ),
        in_specs=[
            in_vmem, in_vmem, in_vmem, pl.BlockSpec(memory_space=pltpu.SMEM), in_vmem, anywhere, anywhere,
        ],
        out_specs=(in_vmem, in_vmem, in_vmem),
        scratch_shapes=scratch,
        compiler_params=pltpu.CompilerParams(
            collective_id=0, has_side_effects=True, vmem_limit_bytes=56 * 1024 * 1024
        ),
    )(
        layer_input[0, 0], loss_cot[0], token_weights, doc_blocks, norm_gain, qkv_weight[0], out_weight[0]
    )
    results = (grad_in, grad_qkv, grad_out)
    grad_in, grad_qkv, grad_out = pl.pallas_call(
        settle,
        out_shape=tuple(jax.ShapeDtypeStruct(r.shape, r.dtype) for r in results),
        in_specs=[in_vmem] * 3,
        out_specs=(anywhere,) * 3,
        scratch_shapes=[dma(3)],
    )(*results)
    return grad_in[None, None], grad_qkv[None], grad_out[None]


def solution(mesh):
    placed = (
        P("section", None, "ctx", "tp"),
        P(None, "ctx", "tp"),
        P(None, "ctx"),
        P(),
        P("section", None),
        P("section", None, "tp"),
        P("section", None, "tp"),
    )
    return jax.shard_map(
        body,
        mesh=mesh,
        in_specs=placed,
        out_specs=(
            P("section", None, "ctx", "tp"),
            P("section", "ctx", "tp"),
            P("section", "ctx", "tp"),
        ),
        check_vma=False,
    )
```

```python
import functools

import jax
import jax.numpy as jnp
from jax import lax
from jax.experimental import pallas as pl
from jax.experimental.pallas import tpu as pltpu
from jax.sharding import PartitionSpec as P

MESH = pl.DeviceIdType.MESH
GROUP_HEADS = 4
HEAD_SIZE = 128
BLOCK = 128
MAX_DOC = 10
EPSILON = 1e-05
NEG_FILL = -1e30
F32 = jnp.float32
BF16 = jnp.bfloat16

NN = (((1,), (0,)), ((), ()))
NT = (((1,), (1,)), ((), ()))
TN = (((0,), (0,)), ((), ()))


def mm(a, b, dims=NN):
    return lax.dot_general(a, b, dims, preferred_element_type=F32)


def kernel(
    n_ctx, n_tp, window,
    x_ref, loss_ref, tw_ref, docs_ref, gain_ref, wq_hbm, wo_hbm,
    gin_ref, gqkv_ref, gout_ref,
    wq, wo, xfull, cotfull, cot_loc, inv_b,
    kv, q_s, hc_s, att_s, gq_n, gkv_n, scores, probs, dscores, peak, denom, acc,
    dkv_part, dkv_in, feat_f, feat_out, feat_in, rs_out, rs_in,
    hid_p, cot_p, hid_z, cot_z, att_z, gq_z, gkv_z, turned,
    y_out_o, y_out_q, y_out_k, y_in_o, y_in_q, y_in_k,
    w_sem, x_s, x_r, c_s, c_r, kv_s, kv_r, kv_f, d_s, d_r, f_s, f_r, r_s, r_r,
    h1_s, h1_r, h2_s, h2_r, c1_s, c1_r, c2_s, c2_r, az_s, az_r, qz_s, qz_r, kz_s, kz_r, y_s, y_r, sec_s, gate,
):
    s = lax.axis_index("section")
    c = lax.axis_index("ctx")
    t = lax.axis_index("tp")
    n_z = n_ctx // 2
    z, lo = c // 2, lax.rem(c, 2)
    part = x_ref.shape[1]
    width = part * n_tp
    half = part // 2
    heads = GROUP_HEADS * HEAD_SIZE
    cols = heads + 2 * HEAD_SIZE
    scale = HEAD_SIZE ** (-0.5)
    last = window - 1

    def remote(src, dst, ss, rs, dev):
        return pltpu.make_async_remote_copy(
            src_ref=src, dst_ref=dst, send_sem=ss, recv_sem=rs, device_id=dev, device_id_type=MESH
        )

    def tp_dev(p):
        return {"tp": p}

    def z_dev(p):
        return {"ctx": p * 2 + lo}

    def exchange(n, me, dev, src_of, slot, ss, rs):
        def copy_to(p):
            return remote(src_of(p), slot(me), ss.at[p], rs.at[me], dev(p))

        def copy_from(p):
            return remote(slot(p), slot(p), ss.at[p], rs.at[p], dev(p))

        def start():
            @pl.loop(1, n)
            def _(i):
                copy_to(lax.rem(me + i, n)).start()

        def wait_recv():
            @pl.loop(1, n)
            def _(i):
                copy_from(lax.rem(me + i, n)).wait_recv()

        def wait_send():
            @pl.loop(1, n)
            def _(i):
                copy_to(lax.rem(me + i, n)).wait_send()

        return start, wait_recv, wait_send, copy_to

    def ring(ref, ss, rs):
        up, down = z_dev(lax.rem(z + 1, n_z)), z_dev(lax.rem(z + n_z - 1, n_z))
        top = n_z // 2

        def piece(p, k, side):
            if k < top:
                return ref.at[pl.ds(p * BLOCK, BLOCK)]
            return ref.at[pl.ds(p * BLOCK + side * (BLOCK // 2), BLOCK // 2)]

        def pair(k, shift):
            below = piece(lax.rem(z - k + shift + n_z, n_z), k, 0)
            above = piece(lax.rem(z + k - shift, n_z), k, 1)
            return (
                remote(below, below, ss.at[k - 1], rs.at[k - 1], up),
                remote(above, above, ss.at[top + k - 1], rs.at[top + k - 1], down),
            )

        def arrive(k):
            for copy in pair(k, 0):
                copy.wait_recv()

        def stage(k):
            if k > top:
                return
            if k > 1:
                arrive(k - 1)
            for copy in pair(k, 1):
                copy.start()

        def wait_send():
            for k in range(1, top + 1):
                for copy in pair(k, 1):
                    copy.wait_send()

        return stage, lambda: arrive(top), wait_send

    whole = lambda ref: lambda p: ref
    share = BLOCK // n_tp
    my_rows = pl.ds(pl.multiple_of(t * share, share), share)

    x_ex = exchange(n_tp, t, tp_dev, whole(x_ref), lambda p: xfull.at[p], x_s, x_r)
    c_ex = exchange(n_tp, t, tp_dev, whole(cot_loc), lambda p: cotfull.at[p], c_s, c_r)
    f_ex = exchange(n_tp, t, tp_dev, lambda p: feat_out.at[p], lambda p: feat_in.at[p], f_s, f_r)
    r_ex = exchange(n_tp, t, tp_dev, whole(rs_out), lambda p: rs_in.at[p], r_s, r_r)
    h1_ex = exchange(n_z, z, z_dev, lambda p: xfull.at[p, my_rows], lambda p: hid_p.at[p], h1_s, h1_r)
    h2_ex = exchange(n_tp, t, tp_dev, whole(hid_p), lambda p: hid_z.at[:, p], h2_s, h2_r)
    c1_ex = exchange(n_z, z, z_dev, lambda p: cotfull.at[p, my_rows], lambda p: cot_p.at[p], c1_s, c1_r)
    c2_ex = exchange(n_tp, t, tp_dev, whole(cot_p), lambda p: cot_z.at[:, p], c2_s, c2_r)
    att_ring = ring(att_z, az_s, az_r)
    gq_ring = ring(gq_z, qz_s, qz_r)
    kz_ex = exchange(n_z, z, z_dev, whole(gkv_n), lambda p: gkv_z.at[pl.ds(p * BLOCK, BLOCK)], kz_s, kz_r)
    own_z = pl.ds(pl.multiple_of(z * BLOCK, BLOCK), BLOCK)
    wq_copy = pltpu.make_async_copy(wq_hbm, wq, w_sem.at[0])
    wo_copy = pltpu.make_async_copy(wo_hbm, wo, w_sem.at[1])

    wq_copy.start()
    wo_copy.start()
    kv[...] = jnp.zeros_like(kv)

    barrier = pltpu.get_barrier_semaphore()

    @pl.loop(1, n_tp)
    def _(i):
        pl.semaphore_signal(barrier, inc=1, device_id={"tp": lax.rem(t + i, n_tp)}, device_id_type=MESH)

    @pl.loop(1, n_ctx)
    def _(i):
        pl.semaphore_signal(barrier, inc=1, device_id={"ctx": lax.rem(c + i, n_ctx)}, device_id_type=MESH)

    @pl.loop(0, n_tp)
    def _(p):
        pl.semaphore_signal(barrier, inc=1, device_id={"section": 1 - s, "tp": p}, device_id_type=MESH)

    pl.semaphore_wait(barrier, 2 * n_tp + n_ctx - 2)

    @pl.when(s == 0)
    def _():
        pl.semaphore_wait(gate, 1)

    x_ex[0]()
    xfull[t] = x_ref[...]

    x_ex[1]()

    @pl.when(s == 1)
    def _():
        pl.semaphore_signal(gate, inc=1, device_id={"section": 1 - s}, device_id_type=MESH)

    square = jnp.zeros((BLOCK, part), F32)
    for p in range(n_tp):
        wide = xfull[p].astype(F32)
        square = square + wide * wide
    inv = lax.rsqrt(jnp.sum(square, axis=1, keepdims=True) / width + EPSILON)
    inv_b[...] = jnp.broadcast_to(inv, inv_b.shape)
    for p in range(n_tp):
        gain = gain_ref[:, p * part : (p + 1) * part]
        xfull[p] = ((xfull[p].astype(F32) * inv) * gain).astype(BF16)

    def project(full, weight, lo_col, n_col):
        total = jnp.zeros((BLOCK, n_col), F32)
        for p in range(n_tp):
            total = total + mm(full[p], weight[p * part : (p + 1) * part, lo_col : lo_col + n_col])
        return total.astype(BF16)

    def slot(j):
        if isinstance(j, int):
            return pl.ds(j * BLOCK, BLOCK)
        return pl.ds(pl.multiple_of(j * BLOCK, BLOCK), BLOCK)

    wq_copy.wait()
    kv[slot(last)] = project(xfull, wq, heads, 2 * HEAD_SIZE)

    steps_z = (window - 1) // 2 + 1
    mate = {"ctx": z * 2 + 1 - lo}
    far = window - 1

    def kv_up(k):
        return remote(
            kv.at[slot(last)], kv.at[slot(last - 2 * k)], kv_s.at[2 * k], kv_r.at[2 * k],
            {"ctx": lax.rem(c + 2 * k, n_ctx)},
        )

    def kv_on(k):
        away = 2 * k + 1 - 2 * lo
        return remote(
            kv.at[slot(last - 2 * k)], kv.at[slot(last - away)], kv_s.at[2 * k + 1], kv_r.at[away], mate
        )

    def kv_far():
        return remote(
            kv.at[slot(last)], kv.at[slot(last - far)], kv_f.at[0], kv_r.at[far],
            {"ctx": lax.rem(c + far, n_ctx)},
        )

    def kv_arrival(d):
        return remote(
            kv.at[slot(last - d)], kv.at[slot(last - d)], kv_s.at[0], kv_r.at[d], mate
        )

    @pl.loop(1, steps_z)
    def _(i):
        k = steps_z - i

        @pl.when(z + k < n_z)
        def _():
            kv_up(k).start()

    @pl.when((lo == 1) & (c + far < n_ctx))
    def _():
        kv_far().start()

    @pl.when(lo == 0)
    def _():
        kv_on(0).start()

    for j in range(0, GROUP_HEADS, 2):
        pair = project(xfull, wq, j * HEAD_SIZE, 2 * HEAD_SIZE)
        q_s[j * BLOCK : (j + 1) * BLOCK] = pair[:, :HEAD_SIZE]
        q_s[(j + 1) * BLOCK : (j + 2) * BLOCK] = pair[:, HEAD_SIZE:]
    h1_ex[0]()
    hid_p[z] = xfull[z, my_rows]

    def pass_hidden():
        h1_ex[1]()
        h2_ex[0]()
        hid_z[:, t] = hid_p[...]

    def head_cotangent():
        wo_copy.wait()
        for j in range(0, GROUP_HEADS, 2):
            pair = project(cotfull, wo, j * HEAD_SIZE, 2 * HEAD_SIZE)
            hc_s[j * BLOCK : (j + 1) * BLOCK] = pair[:, :HEAD_SIZE]
            hc_s[(j + 1) * BLOCK : (j + 2) * BLOCK] = pair[:, HEAD_SIZE:]

    @pl.when(s == 1)
    def _():
        weights = jnp.broadcast_to(tw_ref[...].astype(F32), (BLOCK, BLOCK)).T[:, :1]
        cot_loc[...] = (loss_ref[...].astype(F32) * weights).astype(BF16)
        cotfull[t] = cot_loc[...]
        c_ex[0]()

    @pl.loop(1, steps_z)
    def _(k):
        @pl.when(z - k >= 0)
        def _():
            kv_up(k).wait_recv()
            kv_on(k).start()

    @pl.when(s == 0)
    def _():
        pass_hidden()

    doc_start = jnp.int32(0)
    doc_end = jnp.int32(0)
    for i in range(docs_ref.shape[1]):
        doc_end = doc_end + docs_ref[0, i]
        doc_start = jnp.where(doc_end <= c, doc_end, doc_start)
    pairs = window // 2
    wide = (GROUP_HEADS * BLOCK, 2 * BLOCK)
    query_pos = c * BLOCK + lax.broadcasted_iota(jnp.int32, wide, 0) % BLOCK
    first_key = (c - last) * BLOCK + lax.broadcasted_iota(jnp.int32, wide, 1)

    def keys(g):
        return kv[g * 2 * BLOCK : (g + 1) * 2 * BLOCK, :HEAD_SIZE]

    def values(g):
        return kv[g * 2 * BLOCK : (g + 1) * 2 * BLOCK, HEAD_SIZE:]

    for g in range(pairs - 1, -1, -1):
        for j in (2 * g + 1, 2 * g):
            if j < last:

                if (last - j) % 2 == 1:

                    @pl.when(c - last + j >= 0)
                    def _():
                        kv_arrival(last - j).wait_recv()

        block = mm(q_s[...], keys(g), NT) * scale
        key_pos = first_key + g * 2 * BLOCK
        block = jnp.where((key_pos <= query_pos) & (key_pos >= doc_start * BLOCK), block, NEG_FILL)
        scores[g] = block
        both = jnp.maximum(block[:, :BLOCK], block[:, BLOCK:])
        peak[...] = both if g == pairs - 1 else jnp.maximum(peak[...], both)

    top = jnp.max(peak[...], axis=1, keepdims=True)
    for g in range(pairs):
        e = jnp.exp(scores[g] - top)
        scores[g] = e
        both = e[:, :BLOCK] + e[:, BLOCK:]
        denom[...] = both if g == 0 else denom[...] + both

    inverse = 1.0 / jnp.sum(denom[...], axis=1, keepdims=True)
    for g in range(pairs):
        soft = scores[g] * inverse
        low = soft.astype(BF16)
        scores[g] = soft
        probs[g] = low
        term = mm(low, values(g))
        acc[...] = term if g == 0 else acc[...] + term

    att_s[...] = acc[...].astype(BF16)
    for j in range(GROUP_HEADS):
        att_z[own_z, j * HEAD_SIZE : (j + 1) * HEAD_SIZE] = att_s[j * BLOCK : (j + 1) * BLOCK]

    def sec_copy(p):
        return remote(gin_ref, cotfull.at[t], sec_s.at[p], c_r.at[t], {"section": 1 - s, "tp": p})

    @pl.when(s == 1)
    def _():
        c_ex[1]()
        head_cotangent()

    @pl.when(s == 0)
    def _():
        for k in range(1, min(3, n_z // 2) + 1):
            att_ring[0](k)

        @pl.loop(0, n_tp)
        def _(p):
            remote(cotfull.at[p], cotfull.at[p], sec_s.at[p], c_r.at[p], {"section": 1 - s}).wait_recv()

        head_cotangent()
        att_ring[0](4)

    delta = jnp.sum(hc_s[...].astype(F32) * att_s[...].astype(F32), axis=1, keepdims=True)

    def dkv_copy(d):
        return remote(
            dkv_part.at[slot(last - d)], dkv_in.at[d], d_s.at[d], d_r.at[d],
            {"ctx": lax.rem(c - d + n_ctx, n_ctx)},
        )

    for g in range(pairs):
        block = slice(g * 2 * BLOCK, (g + 1) * 2 * BLOCK)
        dprobs = mm(hc_s[...], values(g), NT)
        ds = (scores[g] * (dprobs - delta)).astype(BF16)
        dkv_part[block, :HEAD_SIZE] = (mm(ds, q_s[...], TN) * scale).astype(BF16)
        dkv_part[block, HEAD_SIZE:] = mm(probs[g], hc_s[...], TN).astype(BF16)
        dscores[g] = ds
        for j in (2 * g, 2 * g + 1):
            if j < last:

                @pl.when(c - last + j >= 0)
                def _():
                    dkv_copy(last - j).start()

    total = mm(dscores[0], keys(0))
    for g in range(1, pairs):
        total = total + mm(dscores[g], keys(g))
    acc[...] = total
    for j in range(GROUP_HEADS):
        gq_n[:, j * HEAD_SIZE : (j + 1) * HEAD_SIZE] = (
            acc[j * BLOCK : (j + 1) * BLOCK] * scale
        ).astype(BF16)
    gq_z[own_z] = gq_n[...]

    def send_cot():
        c1_ex[0]()
        cot_p[z] = cotfull[z, my_rows]

    def pass_cot():
        c1_ex[1]()
        c2_ex[0]()
        cot_z[:, t] = cot_p[...]

    @pl.when(s == 0)
    def _():
        send_cot()
        gq_ring[0](1)

    @pl.when(s == 1)
    def _():
        pass_hidden()

    @pl.loop(0, n_tp)
    def _(p):
        feat_f[p] = mm(gq_n[...], wq[pl.ds(p * part, part), :heads], NT)

    @pl.when(s == 0)
    def _():
        pass_cot()
        gq_ring[0](2)

    acc[:BLOCK] = dkv_part[slot(last), :HEAD_SIZE].astype(F32)
    acc[BLOCK : 2 * BLOCK] = dkv_part[slot(last), HEAD_SIZE:].astype(F32)

    @pl.loop(1, window)
    def _(d):
        @pl.when(c + d < n_ctx)
        def _():
            dkv_copy(d).wait_recv()
            acc[:BLOCK] += dkv_in[d, :, :HEAD_SIZE].astype(F32)
            acc[BLOCK : 2 * BLOCK] += dkv_in[d, :, HEAD_SIZE:].astype(F32)

    gkv_n[:, :HEAD_SIZE] = acc[:BLOCK].astype(BF16)
    gkv_n[:, HEAD_SIZE:] = acc[BLOCK : 2 * BLOCK].astype(BF16)
    gkv_z[own_z] = gkv_n[...]
    kz_ex[0]()

    row_sum = gkv_n[:, :HEAD_SIZE].astype(F32) * kv[slot(last), :HEAD_SIZE].astype(F32)
    row_sum = row_sum + gkv_n[:, HEAD_SIZE:].astype(F32) * kv[slot(last), HEAD_SIZE:].astype(F32)
    for j in range(GROUP_HEADS):
        row_sum = row_sum + gq_n[:, j * HEAD_SIZE : (j + 1) * HEAD_SIZE].astype(F32) * q_s[
            j * BLOCK : (j + 1) * BLOCK
        ].astype(F32)
    row_sum = jnp.sum(row_sum, axis=1, keepdims=True)
    rs_out[...] = jnp.broadcast_to(row_sum, (BLOCK, BLOCK)).T[:8]
    r_ex[0]()
    rs_in[t] = rs_out[...]

    @pl.loop(1, n_tp + 1)
    def _(i):
        p = lax.rem(t + i, n_tp)
        total = feat_f[p] + mm(gkv_n[...], wq[pl.ds(p * part, part), heads:], NT)
        feat_out[p] = total.astype(BF16)

        @pl.when(i < n_tp)
        def _():
            f_ex[3](p).start()

    feat_in[t] = feat_out[t]

    y_copies = [
        remote(y_out_o, y_in_o, y_s.at[0], y_r.at[0], mate),
        remote(y_out_q, y_in_q, y_s.at[1], y_r.at[1], mate),
        remote(y_out_k, y_in_k, y_s.at[2], y_r.at[2], mate),
    ]
    positions = n_z * BLOCK
    theirs = pl.ds(pl.multiple_of((1 - lo) * half, half), half)
    mine = pl.ds(pl.multiple_of(lo * half, half), half)

    def turn(ref):
        turned[...] = ref[...].reshape(positions, part).T

    def weight_part(right, y_out, out, base, copy):
        step = min(256, heads)
        for k in range(0, right.shape[1], step):
            y_out[:, k : k + step] = mm(turned[theirs], right[:, k : k + step]).astype(BF16)
        copy.start()
        for k in range(0, right.shape[1], step):
            out[:, base + k : base + k + step] = mm(turned[mine], right[:, k : k + step])

    def grad_of_out():
        c2_ex[1]()
        att_ring[1]()
        turn(cot_z)
        weight_part(att_z, y_out_o, gout_ref, 0, y_copies[0])

    def grad_of_query():
        h2_ex[1]()
        turn(hid_z)
        gq_ring[1]()
        weight_part(gq_z, y_out_q, gqkv_ref, 0, y_copies[1])

    @pl.when(s == 0)
    def _():
        gq_ring[0](3)
        grad_of_out()
        gq_ring[0](4)
        grad_of_query()

    f_ex[1]()
    r_ex[1]()
    feature = jnp.zeros((BLOCK, part), F32)
    for p in range(n_tp):
        feature = feature + feat_in[p].astype(F32)
    inv = inv_b[:, :1]
    gain = gain_ref[:, pl.ds(pl.multiple_of(t * part, part), part)]
    scaled = feature * gain
    normed = x_ref[...].astype(F32) * inv
    total = rs_in[0]
    for p in range(1, n_tp):
        total = total + rs_in[p]
    mean = jnp.broadcast_to(total[:1] / width, (BLOCK, BLOCK)).T[:, :1]
    gin_ref[...] = (cotfull[t].astype(F32) + inv * (scaled - normed * mean)).astype(BF16)

    @pl.when(s == 1)
    def _():
        @pl.loop(0, n_tp)
        def _(i):
            sec_copy(lax.rem(t + i, n_tp)).start()

        send_cot()
        for k in range(1, n_z // 2 + 1):
            att_ring[0](k)
            gq_ring[0](k)
        pass_cot()
        grad_of_out()
        grad_of_query()

    kz_ex[1]()
    weight_part(gkv_z, y_out_k, gqkv_ref, heads, y_copies[2])
    for y_in, out, base, copy in (
        (y_in_o, gout_ref, 0, y_copies[0]),
        (y_in_q, gqkv_ref, 0, y_copies[1]),
        (y_in_k, gqkv_ref, heads, y_copies[2]),
    ):
        copy.wait_recv()
        out[:, base : base + y_in.shape[1]] += y_in[...].astype(F32)

    for ex in (x_ex, f_ex, r_ex, h1_ex, h2_ex, c1_ex, c2_ex, kz_ex, att_ring, gq_ring):
        ex[2]()
    for copy in y_copies:
        copy.wait_send()

    @pl.loop(1, steps_z)
    def _(k):
        @pl.when(z + k < n_z)
        def _():
            kv_up(k).wait_send()

        @pl.when(z - k >= 0)
        def _():
            kv_on(k).wait_send()

    @pl.when((lo == 1) & (c + far < n_ctx))
    def _():
        kv_far().wait_send()

    @pl.when(lo == 0)
    def _():
        kv_on(0).wait_send()

    @pl.loop(1, window)
    def _(d):
        @pl.when(c - d >= 0)
        def _():
            dkv_copy(d).wait_send()

    @pl.when(s == 1)
    def _():
        c_ex[2]()

        @pl.loop(0, n_tp)
        def _(p):
            sec_copy(p).wait_send()


def settle(a_in, b_in, c_in, a_out, b_out, c_out, sem):
    copies = [
        pltpu.make_async_copy(source, target, sem.at[i])
        for i, (source, target) in enumerate(((a_in, a_out), (b_in, b_out), (c_in, c_out)))
    ]
    for copy in copies:
        copy.start()
    for copy in copies:
        copy.wait()


def body(layer_input, loss_cot, token_weights, doc_blocks, norm_gain, qkv_weight, out_weight):
    n_ctx, n_tp = lax.axis_size("ctx"), lax.axis_size("tp")
    n_z = n_ctx // 2
    part = layer_input.shape[3]
    width = part * n_tp
    cols, heads = qkv_weight.shape[2], out_weight.shape[2]
    window = min(MAX_DOC, n_ctx)
    q_rows = GROUP_HEADS * BLOCK
    kv_cols = 2 * HEAD_SIZE
    half = part // 2
    share = BLOCK // n_tp
    vmem = lambda shape, dtype=BF16: pltpu.VMEM(shape, dtype)
    dma = lambda *n: pltpu.SemaphoreType.DMA(n)
    scratch = [
        vmem((width, cols)), vmem((width, heads)),
        vmem((n_tp, BLOCK, part)), vmem((n_tp, BLOCK, part)), vmem((BLOCK, part)), vmem((BLOCK, BLOCK), F32),
        vmem((window * BLOCK, kv_cols)),
        vmem((q_rows, HEAD_SIZE)), vmem((q_rows, HEAD_SIZE)), vmem((q_rows, HEAD_SIZE)),
        vmem((BLOCK, heads)), vmem((BLOCK, kv_cols)),
        vmem((window // 2, q_rows, 2 * BLOCK), F32), vmem((window // 2, q_rows, 2 * BLOCK)),
        vmem((window // 2, q_rows, 2 * BLOCK)),
        vmem((q_rows, BLOCK), F32), vmem((q_rows, BLOCK), F32), vmem((q_rows, HEAD_SIZE), F32),
        vmem((window * BLOCK, kv_cols)), vmem((window, BLOCK, kv_cols)),
        vmem((n_tp, BLOCK, part), F32), vmem((n_tp, BLOCK, part)), vmem((n_tp, BLOCK, part)),
        vmem((8, BLOCK), F32), vmem((n_tp, 8, BLOCK), F32),
        vmem((n_z, share, part)), vmem((n_z, share, part)),
        vmem((n_z, n_tp, share, part)), vmem((n_z, n_tp, share, part)), vmem((n_z * BLOCK, heads)),
        vmem((n_z * BLOCK, heads)), vmem((n_z * BLOCK, kv_cols)), vmem((part, n_z * BLOCK)),
        vmem((half, heads)), vmem((half, heads)), vmem((half, kv_cols)),
        vmem((half, heads)), vmem((half, heads)), vmem((half, kv_cols)),
        dma(2), dma(n_tp), dma(n_tp), dma(n_tp), dma(n_tp), dma(window), dma(window), dma(1), dma(window), dma(window),
        dma(n_tp), dma(n_tp), dma(n_tp), dma(n_tp),
        dma(n_z), dma(n_z), dma(n_tp), dma(n_tp), dma(n_z), dma(n_z), dma(n_tp), dma(n_tp),
        dma(n_z), dma(n_z), dma(n_z), dma(n_z), dma(n_z), dma(n_z),
        dma(3), dma(3), dma(n_tp), pltpu.SemaphoreType.REGULAR,
    ]
    in_vmem = pl.BlockSpec(memory_space=pltpu.VMEM)
    anywhere = pl.BlockSpec(memory_space=pl.ANY)
    grad_in, grad_qkv, grad_out = pl.pallas_call(
        functools.partial(kernel, n_ctx, n_tp, window),
        out_shape=(
            jax.ShapeDtypeStruct((BLOCK, part), BF16),
            jax.ShapeDtypeStruct((half, cols), F32),
            jax.ShapeDtypeStruct((half, heads), F32),
        ),
        in_specs=[
            in_vmem, in_vmem, in_vmem, pl.BlockSpec(memory_space=pltpu.SMEM), in_vmem, anywhere, anywhere,
        ],
        out_specs=(in_vmem, in_vmem, in_vmem),
        scratch_shapes=scratch,
        compiler_params=pltpu.CompilerParams(
            collective_id=0, has_side_effects=True, vmem_limit_bytes=56 * 1024 * 1024
        ),
    )(
        layer_input[0, 0], loss_cot[0], token_weights, doc_blocks, norm_gain, qkv_weight[0], out_weight[0]
    )
    results = (grad_in, grad_qkv, grad_out)
    grad_in, grad_qkv, grad_out = pl.pallas_call(
        settle,
        out_shape=tuple(jax.ShapeDtypeStruct(r.shape, r.dtype) for r in results),
        in_specs=[in_vmem] * 3,
        out_specs=(anywhere,) * 3,
        scratch_shapes=[dma(3)],
    )(*results)
    return grad_in[None, None], grad_qkv[None], grad_out[None]


def solution(mesh):
    placed = (
        P("section", None, "ctx", "tp"),
        P(None, "ctx", "tp"),
        P(None, "ctx"),
        P(),
        P("section", None),
        P("section", None, "tp"),
        P("section", None, "tp"),
    )
    return jax.shard_map(
        body,
        mesh=mesh,
        in_specs=placed,
        out_specs=(
            P("section", None, "ctx", "tp"),
            P("section", "ctx", "tp"),
            P("section", "ctx", "tp"),
        ),
        check_vma=False,
    )
```

```python
import functools

import jax
import jax.numpy as jnp
from jax import lax
from jax.experimental import pallas as pl
from jax.experimental.pallas import tpu as pltpu
from jax.sharding import PartitionSpec as P

MESH = pl.DeviceIdType.MESH
GROUP_HEADS = 4
HEAD_SIZE = 128
BLOCK = 128
MAX_DOC = 10
EPSILON = 1e-05
NEG_FILL = -1e30
F32 = jnp.float32
BF16 = jnp.bfloat16

NN = (((1,), (0,)), ((), ()))
NT = (((1,), (1,)), ((), ()))
TN = (((0,), (0,)), ((), ()))


def mm(a, b, dims=NN):
    return lax.dot_general(a, b, dims, preferred_element_type=F32)


def kernel(
    n_ctx, n_tp, window,
    x_ref, loss_ref, tw_ref, docs_ref, gain_ref, wq_hbm, wo_hbm,
    gin_ref, gqkv_ref, gout_ref,
    wq, wo, xfull, cotfull, cot_loc, inv_b,
    kv, q_s, hc_s, att_s, gq_n, gkv_n, scores, probs, dscores, peak, denom, acc,
    dkv_part, dkv_in, feat_f, feat_out, feat_in, rs_out, rs_in,
    hid_p, cot_p, hid_z, cot_z, att_z, gq_z, gkv_z, turned,
    y_out_o, y_out_q, y_out_k, y_in_o, y_in_q, y_in_k,
    w_sem, x_s, x_r, c_s, c_r, kv_s, kv_r, kv_f, d_s, d_r, f_s, f_r, r_s, r_r,
    h1_s, h1_r, h2_s, h2_r, c1_s, c1_r, c2_s, c2_r, az_s, az_r, qz_s, qz_r, kz_s, kz_r, y_s, y_r, sec_s, gate,
):
    s = lax.axis_index("section")
    c = lax.axis_index("ctx")
    t = lax.axis_index("tp")
    n_z = n_ctx // 2
    z, lo = c // 2, lax.rem(c, 2)
    part = x_ref.shape[1]
    width = part * n_tp
    half = part // 2
    heads = GROUP_HEADS * HEAD_SIZE
    cols = heads + 2 * HEAD_SIZE
    scale = HEAD_SIZE ** (-0.5)
    last = window - 1

    def remote(src, dst, ss, rs, dev):
        return pltpu.make_async_remote_copy(
            src_ref=src, dst_ref=dst, send_sem=ss, recv_sem=rs, device_id=dev, device_id_type=MESH
        )

    def tp_dev(p):
        return {"tp": p}

    def z_dev(p):
        return {"ctx": p * 2 + lo}

    def exchange(n, me, dev, src_of, slot, ss, rs):
        def copy_to(p):
            return remote(src_of(p), slot(me), ss.at[p], rs.at[me], dev(p))

        def copy_from(p):
            return remote(slot(p), slot(p), ss.at[p], rs.at[p], dev(p))

        def start():
            @pl.loop(1, n)
            def _(i):
                copy_to(lax.rem(me + i, n)).start()

        def wait_recv():
            @pl.loop(1, n)
            def _(i):
                copy_from(lax.rem(me + i, n)).wait_recv()

        def wait_send():
            @pl.loop(1, n)
            def _(i):
                copy_to(lax.rem(me + i, n)).wait_send()

        return start, wait_recv, wait_send, copy_to

    def ring(ref, ss, rs):
        up, down = z_dev(lax.rem(z + 1, n_z)), z_dev(lax.rem(z + n_z - 1, n_z))
        top = n_z // 2

        def piece(p, k, side):
            if k < top:
                return ref.at[pl.ds(p * BLOCK, BLOCK)]
            return ref.at[pl.ds(p * BLOCK + side * (BLOCK // 2), BLOCK // 2)]

        def pair(k, shift):
            below = piece(lax.rem(z - k + shift + n_z, n_z), k, 0)
            above = piece(lax.rem(z + k - shift, n_z), k, 1)
            return (
                remote(below, below, ss.at[k - 1], rs.at[k - 1], up),
                remote(above, above, ss.at[top + k - 1], rs.at[top + k - 1], down),
            )

        def arrive(k):
            for copy in pair(k, 0):
                copy.wait_recv()

        def stage(k):
            if k > top:
                return
            if k > 1:
                arrive(k - 1)
            for copy in pair(k, 1):
                copy.start()

        def wait_send():
            for k in range(1, top + 1):
                for copy in pair(k, 1):
                    copy.wait_send()

        return stage, lambda: arrive(top), wait_send

    whole = lambda ref: lambda p: ref
    share = BLOCK // n_tp
    my_rows = pl.ds(pl.multiple_of(t * share, share), share)

    x_ex = exchange(n_tp, t, tp_dev, whole(x_ref), lambda p: xfull.at[p], x_s, x_r)
    c_ex = exchange(n_tp, t, tp_dev, whole(cot_loc), lambda p: cotfull.at[p], c_s, c_r)
    f_ex = exchange(n_tp, t, tp_dev, lambda p: feat_out.at[p], lambda p: feat_in.at[p], f_s, f_r)
    r_ex = exchange(n_tp, t, tp_dev, whole(rs_out), lambda p: rs_in.at[p], r_s, r_r)
    h1_ex = exchange(n_z, z, z_dev, lambda p: xfull.at[p, my_rows], lambda p: hid_p.at[p], h1_s, h1_r)
    h2_ex = exchange(n_tp, t, tp_dev, whole(hid_p), lambda p: hid_z.at[:, p], h2_s, h2_r)
    c1_ex = exchange(n_z, z, z_dev, lambda p: cotfull.at[p, my_rows], lambda p: cot_p.at[p], c1_s, c1_r)
    c2_ex = exchange(n_tp, t, tp_dev, whole(cot_p), lambda p: cot_z.at[:, p], c2_s, c2_r)
    att_ring = ring(att_z, az_s, az_r)
    gq_ring = ring(gq_z, qz_s, qz_r)
    kz_ex = exchange(n_z, z, z_dev, whole(gkv_n), lambda p: gkv_z.at[pl.ds(p * BLOCK, BLOCK)], kz_s, kz_r)
    own_z = pl.ds(pl.multiple_of(z * BLOCK, BLOCK), BLOCK)
    wq_copy = pltpu.make_async_copy(wq_hbm, wq, w_sem.at[0])
    wo_copy = pltpu.make_async_copy(wo_hbm, wo, w_sem.at[1])

    wq_copy.start()
    wo_copy.start()
    kv[...] = jnp.zeros_like(kv)

    barrier = pltpu.get_barrier_semaphore()

    @pl.loop(1, n_tp)
    def _(i):
        pl.semaphore_signal(barrier, inc=1, device_id={"tp": lax.rem(t + i, n_tp)}, device_id_type=MESH)

    @pl.loop(1, n_ctx)
    def _(i):
        pl.semaphore_signal(barrier, inc=1, device_id={"ctx": lax.rem(c + i, n_ctx)}, device_id_type=MESH)

    @pl.loop(0, n_tp)
    def _(p):
        pl.semaphore_signal(barrier, inc=1, device_id={"section": 1 - s, "tp": p}, device_id_type=MESH)

    pl.semaphore_wait(barrier, 2 * n_tp + n_ctx - 2)

    @pl.when(s == 0)
    def _():
        pl.semaphore_wait(gate, 1)

    x_ex[0]()
    xfull[t] = x_ref[...]

    x_ex[1]()

    @pl.when(s == 1)
    def _():
        weights = jnp.broadcast_to(tw_ref[...].astype(F32), (BLOCK, BLOCK)).T[:, :1]
        cot_loc[...] = (loss_ref[...].astype(F32) * weights).astype(BF16)
        cotfull[t] = cot_loc[...]
        c_ex[0]()

    square = jnp.zeros((BLOCK, part), F32)
    for p in range(n_tp):
        wide = xfull[p].astype(F32)
        square = square + wide * wide
    inv = lax.rsqrt(jnp.sum(square, axis=1, keepdims=True) / width + EPSILON)
    inv_b[...] = jnp.broadcast_to(inv, inv_b.shape)
    for p in range(n_tp):
        gain = gain_ref[:, p * part : (p + 1) * part]
        xfull[p] = ((xfull[p].astype(F32) * inv) * gain).astype(BF16)

    def project(full, weight, lo_col, n_col):
        total = jnp.zeros((BLOCK, n_col), F32)
        for p in range(n_tp):
            total = total + mm(full[p], weight[p * part : (p + 1) * part, lo_col : lo_col + n_col])
        return total.astype(BF16)

    def slot(j):
        if isinstance(j, int):
            return pl.ds(j * BLOCK, BLOCK)
        return pl.ds(pl.multiple_of(j * BLOCK, BLOCK), BLOCK)

    wq_copy.wait()
    kv[slot(last)] = project(xfull, wq, heads, 2 * HEAD_SIZE)

    steps_z = (window - 1) // 2 + 1
    mate = {"ctx": z * 2 + 1 - lo}
    far = window - 1

    def kv_up(k):
        return remote(
            kv.at[slot(last)], kv.at[slot(last - 2 * k)], kv_s.at[2 * k], kv_r.at[2 * k],
            {"ctx": lax.rem(c + 2 * k, n_ctx)},
        )

    def kv_on(k):
        away = 2 * k + 1 - 2 * lo
        return remote(
            kv.at[slot(last - 2 * k)], kv.at[slot(last - away)], kv_s.at[2 * k + 1], kv_r.at[away], mate
        )

    def kv_far():
        return remote(
            kv.at[slot(last)], kv.at[slot(last - far)], kv_f.at[0], kv_r.at[far],
            {"ctx": lax.rem(c + far, n_ctx)},
        )

    def kv_arrival(d):
        return remote(
            kv.at[slot(last - d)], kv.at[slot(last - d)], kv_s.at[0], kv_r.at[d], mate
        )

    @pl.loop(1, steps_z)
    def _(i):
        k = steps_z - i

        @pl.when(z + k < n_z)
        def _():
            kv_up(k).start()

    @pl.when((lo == 1) & (c + far < n_ctx))
    def _():
        kv_far().start()

    @pl.when(lo == 0)
    def _():
        kv_on(0).start()

    @pl.when(s == 1)
    def _():
        pl.semaphore_signal(gate, inc=1, device_id={"section": 1 - s}, device_id_type=MESH)

    for j in range(0, GROUP_HEADS, 2):
        pair = project(xfull, wq, j * HEAD_SIZE, 2 * HEAD_SIZE)
        q_s[j * BLOCK : (j + 1) * BLOCK] = pair[:, :HEAD_SIZE]
        q_s[(j + 1) * BLOCK : (j + 2) * BLOCK] = pair[:, HEAD_SIZE:]
    h1_ex[0]()
    hid_p[z] = xfull[z, my_rows]

    def pass_hidden():
        h1_ex[1]()
        h2_ex[0]()
        hid_z[:, t] = hid_p[...]

    def head_cotangent():
        wo_copy.wait()
        for j in range(0, GROUP_HEADS, 2):
            pair = project(cotfull, wo, j * HEAD_SIZE, 2 * HEAD_SIZE)
            hc_s[j * BLOCK : (j + 1) * BLOCK] = pair[:, :HEAD_SIZE]
            hc_s[(j + 1) * BLOCK : (j + 2) * BLOCK] = pair[:, HEAD_SIZE:]

    @pl.loop(1, steps_z)
    def _(k):
        @pl.when(z - k >= 0)
        def _():
            kv_up(k).wait_recv()
            kv_on(k).start()

    @pl.when(s == 0)
    def _():
        pass_hidden()

    doc_start = jnp.int32(0)
    doc_end = jnp.int32(0)
    for i in range(docs_ref.shape[1]):
        doc_end = doc_end + docs_ref[0, i]
        doc_start = jnp.where(doc_end <= c, doc_end, doc_start)
    pairs = window // 2
    wide = (GROUP_HEADS * BLOCK, 2 * BLOCK)
    query_pos = c * BLOCK + lax.broadcasted_iota(jnp.int32, wide, 0) % BLOCK
    first_key = (c - last) * BLOCK + lax.broadcasted_iota(jnp.int32, wide, 1)

    def keys(g):
        return kv[g * 2 * BLOCK : (g + 1) * 2 * BLOCK, :HEAD_SIZE]

    def values(g):
        return kv[g * 2 * BLOCK : (g + 1) * 2 * BLOCK, HEAD_SIZE:]

    for g in range(pairs - 1, -1, -1):
        for j in (2 * g + 1, 2 * g):
            if j < last:

                if (last - j) % 2 == 1:

                    @pl.when(c - last + j >= 0)
                    def _():
                        kv_arrival(last - j).wait_recv()

        block = mm(q_s[...], keys(g), NT) * scale
        key_pos = first_key + g * 2 * BLOCK
        block = jnp.where((key_pos <= query_pos) & (key_pos >= doc_start * BLOCK), block, NEG_FILL)
        scores[g] = block
        both = jnp.maximum(block[:, :BLOCK], block[:, BLOCK:])
        peak[...] = both if g == pairs - 1 else jnp.maximum(peak[...], both)

    top = jnp.max(peak[...], axis=1, keepdims=True)
    for g in range(pairs):
        e = jnp.exp(scores[g] - top)
        scores[g] = e
        both = e[:, :BLOCK] + e[:, BLOCK:]
        denom[...] = both if g == 0 else denom[...] + both

    inverse = 1.0 / jnp.sum(denom[...], axis=1, keepdims=True)
    for g in range(pairs):
        soft = scores[g] * inverse
        low = soft.astype(BF16)
        scores[g] = soft
        probs[g] = low
        term = mm(low, values(g))
        acc[...] = term if g == 0 else acc[...] + term

    att_s[...] = acc[...].astype(BF16)
    for j in range(GROUP_HEADS):
        att_z[own_z, j * HEAD_SIZE : (j + 1) * HEAD_SIZE] = att_s[j * BLOCK : (j + 1) * BLOCK]

    def sec_copy(p):
        return remote(gin_ref, cotfull.at[t], sec_s.at[p], c_r.at[t], {"section": 1 - s, "tp": p})

    @pl.when(s == 1)
    def _():
        c_ex[1]()
        head_cotangent()
        pass_hidden()

    @pl.when(s == 0)
    def _():
        for k in (1, 2):
            att_ring[0](k)

        @pl.loop(0, n_tp)
        def _(p):
            remote(cotfull.at[p], cotfull.at[p], sec_s.at[p], c_r.at[p], {"section": 1 - s}).wait_recv()

        head_cotangent()
        att_ring[0](3)

    delta = jnp.sum(hc_s[...].astype(F32) * att_s[...].astype(F32), axis=1, keepdims=True)

    def dkv_copy(d):
        return remote(
            dkv_part.at[slot(last - d)], dkv_in.at[d], d_s.at[d], d_r.at[d],
            {"ctx": lax.rem(c - d + n_ctx, n_ctx)},
        )

    for g in range(pairs):
        block = slice(g * 2 * BLOCK, (g + 1) * 2 * BLOCK)
        dprobs = mm(hc_s[...], values(g), NT)
        ds = (scores[g] * (dprobs - delta)).astype(BF16)
        dkv_part[block, :HEAD_SIZE] = (mm(ds, q_s[...], TN) * scale).astype(BF16)
        dkv_part[block, HEAD_SIZE:] = mm(probs[g], hc_s[...], TN).astype(BF16)
        dscores[g] = ds
        for j in (2 * g, 2 * g + 1):
            if j < last:

                @pl.when(c - last + j >= 0)
                def _():
                    dkv_copy(last - j).start()

    total = mm(dscores[0], keys(0))
    for g in range(1, pairs):
        total = total + mm(dscores[g], keys(g))
    acc[...] = total
    for j in range(GROUP_HEADS):
        gq_n[:, j * HEAD_SIZE : (j + 1) * HEAD_SIZE] = (
            acc[j * BLOCK : (j + 1) * BLOCK] * scale
        ).astype(BF16)
    gq_z[own_z] = gq_n[...]

    def send_cot():
        c1_ex[0]()
        cot_p[z] = cotfull[z, my_rows]

    def pass_cot():
        c1_ex[1]()
        c2_ex[0]()
        cot_z[:, t] = cot_p[...]

    @pl.when(s == 0)
    def _():
        send_cot()
        gq_ring[0](1)
        att_ring[0](4)

    @pl.loop(0, n_tp)
    def _(p):
        feat_f[p] = mm(gq_n[...], wq[pl.ds(p * part, part), :heads], NT)

    @pl.when(s == 0)
    def _():
        pass_cot()
        gq_ring[0](2)

    acc[:BLOCK] = dkv_part[slot(last), :HEAD_SIZE].astype(F32)
    acc[BLOCK : 2 * BLOCK] = dkv_part[slot(last), HEAD_SIZE:].astype(F32)

    @pl.loop(1, window)
    def _(d):
        @pl.when(c + d < n_ctx)
        def _():
            dkv_copy(d).wait_recv()
            acc[:BLOCK] += dkv_in[d, :, :HEAD_SIZE].astype(F32)
            acc[BLOCK : 2 * BLOCK] += dkv_in[d, :, HEAD_SIZE:].astype(F32)

    gkv_n[:, :HEAD_SIZE] = acc[:BLOCK].astype(BF16)
    gkv_n[:, HEAD_SIZE:] = acc[BLOCK : 2 * BLOCK].astype(BF16)
    gkv_z[own_z] = gkv_n[...]
    kz_ex[0]()

    row_sum = gkv_n[:, :HEAD_SIZE].astype(F32) * kv[slot(last), :HEAD_SIZE].astype(F32)
    row_sum = row_sum + gkv_n[:, HEAD_SIZE:].astype(F32) * kv[slot(last), HEAD_SIZE:].astype(F32)
    for j in range(GROUP_HEADS):
        row_sum = row_sum + gq_n[:, j * HEAD_SIZE : (j + 1) * HEAD_SIZE].astype(F32) * q_s[
            j * BLOCK : (j + 1) * BLOCK
        ].astype(F32)
    row_sum = jnp.sum(row_sum, axis=1, keepdims=True)
    rs_out[...] = jnp.broadcast_to(row_sum, (BLOCK, BLOCK)).T[:8]
    r_ex[0]()
    rs_in[t] = rs_out[...]

    @pl.loop(1, n_tp + 1)
    def _(i):
        p = lax.rem(t + i, n_tp)
        total = feat_f[p] + mm(gkv_n[...], wq[pl.ds(p * part, part), heads:], NT)
        feat_out[p] = total.astype(BF16)

        @pl.when(i < n_tp)
        def _():
            f_ex[3](p).start()

    feat_in[t] = feat_out[t]

    y_copies = [
        remote(y_out_o, y_in_o, y_s.at[0], y_r.at[0], mate),
        remote(y_out_q, y_in_q, y_s.at[1], y_r.at[1], mate),
        remote(y_out_k, y_in_k, y_s.at[2], y_r.at[2], mate),
    ]
    positions = n_z * BLOCK
    theirs = pl.ds(pl.multiple_of((1 - lo) * half, half), half)
    mine = pl.ds(pl.multiple_of(lo * half, half), half)

    def turn(ref):
        turned[...] = ref[...].reshape(positions, part).T

    def weight_part(right, y_out, out, base, copy):
        step = min(256, heads)
        for k in range(0, right.shape[1], step):
            y_out[:, k : k + step] = mm(turned[theirs], right[:, k : k + step]).astype(BF16)
        copy.start()
        for k in range(0, right.shape[1], step):
            out[:, base + k : base + k + step] = mm(turned[mine], right[:, k : k + step])

    def grad_of_out():
        c2_ex[1]()
        att_ring[1]()
        turn(cot_z)
        weight_part(att_z, y_out_o, gout_ref, 0, y_copies[0])

    def grad_of_query():
        h2_ex[1]()
        turn(hid_z)
        gq_ring[1]()
        weight_part(gq_z, y_out_q, gqkv_ref, 0, y_copies[1])

    @pl.when(s == 0)
    def _():
        gq_ring[0](3)
        grad_of_out()
        gq_ring[0](4)
        grad_of_query()

    f_ex[1]()
    r_ex[1]()
    feature = jnp.zeros((BLOCK, part), F32)
    for p in range(n_tp):
        feature = feature + feat_in[p].astype(F32)
    inv = inv_b[:, :1]
    gain = gain_ref[:, pl.ds(pl.multiple_of(t * part, part), part)]
    scaled = feature * gain
    normed = x_ref[...].astype(F32) * inv
    total = rs_in[0]
    for p in range(1, n_tp):
        total = total + rs_in[p]
    mean = jnp.broadcast_to(total[:1] / width, (BLOCK, BLOCK)).T[:, :1]
    gin_ref[...] = (cotfull[t].astype(F32) + inv * (scaled - normed * mean)).astype(BF16)

    @pl.when(s == 1)
    def _():
        @pl.loop(0, n_tp)
        def _(i):
            sec_copy(lax.rem(t + i, n_tp)).start()

        send_cot()
        for k in range(1, n_z // 2 + 1):
            att_ring[0](k)
            gq_ring[0](k)
        pass_cot()
        grad_of_out()
        grad_of_query()

    kz_ex[1]()
    weight_part(gkv_z, y_out_k, gqkv_ref, heads, y_copies[2])
    for y_in, out, base, copy in (
        (y_in_o, gout_ref, 0, y_copies[0]),
        (y_in_q, gqkv_ref, 0, y_copies[1]),
        (y_in_k, gqkv_ref, heads, y_copies[2]),
    ):
        copy.wait_recv()
        out[:, base : base + y_in.shape[1]] += y_in[...].astype(F32)

    for ex in (x_ex, f_ex, r_ex, h1_ex, h2_ex, c1_ex, c2_ex, kz_ex, att_ring, gq_ring):
        ex[2]()
    for copy in y_copies:
        copy.wait_send()

    @pl.loop(1, steps_z)
    def _(k):
        @pl.when(z + k < n_z)
        def _():
            kv_up(k).wait_send()

        @pl.when(z - k >= 0)
        def _():
            kv_on(k).wait_send()

    @pl.when((lo == 1) & (c + far < n_ctx))
    def _():
        kv_far().wait_send()

    @pl.when(lo == 0)
    def _():
        kv_on(0).wait_send()

    @pl.loop(1, window)
    def _(d):
        @pl.when(c - d >= 0)
        def _():
            dkv_copy(d).wait_send()

    @pl.when(s == 1)
    def _():
        c_ex[2]()

        @pl.loop(0, n_tp)
        def _(p):
            sec_copy(p).wait_send()


def settle(a_in, b_in, c_in, a_out, b_out, c_out, sem):
    copies = [
        pltpu.make_async_copy(source, target, sem.at[i])
        for i, (source, target) in enumerate(((a_in, a_out), (b_in, b_out), (c_in, c_out)))
    ]
    for copy in copies:
        copy.start()
    for copy in copies:
        copy.wait()


def body(layer_input, loss_cot, token_weights, doc_blocks, norm_gain, qkv_weight, out_weight):
    n_ctx, n_tp = lax.axis_size("ctx"), lax.axis_size("tp")
    n_z = n_ctx // 2
    part = layer_input.shape[3]
    width = part * n_tp
    cols, heads = qkv_weight.shape[2], out_weight.shape[2]
    window = min(MAX_DOC, n_ctx)
    q_rows = GROUP_HEADS * BLOCK
    kv_cols = 2 * HEAD_SIZE
    half = part // 2
    share = BLOCK // n_tp
    vmem = lambda shape, dtype=BF16: pltpu.VMEM(shape, dtype)
    dma = lambda *n: pltpu.SemaphoreType.DMA(n)
    scratch = [
        vmem((width, cols)), vmem((width, heads)),
        vmem((n_tp, BLOCK, part)), vmem((n_tp, BLOCK, part)), vmem((BLOCK, part)), vmem((BLOCK, BLOCK), F32),
        vmem((window * BLOCK, kv_cols)),
        vmem((q_rows, HEAD_SIZE)), vmem((q_rows, HEAD_SIZE)), vmem((q_rows, HEAD_SIZE)),
        vmem((BLOCK, heads)), vmem((BLOCK, kv_cols)),
        vmem((window // 2, q_rows, 2 * BLOCK), F32), vmem((window // 2, q_rows, 2 * BLOCK)),
        vmem((window // 2, q_rows, 2 * BLOCK)),
        vmem((q_rows, BLOCK), F32), vmem((q_rows, BLOCK), F32), vmem((q_rows, HEAD_SIZE), F32),
        vmem((window * BLOCK, kv_cols)), vmem((window, BLOCK, kv_cols)),
        vmem((n_tp, BLOCK, part), F32), vmem((n_tp, BLOCK, part)), vmem((n_tp, BLOCK, part)),
        vmem((8, BLOCK), F32), vmem((n_tp, 8, BLOCK), F32),
        vmem((n_z, share, part)), vmem((n_z, share, part)),
        vmem((n_z, n_tp, share, part)), vmem((n_z, n_tp, share, part)), vmem((n_z * BLOCK, heads)),
        vmem((n_z * BLOCK, heads)), vmem((n_z * BLOCK, kv_cols)), vmem((part, n_z * BLOCK)),
        vmem((half, heads)), vmem((half, heads)), vmem((half, kv_cols)),
        vmem((half, heads)), vmem((half, heads)), vmem((half, kv_cols)),
        dma(2), dma(n_tp), dma(n_tp), dma(n_tp), dma(n_tp), dma(window), dma(window), dma(1), dma(window), dma(window),
        dma(n_tp), dma(n_tp), dma(n_tp), dma(n_tp),
        dma(n_z), dma(n_z), dma(n_tp), dma(n_tp), dma(n_z), dma(n_z), dma(n_tp), dma(n_tp),
        dma(n_z), dma(n_z), dma(n_z), dma(n_z), dma(n_z), dma(n_z),
        dma(3), dma(3), dma(n_tp), pltpu.SemaphoreType.REGULAR,
    ]
    in_vmem = pl.BlockSpec(memory_space=pltpu.VMEM)
    anywhere = pl.BlockSpec(memory_space=pl.ANY)
    grad_in, grad_qkv, grad_out = pl.pallas_call(
        functools.partial(kernel, n_ctx, n_tp, window),
        out_shape=(
            jax.ShapeDtypeStruct((BLOCK, part), BF16),
            jax.ShapeDtypeStruct((half, cols), F32),
            jax.ShapeDtypeStruct((half, heads), F32),
        ),
        in_specs=[
            in_vmem, in_vmem, in_vmem, pl.BlockSpec(memory_space=pltpu.SMEM), in_vmem, anywhere, anywhere,
        ],
        out_specs=(in_vmem, in_vmem, in_vmem),
        scratch_shapes=scratch,
        compiler_params=pltpu.CompilerParams(
            collective_id=0, has_side_effects=True, vmem_limit_bytes=56 * 1024 * 1024
        ),
    )(
        layer_input[0, 0], loss_cot[0], token_weights, doc_blocks, norm_gain, qkv_weight[0], out_weight[0]
    )
    results = (grad_in, grad_qkv, grad_out)
    grad_in, grad_qkv, grad_out = pl.pallas_call(
        settle,
        out_shape=tuple(jax.ShapeDtypeStruct(r.shape, r.dtype) for r in results),
        in_specs=[in_vmem] * 3,
        out_specs=(anywhere,) * 3,
        scratch_shapes=[dma(3)],
    )(*results)
    return grad_in[None, None], grad_qkv[None], grad_out[None]


def solution(mesh):
    placed = (
        P("section", None, "ctx", "tp"),
        P(None, "ctx", "tp"),
        P(None, "ctx"),
        P(),
        P("section", None),
        P("section", None, "tp"),
        P("section", None, "tp"),
    )
    return jax.shard_map(
        body,
        mesh=mesh,
        in_specs=placed,
        out_specs=(
            P("section", None, "ctx", "tp"),
            P("section", "ctx", "tp"),
            P("section", "ctx", "tp"),
        ),
        check_vma=False,
    )
```

```python
import functools

import jax
import jax.numpy as jnp
from jax import lax
from jax.experimental import pallas as pl
from jax.experimental.pallas import tpu as pltpu
from jax.sharding import PartitionSpec as P

MESH = pl.DeviceIdType.MESH
GROUP_HEADS = 4
HEAD_SIZE = 128
BLOCK = 128
MAX_DOC = 10
EPSILON = 1e-05
NEG_FILL = -1e30
F32 = jnp.float32
BF16 = jnp.bfloat16

NN = (((1,), (0,)), ((), ()))
NT = (((1,), (1,)), ((), ()))
TN = (((0,), (0,)), ((), ()))


def mm(a, b, dims=NN):
    return lax.dot_general(a, b, dims, preferred_element_type=F32)


def kernel(
    n_ctx, n_tp, window,
    x_ref, loss_ref, tw_ref, docs_ref, gain_ref, wq_hbm, wo_hbm,
    gin_ref, gqkv_ref, gout_ref,
    wq, wo, xfull, cotfull, cot_loc, inv_b,
    kv, q_s, hc_s, att_s, gq_n, gkv_n, scores, probs, dscores, peak, denom, acc, row_acc,
    dkv_part, dkv_in, dkv_mate, dkv_sum, feat_f, feat_out, feat_in, rs_out, rs_in,
    hid_p, cot_p, hid_z, cot_z, att_z, gq_z, gkv_z, turned,
    y_out_o, y_out_q, y_out_k, y_in_o, y_in_q, y_in_k,
    w_sem, x_s, x_r, c_s, c_r, kv_s, kv_r, kv_f, d_s, d_r, f_s, f_r, r_s, r_r,
    h1_s, h1_r, h2_s, h2_r, c1_s, c1_r, c2_s, c2_r, az_s, az_r, qz_s, qz_r, kz_s, kz_r, y_s, y_r, sec_s, m_s, m_r, gate,
):
    s = lax.axis_index("section")
    c = lax.axis_index("ctx")
    t = lax.axis_index("tp")
    n_z = n_ctx // 2
    z, lo = c // 2, lax.rem(c, 2)
    part = x_ref.shape[1]
    width = part * n_tp
    half = part // 2
    heads = GROUP_HEADS * HEAD_SIZE
    cols = heads + 2 * HEAD_SIZE
    scale = HEAD_SIZE ** (-0.5)
    last = window - 1

    def remote(src, dst, ss, rs, dev):
        return pltpu.make_async_remote_copy(
            src_ref=src, dst_ref=dst, send_sem=ss, recv_sem=rs, device_id=dev, device_id_type=MESH
        )

    def tp_dev(p):
        return {"tp": p}

    def z_dev(p):
        return {"ctx": p * 2 + lo}

    def exchange(n, me, dev, src_of, slot, ss, rs):
        def copy_to(p):
            return remote(src_of(p), slot(me), ss.at[p], rs.at[me], dev(p))

        def copy_from(p):
            return remote(slot(p), slot(p), ss.at[p], rs.at[p], dev(p))

        def start():
            @pl.loop(1, n)
            def _(i):
                copy_to(lax.rem(me + i, n)).start()

        def wait_recv():
            @pl.loop(1, n)
            def _(i):
                copy_from(lax.rem(me + i, n)).wait_recv()

        def wait_send():
            @pl.loop(1, n)
            def _(i):
                copy_to(lax.rem(me + i, n)).wait_send()

        return start, wait_recv, wait_send, copy_to

    def ring(ref, ss, rs):
        up, down = z_dev(lax.rem(z + 1, n_z)), z_dev(lax.rem(z + n_z - 1, n_z))
        top = n_z // 2

        def piece(p, k, side):
            if k < top:
                return ref.at[pl.ds(p * BLOCK, BLOCK)]
            return ref.at[pl.ds(p * BLOCK + side * (BLOCK // 2), BLOCK // 2)]

        def pair(k, shift):
            below = piece(lax.rem(z - k + shift + n_z, n_z), k, 0)
            above = piece(lax.rem(z + k - shift, n_z), k, 1)
            return (
                remote(below, below, ss.at[k - 1], rs.at[k - 1], up),
                remote(above, above, ss.at[top + k - 1], rs.at[top + k - 1], down),
            )

        def arrive(k):
            for copy in pair(k, 0):
                copy.wait_recv()

        def stage(k):
            if k > top:
                return
            if k > 1:
                arrive(k - 1)
            for copy in pair(k, 1):
                copy.start()

        def wait_send():
            for k in range(1, top + 1):
                for copy in pair(k, 1):
                    copy.wait_send()

        return stage, lambda: arrive(top), wait_send

    whole = lambda ref: lambda p: ref
    share = BLOCK // n_tp
    my_rows = pl.ds(pl.multiple_of(t * share, share), share)

    x_ex = exchange(n_tp, t, tp_dev, whole(x_ref), lambda p: xfull.at[p], x_s, x_r)
    c_ex = exchange(n_tp, t, tp_dev, whole(cot_loc), lambda p: cotfull.at[p], c_s, c_r)
    f_ex = exchange(n_tp, t, tp_dev, lambda p: feat_out.at[p], lambda p: feat_in.at[p], f_s, f_r)
    r_ex = exchange(n_tp, t, tp_dev, whole(rs_out), lambda p: rs_in.at[p], r_s, r_r)
    h1_ex = exchange(n_z, z, z_dev, lambda p: xfull.at[p, my_rows], lambda p: hid_p.at[p], h1_s, h1_r)
    h2_ex = exchange(n_tp, t, tp_dev, whole(hid_p), lambda p: hid_z.at[:, p], h2_s, h2_r)
    c1_ex = exchange(n_z, z, z_dev, lambda p: cotfull.at[p, my_rows], lambda p: cot_p.at[p], c1_s, c1_r)
    c2_ex = exchange(n_tp, t, tp_dev, whole(cot_p), lambda p: cot_z.at[:, p], c2_s, c2_r)
    att_ring = ring(att_z, az_s, az_r)
    gq_ring = ring(gq_z, qz_s, qz_r)
    kz_ex = exchange(n_z, z, z_dev, whole(gkv_n), lambda p: gkv_z.at[pl.ds(p * BLOCK, BLOCK)], kz_s, kz_r)
    own_z = pl.ds(pl.multiple_of(z * BLOCK, BLOCK), BLOCK)
    wq_copy = pltpu.make_async_copy(wq_hbm, wq, w_sem.at[0])
    wo_copy = pltpu.make_async_copy(wo_hbm, wo, w_sem.at[1])

    wq_copy.start()
    wo_copy.start()
    kv[...] = jnp.zeros_like(kv)

    barrier = pltpu.get_barrier_semaphore()

    @pl.loop(1, n_tp)
    def _(i):
        pl.semaphore_signal(barrier, inc=1, device_id={"tp": lax.rem(t + i, n_tp)}, device_id_type=MESH)

    @pl.loop(1, n_ctx)
    def _(i):
        pl.semaphore_signal(barrier, inc=1, device_id={"ctx": lax.rem(c + i, n_ctx)}, device_id_type=MESH)

    @pl.loop(0, n_tp)
    def _(p):
        pl.semaphore_signal(barrier, inc=1, device_id={"section": 1 - s, "tp": p}, device_id_type=MESH)

    pl.semaphore_wait(barrier, 2 * n_tp + n_ctx - 2)

    @pl.when(s == 0)
    def _():
        pl.semaphore_wait(gate, 1)

    x_ex[0]()
    xfull[t] = x_ref[...]

    @pl.when(s == 1)
    def _():
        weights = jnp.broadcast_to(tw_ref[...].astype(F32), (BLOCK, BLOCK)).T[:, :1]
        cot_loc[...] = (loss_ref[...].astype(F32) * weights).astype(BF16)
        cotfull[t] = cot_loc[...]
        c_ex[0]()

    x_ex[1]()

    @pl.when(s == 1)
    def _():
        pl.semaphore_signal(gate, inc=1, device_id={"section": 1 - s}, device_id_type=MESH)

    square = jnp.zeros((BLOCK, part), F32)
    for p in range(n_tp):
        wide = xfull[p].astype(F32)
        square = square + wide * wide
    inv = lax.rsqrt(jnp.sum(square, axis=1, keepdims=True) / width + EPSILON)
    inv_b[...] = jnp.broadcast_to(inv, inv_b.shape)
    for p in range(n_tp):
        gain = gain_ref[:, p * part : (p + 1) * part]
        xfull[p] = ((xfull[p].astype(F32) * inv) * gain).astype(BF16)

    def project(full, weight, lo_col, n_col):
        total = jnp.zeros((BLOCK, n_col), F32)
        for p in range(n_tp):
            total = total + mm(full[p], weight[p * part : (p + 1) * part, lo_col : lo_col + n_col])
        return total.astype(BF16)

    def slot(j):
        if isinstance(j, int):
            return pl.ds(j * BLOCK, BLOCK)
        return pl.ds(pl.multiple_of(j * BLOCK, BLOCK), BLOCK)

    wq_copy.wait()
    kv[slot(last)] = project(xfull, wq, heads, 2 * HEAD_SIZE)

    steps_z = (window - 1) // 2 + 1
    mate = {"ctx": z * 2 + 1 - lo}
    far = window - 1

    def kv_up(k):
        return remote(
            kv.at[slot(last)], kv.at[slot(last - 2 * k)], kv_s.at[2 * k], kv_r.at[2 * k],
            {"ctx": lax.rem(c + 2 * k, n_ctx)},
        )

    def kv_on(k):
        away = 2 * k + 1 - 2 * lo
        return remote(
            kv.at[slot(last - 2 * k)], kv.at[slot(last - away)], kv_s.at[2 * k + 1], kv_r.at[away], mate
        )

    def kv_far():
        return remote(
            kv.at[slot(last)], kv.at[slot(last - far)], kv_f.at[0], kv_r.at[far],
            {"ctx": lax.rem(c + far, n_ctx)},
        )

    def kv_arrival(d):
        return remote(
            kv.at[slot(last - d)], kv.at[slot(last - d)], kv_s.at[0], kv_r.at[d], mate
        )

    @pl.loop(1, steps_z)
    def _(i):
        k = steps_z - i

        @pl.when(z + k < n_z)
        def _():
            kv_up(k).start()

    @pl.when((lo == 1) & (c + far < n_ctx))
    def _():
        kv_far().start()

    @pl.when(lo == 0)
    def _():
        kv_on(0).start()

    for j in range(0, GROUP_HEADS, 2):
        pair = project(xfull, wq, j * HEAD_SIZE, 2 * HEAD_SIZE)
        q_s[j * BLOCK : (j + 1) * BLOCK] = pair[:, :HEAD_SIZE]
        q_s[(j + 1) * BLOCK : (j + 2) * BLOCK] = pair[:, HEAD_SIZE:]
    h1_ex[0]()
    hid_p[z] = xfull[z, my_rows]

    def pass_hidden():
        h1_ex[1]()
        h2_ex[0]()
        hid_z[:, t] = hid_p[...]

    def head_cotangent():
        wo_copy.wait()
        for j in range(0, GROUP_HEADS, 2):
            pair = project(cotfull, wo, j * HEAD_SIZE, 2 * HEAD_SIZE)
            hc_s[j * BLOCK : (j + 1) * BLOCK] = pair[:, :HEAD_SIZE]
            hc_s[(j + 1) * BLOCK : (j + 2) * BLOCK] = pair[:, HEAD_SIZE:]

    @pl.loop(1, steps_z)
    def _(k):
        @pl.when(z - k >= 0)
        def _():
            kv_up(k).wait_recv()
            kv_on(k).start()

    @pl.when(s == 0)
    def _():
        pass_hidden()

    @pl.when(s == 1)
    def _():
        c_ex[1]()
        head_cotangent()

    doc_start = jnp.int32(0)
    doc_end = jnp.int32(0)
    for i in range(docs_ref.shape[1]):
        doc_end = doc_end + docs_ref[0, i]
        doc_start = jnp.where(doc_end <= c, doc_end, doc_start)
    pairs = window // 2
    wide = (GROUP_HEADS * BLOCK, 2 * BLOCK)
    query_pos = c * BLOCK + lax.broadcasted_iota(jnp.int32, wide, 0) % BLOCK
    first_key = (c - last) * BLOCK + lax.broadcasted_iota(jnp.int32, wide, 1)

    def keys(g):
        return kv[g * 2 * BLOCK : (g + 1) * 2 * BLOCK, :HEAD_SIZE]

    def values(g):
        return kv[g * 2 * BLOCK : (g + 1) * 2 * BLOCK, HEAD_SIZE:]

    for g in range(pairs - 1, -1, -1):
        for j in (2 * g + 1, 2 * g):
            if j < last:

                if (last - j) % 2 == 1:

                    @pl.when(c - last + j >= 0)
                    def _():
                        kv_arrival(last - j).wait_recv()

        block = mm(q_s[...], keys(g), NT) * scale
        key_pos = first_key + g * 2 * BLOCK
        block = jnp.where((key_pos <= query_pos) & (key_pos >= doc_start * BLOCK), block, NEG_FILL)
        scores[g] = block
        both = jnp.maximum(block[:, :BLOCK], block[:, BLOCK:])
        peak[...] = both if g == pairs - 1 else jnp.maximum(peak[...], both)

    top = jnp.max(peak[...], axis=1, keepdims=True)
    for g in range(pairs):
        e = jnp.exp(scores[g] - top)
        scores[g] = e
        both = e[:, :BLOCK] + e[:, BLOCK:]
        denom[...] = both if g == 0 else denom[...] + both

    inverse = 1.0 / jnp.sum(denom[...], axis=1, keepdims=True)
    for g in range(pairs):
        soft = scores[g] * inverse
        low = soft.astype(BF16)
        scores[g] = soft
        probs[g] = low
        term = mm(low, values(g))
        acc[...] = term if g == 0 else acc[...] + term

    att_s[...] = acc[...].astype(BF16)
    for j in range(GROUP_HEADS):
        att_z[own_z, j * HEAD_SIZE : (j + 1) * HEAD_SIZE] = att_s[j * BLOCK : (j + 1) * BLOCK]

    def sec_copy(p):
        return remote(gin_ref, cotfull.at[t], sec_s.at[p], c_r.at[t], {"section": 1 - s, "tp": p})

    @pl.when(s == 1)
    def _():
        pass_hidden()

    @pl.when(s == 0)
    def _():
        for k in range(1, n_z // 2 + 1):
            att_ring[0](k)

        @pl.loop(0, n_tp)
        def _(p):
            remote(cotfull.at[p], cotfull.at[p], sec_s.at[p], c_r.at[p], {"section": 1 - s}).wait_recv()

        head_cotangent()

    delta = jnp.sum(hc_s[...].astype(F32) * att_s[...].astype(F32), axis=1, keepdims=True)

    def dkv_mate_copy(d, k):
        return remote(dkv_part.at[slot(last - d)], dkv_mate.at[k], m_s.at[k], m_r.at[k], mate)

    def dkv_next():
        return remote(dkv_part.at[slot(last - 1)], dkv_in.at[0], d_s.at[0], d_r.at[0], mate)

    def dkv_far():
        return remote(
            dkv_part.at[slot(0)], dkv_in.at[steps_z], d_s.at[steps_z], d_r.at[steps_z],
            {"ctx": lax.rem(c - far + n_ctx, n_ctx)},
        )

    def dkv_down(k):
        return remote(
            dkv_sum.at[k], dkv_in.at[k], d_s.at[k], d_r.at[k], {"ctx": lax.rem(c - 2 * k + n_ctx, n_ctx)}
        )

    def dkv_send_mate(d):
        for side in (0, 1):
            k = (d + 1) // 2 - side

            @pl.when(lo == side)
            def _():
                if k == steps_z:

                    @pl.when(c - far >= 0)
                    def _():
                        dkv_far().start()

                elif k == 0:
                    dkv_next().start()
                else:

                    @pl.when(z - k >= 0)
                    def _():
                        dkv_mate_copy(d, k).start()

    def dkv_add(k):
        @pl.when(z - k >= 0)
        def _():
            dkv_mate_copy(1, k).wait_recv()
            own_part = dkv_part[slot(last - 2 * k)].astype(F32)
            dkv_sum[k] = (own_part + dkv_mate[k].astype(F32)).astype(BF16)
            dkv_down(k).start()

    for g in range(pairs):
        block = slice(g * 2 * BLOCK, (g + 1) * 2 * BLOCK)
        dprobs = mm(hc_s[...], values(g), NT)
        ds = (scores[g] * (dprobs - delta)).astype(BF16)
        dkv_part[block, :HEAD_SIZE] = (mm(ds, q_s[...], TN) * scale).astype(BF16)
        dkv_part[block, HEAD_SIZE:] = mm(probs[g], hc_s[...], TN).astype(BF16)
        dscores[g] = ds
        dkv_send_mate(last - 2 * g)
        if g >= 2:
            dkv_add(pairs + 1 - g)

    dkv_add(1)
    total = mm(dscores[0], keys(0))
    for g in range(1, pairs):
        total = total + mm(dscores[g], keys(g))
    acc[...] = total
    for j in range(GROUP_HEADS):
        gq_n[:, j * HEAD_SIZE : (j + 1) * HEAD_SIZE] = (
            acc[j * BLOCK : (j + 1) * BLOCK] * scale
        ).astype(BF16)
    gq_z[own_z] = gq_n[...]

    def send_cot():
        c1_ex[0]()
        cot_p[z] = cotfull[z, my_rows]

    def pass_cot():
        c1_ex[1]()
        c2_ex[0]()
        cot_z[:, t] = cot_p[...]

    @pl.when(s == 0)
    def _():
        send_cot()
        gq_ring[0](1)

    @pl.loop(0, n_tp)
    def _(p):
        feat_f[p] = mm(gq_n[...], wq[pl.ds(p * part, part), :heads], NT)

    @pl.when(s == 0)
    def _():
        pass_cot()
        gq_ring[0](2)

    acc[:BLOCK] = dkv_part[slot(last), :HEAD_SIZE].astype(F32)
    acc[BLOCK : 2 * BLOCK] = dkv_part[slot(last), HEAD_SIZE:].astype(F32)

    def dkv_take(copy, k):
        copy.wait_recv()
        acc[:BLOCK] += dkv_in[k, :, :HEAD_SIZE].astype(F32)
        acc[BLOCK : 2 * BLOCK] += dkv_in[k, :, HEAD_SIZE:].astype(F32)

    @pl.when(lo == 0)
    def _():
        dkv_take(dkv_next(), 0)

    @pl.loop(1, steps_z)
    def _(k):
        @pl.when(z + k < n_z)
        def _():
            dkv_take(dkv_down(k), k)

    @pl.when((lo == 1) & (c + far < n_ctx))
    def _():
        dkv_take(dkv_far(), steps_z)

    gkv_n[:, :HEAD_SIZE] = acc[:BLOCK].astype(BF16)
    gkv_n[:, HEAD_SIZE:] = acc[BLOCK : 2 * BLOCK].astype(BF16)
    gkv_z[own_z] = gkv_n[...]
    kz_ex[0]()
    row_acc[...] = jnp.zeros_like(row_acc)

    @pl.loop(1, n_tp + 1)
    def _(i):
        p = lax.rem(t + i, n_tp)
        total = feat_f[p] + mm(gkv_n[...], wq[pl.ds(p * part, part), heads:], NT)
        total = total.astype(BF16)
        feat_out[p] = total
        row_acc[...] += total.astype(F32) * xfull[p].astype(F32)

        @pl.when(i < n_tp)
        def _():
            f_ex[3](p).start()

    row_sum = jnp.sum(row_acc[...], axis=1, keepdims=True)
    rs_out[...] = jnp.broadcast_to(row_sum, (BLOCK, BLOCK)).T[:8]
    r_ex[0]()
    rs_in[t] = rs_out[...]
    feat_in[t] = feat_out[t]

    y_copies = [
        remote(y_out_o, y_in_o, y_s.at[0], y_r.at[0], mate),
        remote(y_out_q, y_in_q, y_s.at[1], y_r.at[1], mate),
        remote(y_out_k, y_in_k, y_s.at[2], y_r.at[2], mate),
    ]
    positions = n_z * BLOCK
    theirs = pl.ds(pl.multiple_of((1 - lo) * half, half), half)
    mine = pl.ds(pl.multiple_of(lo * half, half), half)

    def turn(ref):
        turned[...] = ref[...].reshape(positions, part).T

    def weight_part(right, y_out, out, base, copy):
        step = min(256, heads)
        for k in range(0, right.shape[1], step):
            y_out[:, k : k + step] = mm(turned[theirs], right[:, k : k + step]).astype(BF16)
        copy.start()
        for k in range(0, right.shape[1], step):
            out[:, base + k : base + k + step] = mm(turned[mine], right[:, k : k + step])

    def grad_of_out():
        c2_ex[1]()
        att_ring[1]()
        turn(cot_z)
        weight_part(att_z, y_out_o, gout_ref, 0, y_copies[0])

    def grad_of_query():
        h2_ex[1]()
        turn(hid_z)
        gq_ring[1]()
        weight_part(gq_z, y_out_q, gqkv_ref, 0, y_copies[1])

    @pl.when(s == 0)
    def _():
        gq_ring[0](3)
        grad_of_out()
        gq_ring[0](4)
        grad_of_query()

    f_ex[1]()
    r_ex[1]()
    feature = jnp.zeros((BLOCK, part), F32)
    for p in range(n_tp):
        feature = feature + feat_in[p].astype(F32)
    inv = inv_b[:, :1]
    gain = gain_ref[:, pl.ds(pl.multiple_of(t * part, part), part)]
    scaled = feature * gain
    normed = x_ref[...].astype(F32) * inv
    total = rs_in[0]
    for p in range(1, n_tp):
        total = total + rs_in[p]
    mean = jnp.broadcast_to(total[:1] / width, (BLOCK, BLOCK)).T[:, :1]
    gin_ref[...] = (cotfull[t].astype(F32) + inv * (scaled - normed * mean)).astype(BF16)

    @pl.when(s == 1)
    def _():
        @pl.loop(0, n_tp)
        def _(i):
            sec_copy(lax.rem(t + 1 + i, n_tp)).start()

        send_cot()
        for k in range(1, n_z // 2 + 1):
            att_ring[0](k)
            gq_ring[0](k)
            if k == 2 or n_z == 2:
                pass_cot()
        grad_of_out()
        grad_of_query()

    kz_ex[1]()
    weight_part(gkv_z, y_out_k, gqkv_ref, heads, y_copies[2])
    for y_in, out, base, copy in (
        (y_in_o, gout_ref, 0, y_copies[0]),
        (y_in_q, gqkv_ref, 0, y_copies[1]),
        (y_in_k, gqkv_ref, heads, y_copies[2]),
    ):
        copy.wait_recv()
        out[:, base : base + y_in.shape[1]] += y_in[...].astype(F32)

    for ex in (x_ex, f_ex, r_ex, h1_ex, h2_ex, c1_ex, c2_ex, kz_ex, att_ring, gq_ring):
        ex[2]()
    for copy in y_copies:
        copy.wait_send()

    @pl.loop(1, steps_z)
    def _(k):
        @pl.when(z + k < n_z)
        def _():
            kv_up(k).wait_send()

        @pl.when(z - k >= 0)
        def _():
            kv_on(k).wait_send()

    @pl.when((lo == 1) & (c + far < n_ctx))
    def _():
        kv_far().wait_send()

    @pl.when(lo == 0)
    def _():
        kv_on(0).wait_send()

    @pl.loop(1, steps_z)
    def _(k):
        @pl.when(z - k >= 0)
        def _():
            dkv_mate_copy(1, k).wait_send()
            dkv_down(k).wait_send()

    @pl.when(lo == 1)
    def _():
        dkv_next().wait_send()

    @pl.when((lo == 0) & (c - far >= 0))
    def _():
        dkv_far().wait_send()

    @pl.when(s == 1)
    def _():
        c_ex[2]()

        @pl.loop(0, n_tp)
        def _(p):
            sec_copy(p).wait_send()


def settle(a_in, b_in, c_in, a_out, b_out, c_out, sem):
    copies = [
        pltpu.make_async_copy(source, target, sem.at[i])
        for i, (source, target) in enumerate(((a_in, a_out), (b_in, b_out), (c_in, c_out)))
    ]
    for copy in copies:
        copy.start()
    for copy in copies:
        copy.wait()


def body(layer_input, loss_cot, token_weights, doc_blocks, norm_gain, qkv_weight, out_weight):
    n_ctx, n_tp = lax.axis_size("ctx"), lax.axis_size("tp")
    n_z = n_ctx // 2
    part = layer_input.shape[3]
    width = part * n_tp
    cols, heads = qkv_weight.shape[2], out_weight.shape[2]
    window = min(MAX_DOC, n_ctx)
    q_rows = GROUP_HEADS * BLOCK
    kv_cols = 2 * HEAD_SIZE
    half = part // 2
    share = BLOCK // n_tp
    vmem = lambda shape, dtype=BF16: pltpu.VMEM(shape, dtype)
    dma = lambda *n: pltpu.SemaphoreType.DMA(n)
    scratch = [
        vmem((width, cols)), vmem((width, heads)),
        vmem((n_tp, BLOCK, part)), vmem((n_tp, BLOCK, part)), vmem((BLOCK, part)), vmem((BLOCK, BLOCK), F32),
        vmem((window * BLOCK, kv_cols)),
        vmem((q_rows, HEAD_SIZE)), vmem((q_rows, HEAD_SIZE)), vmem((q_rows, HEAD_SIZE)),
        vmem((BLOCK, heads)), vmem((BLOCK, kv_cols)),
        vmem((window // 2, q_rows, 2 * BLOCK), F32), vmem((window // 2, q_rows, 2 * BLOCK)),
        vmem((window // 2, q_rows, 2 * BLOCK)),
        vmem((q_rows, BLOCK), F32), vmem((q_rows, BLOCK), F32), vmem((q_rows, HEAD_SIZE), F32), vmem((BLOCK, part), F32),
        vmem((window * BLOCK, kv_cols)), vmem((window, BLOCK, kv_cols)),
        vmem((window // 2, BLOCK, kv_cols)), vmem((window // 2, BLOCK, kv_cols)),
        vmem((n_tp, BLOCK, part), F32), vmem((n_tp, BLOCK, part)), vmem((n_tp, BLOCK, part)),
        vmem((8, BLOCK), F32), vmem((n_tp, 8, BLOCK), F32),
        vmem((n_z, share, part)), vmem((n_z, share, part)),
        vmem((n_z, n_tp, share, part)), vmem((n_z, n_tp, share, part)), vmem((n_z * BLOCK, heads)),
        vmem((n_z * BLOCK, heads)), vmem((n_z * BLOCK, kv_cols)), vmem((part, n_z * BLOCK)),
        vmem((half, heads)), vmem((half, heads)), vmem((half, kv_cols)),
        vmem((half, heads)), vmem((half, heads)), vmem((half, kv_cols)),
        dma(2), dma(n_tp), dma(n_tp), dma(n_tp), dma(n_tp), dma(window), dma(window), dma(1), dma(window), dma(window),
        dma(n_tp), dma(n_tp), dma(n_tp), dma(n_tp),
        dma(n_z), dma(n_z), dma(n_tp), dma(n_tp), dma(n_z), dma(n_z), dma(n_tp), dma(n_tp),
        dma(n_z), dma(n_z), dma(n_z), dma(n_z), dma(n_z), dma(n_z),
        dma(3), dma(3), dma(n_tp), dma(window), dma(window), pltpu.SemaphoreType.REGULAR,
    ]
    in_vmem = pl.BlockSpec(memory_space=pltpu.VMEM)
    anywhere = pl.BlockSpec(memory_space=pl.ANY)
    grad_in, grad_qkv, grad_out = pl.pallas_call(
        functools.partial(kernel, n_ctx, n_tp, window),
        out_shape=(
            jax.ShapeDtypeStruct((BLOCK, part), BF16),
            jax.ShapeDtypeStruct((half, cols), F32),
            jax.ShapeDtypeStruct((half, heads), F32),
        ),
        in_specs=[
            in_vmem, in_vmem, in_vmem, pl.BlockSpec(memory_space=pltpu.SMEM), in_vmem, anywhere, anywhere,
        ],
        out_specs=(in_vmem, in_vmem, in_vmem),
        scratch_shapes=scratch,
        compiler_params=pltpu.CompilerParams(
            collective_id=0, has_side_effects=True, vmem_limit_bytes=56 * 1024 * 1024
        ),
    )(
        layer_input[0, 0], loss_cot[0], token_weights, doc_blocks, norm_gain, qkv_weight[0], out_weight[0]
    )
    results = (grad_in, grad_qkv, grad_out)
    grad_in, grad_qkv, grad_out = pl.pallas_call(
        settle,
        out_shape=tuple(jax.ShapeDtypeStruct(r.shape, r.dtype) for r in results),
        in_specs=[in_vmem] * 3,
        out_specs=(anywhere,) * 3,
        scratch_shapes=[dma(3)],
    )(*results)
    return grad_in[None, None], grad_qkv[None], grad_out[None]


def solution(mesh):
    placed = (
        P("section", None, "ctx", "tp"),
        P(None, "ctx", "tp"),
        P(None, "ctx"),
        P(),
        P("section", None),
        P("section", None, "tp"),
        P("section", None, "tp"),
    )
    return jax.shard_map(
        body,
        mesh=mesh,
        in_specs=placed,
        out_specs=(
            P("section", None, "ctx", "tp"),
            P("section", "ctx", "tp"),
            P("section", "ctx", "tp"),
        ),
        check_vma=False,
    )
```

```python
import functools

import jax
import jax.numpy as jnp
from jax import lax
from jax.experimental import pallas as pl
from jax.experimental.pallas import tpu as pltpu
from jax.sharding import PartitionSpec as P

MESH = pl.DeviceIdType.MESH
GROUP_HEADS = 4
HEAD_SIZE = 128
BLOCK = 128
MAX_DOC = 10
EPSILON = 1e-05
NEG_FILL = -1e30
F32 = jnp.float32
BF16 = jnp.bfloat16

NN = (((1,), (0,)), ((), ()))
NT = (((1,), (1,)), ((), ()))
TN = (((0,), (0,)), ((), ()))


def mm(a, b, dims=NN):
    return lax.dot_general(a, b, dims, preferred_element_type=F32)


def kernel(
    n_ctx, n_tp, window,
    x_ref, loss_ref, tw_ref, docs_ref, gain_ref, wq_hbm, wo_hbm,
    gin_ref, gqkv_ref, gout_ref,
    wq, wo, xfull, cotfull, cot_loc, inv_b,
    kv, q_s, hc_s, att_s, gq_n, gkv_n, scores, probs, dscores, peak, denom, acc, row_acc,
    dkv_part, dkv_in, dkv_mate, dkv_sum, feat_f, feat_out, feat_in, rs_out, rs_in,
    hid_p, cot_p, hid_z, cot_z, att_z, gq_z, gkv_z, turned,
    y_out_o, y_out_q, y_out_k, y_in_o, y_in_q, y_in_k,
    w_sem, x_s, x_r, c_s, c_r, kv_s, kv_r, kv_f, d_s, d_r, f_s, f_r, r_s, r_r,
    h1_s, h1_r, h2_s, h2_r, c1_s, c1_r, c2_s, c2_r, az_s, az_r, qz_s, qz_r, kz_s, kz_r, y_s, y_r, sec_s, m_s, m_r, gate,
):
    s = lax.axis_index("section")
    c = lax.axis_index("ctx")
    t = lax.axis_index("tp")
    n_z = n_ctx // 2
    z, lo = c // 2, lax.rem(c, 2)
    part = x_ref.shape[1]
    width = part * n_tp
    half = part // 2
    heads = GROUP_HEADS * HEAD_SIZE
    cols = heads + 2 * HEAD_SIZE
    scale = HEAD_SIZE ** (-0.5)
    last = window - 1

    def remote(src, dst, ss, rs, dev):
        return pltpu.make_async_remote_copy(
            src_ref=src, dst_ref=dst, send_sem=ss, recv_sem=rs, device_id=dev, device_id_type=MESH
        )

    def tp_dev(p):
        return {"tp": p}

    def z_dev(p):
        return {"ctx": p * 2 + lo}

    def exchange(n, me, dev, src_of, slot, ss, rs):
        def copy_to(p):
            return remote(src_of(p), slot(me), ss.at[p], rs.at[me], dev(p))

        def copy_from(p):
            return remote(slot(p), slot(p), ss.at[p], rs.at[p], dev(p))

        def start():
            @pl.loop(1, n)
            def _(i):
                copy_to(lax.rem(me + i, n)).start()

        def wait_recv():
            @pl.loop(1, n)
            def _(i):
                copy_from(lax.rem(me + i, n)).wait_recv()

        def wait_send():
            @pl.loop(1, n)
            def _(i):
                copy_to(lax.rem(me + i, n)).wait_send()

        return start, wait_recv, wait_send, copy_to

    def ring(ref, ss, rs):
        up, down = z_dev(lax.rem(z + 1, n_z)), z_dev(lax.rem(z + n_z - 1, n_z))
        top = n_z // 2

        def piece(p, k, side):
            if k < top:
                return ref.at[pl.ds(p * BLOCK, BLOCK)]
            return ref.at[pl.ds(p * BLOCK + side * (BLOCK // 2), BLOCK // 2)]

        def pair(k, shift):
            below = piece(lax.rem(z - k + shift + n_z, n_z), k, 0)
            above = piece(lax.rem(z + k - shift, n_z), k, 1)
            return (
                remote(below, below, ss.at[k - 1], rs.at[k - 1], up),
                remote(above, above, ss.at[top + k - 1], rs.at[top + k - 1], down),
            )

        def arrive(k):
            for copy in pair(k, 0):
                copy.wait_recv()

        def stage(k):
            if k > top:
                return
            if k > 1:
                arrive(k - 1)
            for copy in pair(k, 1):
                copy.start()

        def wait_send():
            for k in range(1, top + 1):
                for copy in pair(k, 1):
                    copy.wait_send()

        return stage, lambda: arrive(top), wait_send

    whole = lambda ref: lambda p: ref
    share = BLOCK // n_tp
    my_rows = pl.ds(pl.multiple_of(t * share, share), share)

    x_ex = exchange(n_tp, t, tp_dev, whole(x_ref), lambda p: xfull.at[p], x_s, x_r)
    c_ex = exchange(n_tp, t, tp_dev, whole(cot_loc), lambda p: cotfull.at[p], c_s, c_r)
    f_ex = exchange(n_tp, t, tp_dev, lambda p: feat_out.at[p], lambda p: feat_in.at[p], f_s, f_r)
    r_ex = exchange(n_tp, t, tp_dev, whole(rs_out), lambda p: rs_in.at[p], r_s, r_r)
    h1_ex = exchange(n_z, z, z_dev, lambda p: xfull.at[p, my_rows], lambda p: hid_p.at[p], h1_s, h1_r)
    h2_ex = exchange(n_tp, t, tp_dev, whole(hid_p), lambda p: hid_z.at[:, p], h2_s, h2_r)
    c1_ex = exchange(n_z, z, z_dev, lambda p: cotfull.at[p, my_rows], lambda p: cot_p.at[p], c1_s, c1_r)
    c2_ex = exchange(n_tp, t, tp_dev, whole(cot_p), lambda p: cot_z.at[:, p], c2_s, c2_r)
    att_ring = ring(att_z, az_s, az_r)
    gq_ring = ring(gq_z, qz_s, qz_r)
    kz_ex = exchange(n_z, z, z_dev, whole(gkv_n), lambda p: gkv_z.at[pl.ds(p * BLOCK, BLOCK)], kz_s, kz_r)
    own_z = pl.ds(pl.multiple_of(z * BLOCK, BLOCK), BLOCK)
    wq_copy = pltpu.make_async_copy(wq_hbm, wq, w_sem.at[0])
    wo_copy = pltpu.make_async_copy(wo_hbm, wo, w_sem.at[1])

    wq_copy.start()
    wo_copy.start()
    kv[...] = jnp.zeros_like(kv)

    barrier = pltpu.get_barrier_semaphore()

    @pl.loop(1, n_tp)
    def _(i):
        pl.semaphore_signal(barrier, inc=1, device_id={"tp": lax.rem(t + i, n_tp)}, device_id_type=MESH)

    @pl.loop(1, n_ctx)
    def _(i):
        pl.semaphore_signal(barrier, inc=1, device_id={"ctx": lax.rem(c + i, n_ctx)}, device_id_type=MESH)

    @pl.loop(0, n_tp)
    def _(p):
        pl.semaphore_signal(barrier, inc=1, device_id={"section": 1 - s, "tp": p}, device_id_type=MESH)

    pl.semaphore_wait(barrier, 2 * n_tp + n_ctx - 2)

    @pl.when(s == 0)
    def _():
        pl.semaphore_wait(gate, 1)

    x_ex[0]()
    xfull[t] = x_ref[...]

    @pl.when(s == 1)
    def _():
        weights = jnp.broadcast_to(tw_ref[...].astype(F32), (BLOCK, BLOCK)).T[:, :1]
        cot_loc[...] = (loss_ref[...].astype(F32) * weights).astype(BF16)
        cotfull[t] = cot_loc[...]
        c_ex[0]()

    x_ex[1]()

    @pl.when(s == 1)
    def _():
        pl.semaphore_signal(gate, inc=1, device_id={"section": 1 - s}, device_id_type=MESH)

    square = jnp.zeros((BLOCK, part), F32)
    for p in range(n_tp):
        wide = xfull[p].astype(F32)
        square = square + wide * wide
    inv = lax.rsqrt(jnp.sum(square, axis=1, keepdims=True) / width + EPSILON)
    inv_b[...] = jnp.broadcast_to(inv, inv_b.shape)
    for p in range(n_tp):
        gain = gain_ref[:, p * part : (p + 1) * part]
        xfull[p] = ((xfull[p].astype(F32) * inv) * gain).astype(BF16)

    def project(full, weight, lo_col, n_col):
        total = jnp.zeros((BLOCK, n_col), F32)
        for p in range(n_tp):
            total = total + mm(full[p], weight[p * part : (p + 1) * part, lo_col : lo_col + n_col])
        return total.astype(BF16)

    def slot(j):
        if isinstance(j, int):
            return pl.ds(j * BLOCK, BLOCK)
        return pl.ds(pl.multiple_of(j * BLOCK, BLOCK), BLOCK)

    wq_copy.wait()
    kv[slot(last)] = project(xfull, wq, heads, 2 * HEAD_SIZE)

    steps_z = (window - 1) // 2 + 1
    mate = {"ctx": z * 2 + 1 - lo}
    far = window - 1

    def kv_up(k):
        return remote(
            kv.at[slot(last)], kv.at[slot(last - 2 * k)], kv_s.at[2 * k], kv_r.at[2 * k],
            {"ctx": lax.rem(c + 2 * k, n_ctx)},
        )

    def kv_on(k):
        away = 2 * k + 1 - 2 * lo
        return remote(
            kv.at[slot(last - 2 * k)], kv.at[slot(last - away)], kv_s.at[2 * k + 1], kv_r.at[away], mate
        )

    def kv_far():
        return remote(
            kv.at[slot(last)], kv.at[slot(last - far)], kv_f.at[0], kv_r.at[far],
            {"ctx": lax.rem(c + far, n_ctx)},
        )

    def kv_arrival(d):
        return remote(
            kv.at[slot(last - d)], kv.at[slot(last - d)], kv_s.at[0], kv_r.at[d], mate
        )

    @pl.loop(1, steps_z)
    def _(i):
        k = steps_z - i

        @pl.when(z + k < n_z)
        def _():
            kv_up(k).start()

    @pl.when((lo == 1) & (c + far < n_ctx))
    def _():
        kv_far().start()

    @pl.when(lo == 0)
    def _():
        kv_on(0).start()

    for j in range(0, GROUP_HEADS, 2):
        pair = project(xfull, wq, j * HEAD_SIZE, 2 * HEAD_SIZE)
        q_s[j * BLOCK : (j + 1) * BLOCK] = pair[:, :HEAD_SIZE]
        q_s[(j + 1) * BLOCK : (j + 2) * BLOCK] = pair[:, HEAD_SIZE:]
    h1_ex[0]()
    hid_p[z] = xfull[z, my_rows]

    def pass_hidden():
        h1_ex[1]()
        h2_ex[0]()
        hid_z[:, t] = hid_p[...]

    def head_cotangent():
        wo_copy.wait()
        for j in range(0, GROUP_HEADS, 2):
            pair = project(cotfull, wo, j * HEAD_SIZE, 2 * HEAD_SIZE)
            hc_s[j * BLOCK : (j + 1) * BLOCK] = pair[:, :HEAD_SIZE]
            hc_s[(j + 1) * BLOCK : (j + 2) * BLOCK] = pair[:, HEAD_SIZE:]

    @pl.loop(1, steps_z)
    def _(k):
        @pl.when(z - k >= 0)
        def _():
            kv_up(k).wait_recv()
            kv_on(k).start()

    @pl.when(s == 0)
    def _():
        pass_hidden()

    @pl.when(s == 1)
    def _():
        c_ex[1]()
        head_cotangent()

    doc_start = jnp.int32(0)
    doc_end = jnp.int32(0)
    for i in range(docs_ref.shape[1]):
        doc_end = doc_end + docs_ref[0, i]
        doc_start = jnp.where(doc_end <= c, doc_end, doc_start)
    pairs = window // 2
    wide = (GROUP_HEADS * BLOCK, 2 * BLOCK)
    query_pos = c * BLOCK + lax.broadcasted_iota(jnp.int32, wide, 0) % BLOCK
    first_key = (c - last) * BLOCK + lax.broadcasted_iota(jnp.int32, wide, 1)

    def keys(g):
        return kv[g * 2 * BLOCK : (g + 1) * 2 * BLOCK, :HEAD_SIZE]

    def values(g):
        return kv[g * 2 * BLOCK : (g + 1) * 2 * BLOCK, HEAD_SIZE:]

    for g in range(pairs - 1, -1, -1):
        for j in (2 * g + 1, 2 * g):
            if j < last:

                if (last - j) % 2 == 1:

                    @pl.when(c - last + j >= 0)
                    def _():
                        kv_arrival(last - j).wait_recv()

        block = mm(q_s[...], keys(g), NT) * scale
        key_pos = first_key + g * 2 * BLOCK
        block = jnp.where((key_pos <= query_pos) & (key_pos >= doc_start * BLOCK), block, NEG_FILL)
        scores[g] = block
        both = jnp.maximum(block[:, :BLOCK], block[:, BLOCK:])
        peak[...] = both if g == pairs - 1 else jnp.maximum(peak[...], both)

    top = jnp.max(peak[...], axis=1, keepdims=True)
    for g in range(pairs):
        e = jnp.exp(scores[g] - top)
        scores[g] = e
        both = e[:, :BLOCK] + e[:, BLOCK:]
        denom[...] = both if g == 0 else denom[...] + both

    inverse = 1.0 / jnp.sum(denom[...], axis=1, keepdims=True)
    for g in range(pairs):
        soft = scores[g] * inverse
        low = soft.astype(BF16)
        scores[g] = soft
        probs[g] = low
        term = mm(low, values(g))
        acc[...] = term if g == 0 else acc[...] + term

    att_s[...] = acc[...].astype(BF16)
    for j in range(GROUP_HEADS):
        att_z[own_z, j * HEAD_SIZE : (j + 1) * HEAD_SIZE] = att_s[j * BLOCK : (j + 1) * BLOCK]

    def sec_copy(p):
        return remote(gin_ref, cotfull.at[t], sec_s.at[p], c_r.at[t], {"section": 1 - s, "tp": p})

    @pl.when(s == 1)
    def _():
        pass_hidden()

    @pl.when(s == 0)
    def _():
        att_ring[0](1)

        @pl.loop(0, n_tp)
        def _(p):
            remote(cotfull.at[p], cotfull.at[p], sec_s.at[p], c_r.at[p], {"section": 1 - s}).wait_recv()

        head_cotangent()
        att_ring[0](2)

    delta = jnp.sum(hc_s[...].astype(F32) * att_s[...].astype(F32), axis=1, keepdims=True)

    def dkv_mate_copy(d, k):
        return remote(dkv_part.at[slot(last - d)], dkv_mate.at[k], m_s.at[k], m_r.at[k], mate)

    def dkv_next():
        return remote(dkv_part.at[slot(last - 1)], dkv_in.at[0], d_s.at[0], d_r.at[0], mate)

    def dkv_far():
        return remote(
            dkv_part.at[slot(0)], dkv_in.at[steps_z], d_s.at[steps_z], d_r.at[steps_z],
            {"ctx": lax.rem(c - far + n_ctx, n_ctx)},
        )

    def dkv_down(k):
        return remote(
            dkv_sum.at[k], dkv_in.at[k], d_s.at[k], d_r.at[k], {"ctx": lax.rem(c - 2 * k + n_ctx, n_ctx)}
        )

    def dkv_send_mate(d):
        for side in (0, 1):
            k = (d + 1) // 2 - side

            @pl.when(lo == side)
            def _():
                if k == steps_z:

                    @pl.when(c - far >= 0)
                    def _():
                        dkv_far().start()

                elif k == 0:
                    dkv_next().start()
                else:

                    @pl.when(z - k >= 0)
                    def _():
                        dkv_mate_copy(d, k).start()

    def dkv_add(k):
        @pl.when(z - k >= 0)
        def _():
            dkv_mate_copy(1, k).wait_recv()
            own_part = dkv_part[slot(last - 2 * k)].astype(F32)
            dkv_sum[k] = (own_part + dkv_mate[k].astype(F32)).astype(BF16)
            dkv_down(k).start()

    for g in range(pairs):
        block = slice(g * 2 * BLOCK, (g + 1) * 2 * BLOCK)
        dprobs = mm(hc_s[...], values(g), NT)
        ds = (scores[g] * (dprobs - delta)).astype(BF16)
        dkv_part[block, :HEAD_SIZE] = (mm(ds, q_s[...], TN) * scale).astype(BF16)
        dkv_part[block, HEAD_SIZE:] = mm(probs[g], hc_s[...], TN).astype(BF16)
        dscores[g] = ds
        dkv_send_mate(last - 2 * g)
        if g >= 2:
            dkv_add(pairs + 1 - g)

    dkv_add(1)
    total = mm(dscores[0], keys(0))
    for g in range(1, pairs):
        total = total + mm(dscores[g], keys(g))
    acc[...] = total
    for j in range(GROUP_HEADS):
        gq_n[:, j * HEAD_SIZE : (j + 1) * HEAD_SIZE] = (
            acc[j * BLOCK : (j + 1) * BLOCK] * scale
        ).astype(BF16)
    gq_z[own_z] = gq_n[...]

    def send_cot():
        c1_ex[0]()
        cot_p[z] = cotfull[z, my_rows]

    def pass_cot():
        c1_ex[1]()
        c2_ex[0]()
        cot_z[:, t] = cot_p[...]

    @pl.when(s == 0)
    def _():
        send_cot()
        gq_ring[0](1)
        att_ring[0](3)

    @pl.loop(0, n_tp)
    def _(p):
        feat_f[p] = mm(gq_n[...], wq[pl.ds(p * part, part), :heads], NT)

    @pl.when(s == 0)
    def _():
        pass_cot()
        gq_ring[0](2)
        att_ring[0](4)

    acc[:BLOCK] = dkv_part[slot(last), :HEAD_SIZE].astype(F32)
    acc[BLOCK : 2 * BLOCK] = dkv_part[slot(last), HEAD_SIZE:].astype(F32)

    def dkv_take(copy, k):
        copy.wait_recv()
        acc[:BLOCK] += dkv_in[k, :, :HEAD_SIZE].astype(F32)
        acc[BLOCK : 2 * BLOCK] += dkv_in[k, :, HEAD_SIZE:].astype(F32)

    @pl.when(lo == 0)
    def _():
        dkv_take(dkv_next(), 0)

    @pl.loop(1, steps_z)
    def _(k):
        @pl.when(z + k < n_z)
        def _():
            dkv_take(dkv_down(k), k)

    @pl.when((lo == 1) & (c + far < n_ctx))
    def _():
        dkv_take(dkv_far(), steps_z)

    gkv_n[:, :HEAD_SIZE] = acc[:BLOCK].astype(BF16)
    gkv_n[:, HEAD_SIZE:] = acc[BLOCK : 2 * BLOCK].astype(BF16)
    gkv_z[own_z] = gkv_n[...]
    kz_ex[0]()
    row_acc[...] = jnp.zeros_like(row_acc)

    @pl.loop(1, n_tp + 1)
    def _(i):
        p = lax.rem(t + i, n_tp)
        total = feat_f[p] + mm(gkv_n[...], wq[pl.ds(p * part, part), heads:], NT)
        total = total.astype(BF16)
        feat_out[p] = total
        row_acc[...] += total.astype(F32) * xfull[p].astype(F32)

        @pl.when(i < n_tp)
        def _():
            f_ex[3](p).start()

    row_sum = jnp.sum(row_acc[...], axis=1, keepdims=True)
    rs_out[...] = jnp.broadcast_to(row_sum, (BLOCK, BLOCK)).T[:8]
    r_ex[0]()
    rs_in[t] = rs_out[...]
    feat_in[t] = feat_out[t]

    y_copies = [
        remote(y_out_o, y_in_o, y_s.at[0], y_r.at[0], mate),
        remote(y_out_q, y_in_q, y_s.at[1], y_r.at[1], mate),
        remote(y_out_k, y_in_k, y_s.at[2], y_r.at[2], mate),
    ]
    positions = n_z * BLOCK
    theirs = pl.ds(pl.multiple_of((1 - lo) * half, half), half)
    mine = pl.ds(pl.multiple_of(lo * half, half), half)

    def turn(ref):
        turned[...] = ref[...].reshape(positions, part).T

    def weight_part(right, y_out, out, base, copy):
        step = min(256, heads)
        for k in range(0, right.shape[1], step):
            y_out[:, k : k + step] = mm(turned[theirs], right[:, k : k + step]).astype(BF16)
        copy.start()
        for k in range(0, right.shape[1], step):
            out[:, base + k : base + k + step] = mm(turned[mine], right[:, k : k + step])

    def grad_of_out():
        c2_ex[1]()
        att_ring[1]()
        turn(cot_z)
        weight_part(att_z, y_out_o, gout_ref, 0, y_copies[0])

    def grad_of_query():
        h2_ex[1]()
        turn(hid_z)
        gq_ring[1]()
        weight_part(gq_z, y_out_q, gqkv_ref, 0, y_copies[1])

    @pl.when(s == 0)
    def _():
        gq_ring[0](3)
        grad_of_out()
        gq_ring[0](4)
        grad_of_query()

    f_ex[1]()
    r_ex[1]()
    feature = jnp.zeros((BLOCK, part), F32)
    for p in range(n_tp):
        feature = feature + feat_in[p].astype(F32)
    inv = inv_b[:, :1]
    gain = gain_ref[:, pl.ds(pl.multiple_of(t * part, part), part)]
    scaled = feature * gain
    normed = x_ref[...].astype(F32) * inv
    total = rs_in[0]
    for p in range(1, n_tp):
        total = total + rs_in[p]
    mean = jnp.broadcast_to(total[:1] / width, (BLOCK, BLOCK)).T[:, :1]
    gin_ref[...] = (cotfull[t].astype(F32) + inv * (scaled - normed * mean)).astype(BF16)

    @pl.when(s == 1)
    def _():
        @pl.loop(0, n_tp)
        def _(i):
            sec_copy(lax.rem(t + 1 + i, n_tp)).start()

        send_cot()
        for k in range(1, n_z // 2 + 1):
            att_ring[0](k)
            gq_ring[0](k)
            if k == 2 or n_z == 2:
                pass_cot()
        grad_of_out()
        grad_of_query()

    kz_ex[1]()
    weight_part(gkv_z, y_out_k, gqkv_ref, heads, y_copies[2])
    for y_in, out, base, copy in (
        (y_in_o, gout_ref, 0, y_copies[0]),
        (y_in_q, gqkv_ref, 0, y_copies[1]),
        (y_in_k, gqkv_ref, heads, y_copies[2]),
    ):
        copy.wait_recv()
        out[:, base : base + y_in.shape[1]] += y_in[...].astype(F32)

    for ex in (x_ex, f_ex, r_ex, h1_ex, h2_ex, c1_ex, c2_ex, kz_ex, att_ring, gq_ring):
        ex[2]()
    for copy in y_copies:
        copy.wait_send()

    @pl.loop(1, steps_z)
    def _(k):
        @pl.when(z + k < n_z)
        def _():
            kv_up(k).wait_send()

        @pl.when(z - k >= 0)
        def _():
            kv_on(k).wait_send()

    @pl.when((lo == 1) & (c + far < n_ctx))
    def _():
        kv_far().wait_send()

    @pl.when(lo == 0)
    def _():
        kv_on(0).wait_send()

    @pl.loop(1, steps_z)
    def _(k):
        @pl.when(z - k >= 0)
        def _():
            dkv_mate_copy(1, k).wait_send()
            dkv_down(k).wait_send()

    @pl.when(lo == 1)
    def _():
        dkv_next().wait_send()

    @pl.when((lo == 0) & (c - far >= 0))
    def _():
        dkv_far().wait_send()

    @pl.when(s == 1)
    def _():
        c_ex[2]()

        @pl.loop(0, n_tp)
        def _(p):
            sec_copy(p).wait_send()


def settle(a_in, b_in, c_in, a_out, b_out, c_out, sem):
    copies = [
        pltpu.make_async_copy(source, target, sem.at[i])
        for i, (source, target) in enumerate(((a_in, a_out), (b_in, b_out), (c_in, c_out)))
    ]
    for copy in copies:
        copy.start()
    for copy in copies:
        copy.wait()


def body(layer_input, loss_cot, token_weights, doc_blocks, norm_gain, qkv_weight, out_weight):
    n_ctx, n_tp = lax.axis_size("ctx"), lax.axis_size("tp")
    n_z = n_ctx // 2
    part = layer_input.shape[3]
    width = part * n_tp
    cols, heads = qkv_weight.shape[2], out_weight.shape[2]
    window = min(MAX_DOC, n_ctx)
    q_rows = GROUP_HEADS * BLOCK
    kv_cols = 2 * HEAD_SIZE
    half = part // 2
    share = BLOCK // n_tp
    vmem = lambda shape, dtype=BF16: pltpu.VMEM(shape, dtype)
    dma = lambda *n: pltpu.SemaphoreType.DMA(n)
    scratch = [
        vmem((width, cols)), vmem((width, heads)),
        vmem((n_tp, BLOCK, part)), vmem((n_tp, BLOCK, part)), vmem((BLOCK, part)), vmem((BLOCK, BLOCK), F32),
        vmem((window * BLOCK, kv_cols)),
        vmem((q_rows, HEAD_SIZE)), vmem((q_rows, HEAD_SIZE)), vmem((q_rows, HEAD_SIZE)),
        vmem((BLOCK, heads)), vmem((BLOCK, kv_cols)),
        vmem((window // 2, q_rows, 2 * BLOCK), F32), vmem((window // 2, q_rows, 2 * BLOCK)),
        vmem((window // 2, q_rows, 2 * BLOCK)),
        vmem((q_rows, BLOCK), F32), vmem((q_rows, BLOCK), F32), vmem((q_rows, HEAD_SIZE), F32), vmem((BLOCK, part), F32),
        vmem((window * BLOCK, kv_cols)), vmem((window, BLOCK, kv_cols)),
        vmem((window // 2, BLOCK, kv_cols)), vmem((window // 2, BLOCK, kv_cols)),
        vmem((n_tp, BLOCK, part), F32), vmem((n_tp, BLOCK, part)), vmem((n_tp, BLOCK, part)),
        vmem((8, BLOCK), F32), vmem((n_tp, 8, BLOCK), F32),
        vmem((n_z, share, part)), vmem((n_z, share, part)),
        vmem((n_z, n_tp, share, part)), vmem((n_z, n_tp, share, part)), vmem((n_z * BLOCK, heads)),
        vmem((n_z * BLOCK, heads)), vmem((n_z * BLOCK, kv_cols)), vmem((part, n_z * BLOCK)),
        vmem((half, heads)), vmem((half, heads)), vmem((half, kv_cols)),
        vmem((half, heads)), vmem((half, heads)), vmem((half, kv_cols)),
        dma(2), dma(n_tp), dma(n_tp), dma(n_tp), dma(n_tp), dma(window), dma(window), dma(1), dma(window), dma(window),
        dma(n_tp), dma(n_tp), dma(n_tp), dma(n_tp),
        dma(n_z), dma(n_z), dma(n_tp), dma(n_tp), dma(n_z), dma(n_z), dma(n_tp), dma(n_tp),
        dma(n_z), dma(n_z), dma(n_z), dma(n_z), dma(n_z), dma(n_z),
        dma(3), dma(3), dma(n_tp), dma(window), dma(window), pltpu.SemaphoreType.REGULAR,
    ]
    in_vmem = pl.BlockSpec(memory_space=pltpu.VMEM)
    anywhere = pl.BlockSpec(memory_space=pl.ANY)
    grad_in, grad_qkv, grad_out = pl.pallas_call(
        functools.partial(kernel, n_ctx, n_tp, window),
        out_shape=(
            jax.ShapeDtypeStruct((BLOCK, part), BF16),
            jax.ShapeDtypeStruct((half, cols), F32),
            jax.ShapeDtypeStruct((half, heads), F32),
        ),
        in_specs=[
            in_vmem, in_vmem, in_vmem, pl.BlockSpec(memory_space=pltpu.SMEM), in_vmem, anywhere, anywhere,
        ],
        out_specs=(in_vmem, in_vmem, in_vmem),
        scratch_shapes=scratch,
        compiler_params=pltpu.CompilerParams(
            collective_id=0, has_side_effects=True, vmem_limit_bytes=56 * 1024 * 1024
        ),
    )(
        layer_input[0, 0], loss_cot[0], token_weights, doc_blocks, norm_gain, qkv_weight[0], out_weight[0]
    )
    results = (grad_in, grad_qkv, grad_out)
    grad_in, grad_qkv, grad_out = pl.pallas_call(
        settle,
        out_shape=tuple(jax.ShapeDtypeStruct(r.shape, r.dtype) for r in results),
        in_specs=[in_vmem] * 3,
        out_specs=(anywhere,) * 3,
        scratch_shapes=[dma(3)],
    )(*results)
    return grad_in[None, None], grad_qkv[None], grad_out[None]


def solution(mesh):
    placed = (
        P("section", None, "ctx", "tp"),
        P(None, "ctx", "tp"),
        P(None, "ctx"),
        P(),
        P("section", None),
        P("section", None, "tp"),
        P("section", None, "tp"),
    )
    return jax.shard_map(
        body,
        mesh=mesh,
        in_specs=placed,
        out_specs=(
            P("section", None, "ctx", "tp"),
            P("section", "ctx", "tp"),
            P("section", "ctx", "tp"),
        ),
        check_vma=False,
    )
```
